128 devices in a mesh: seq: 32 (over x, y, core), head: 4 (over z).
Axes of the slice: x: 4, y: 4, z: 4, core: 2. Of those that a mesh axis runs over, the one named last changes fastest.
Arguments:
- inputs: bfloat16 [49152, 512], P(('seq', 'head')), may hold values from -6 to 6
- lengths: int32 [32], P('seq'), may hold values from 768 to 1536, as said below
- cotangent: bfloat16 [49152, 512], P(('seq', 'head')), may hold values from -6 to 6
- attention_gain: float32 [512], replicated, may hold values from 0.5 to 1.5
- attention_shift: float32 [512], replicated, may hold values from -2 to 2
- query_weight: bfloat16 [512, 512], replicated, may hold values from -0.25 to 0.25
- key_weight: bfloat16 [512, 512], replicated, may hold values from -0.25 to 0.25
- value_weight: bfloat16 [512, 512], replicated, may hold values from -0.25 to 0.25
- output_weight: bfloat16 [512, 512], replicated, may hold values from -1 to 1
- feedforward_gain: float32 [512], replicated, may hold values from 0.5 to 1.5
- feedforward_shift: float32 [512], replicated, may hold values from -2 to 2
- expand_weight: bfloat16 [512, 2048], replicated, may hold values from -0.25 to 0.25
- contract_weight: bfloat16 [2048, 512], replicated, may hold values from -0.125 to 0.125
- pooling_weight: bfloat16 [1536, 512], replicated, may hold values from -0.15625 to 0.15625
- coarse_gain: float32 [512], replicated, may hold values from 0.5 to 1.5
- coarse_shift: float32 [512], replicated, may hold values from -2 to 2
- coarse_query: bfloat16 [512, 512], P(None, 'head'), may hold values from -0.25 to 0.25
- coarse_key: bfloat16 [512, 512], P(None, 'head'), may hold values from -0.25 to 0.25
- coarse_value: bfloat16 [512, 512], P(None, 'head'), may hold values from -0.25 to 0.25
- coarse_output: bfloat16 [512, 512], P('head'), may hold values from -1 to 1
- widen_gain: float32 [512], replicated, may hold values from 0.5 to 1.5
- widen_shift: float32 [512], replicated, may hold values from -2 to 2
- coarse_expand: bfloat16 [512, 2048], P(None, 'head'), may hold values from -0.25 to 0.25
- coarse_contract: bfloat16 [2048, 512], P('head'), may hold values from -0.125 to 0.125
- upsample_weight: bfloat16 [512, 1536], replicated, may hold values from -0.25 to 0.25
Outputs:
- mixed: bfloat16 [49152, 512], P(('seq', 'head'))
- input_grad: float32 [49152, 512], P(('seq', 'head'))
- attention_gain_grad: float32 [512], replicated
- attention_shift_grad: float32 [512], replicated
- query_weight_grad: float32 [512, 512], replicated
- key_weight_grad: float32 [512, 512], replicated
- value_weight_grad: float32 [512, 512], replicated
- output_weight_grad: float32 [512, 512], replicated
- feedforward_gain_grad: float32 [512], replicated
- feedforward_shift_grad: float32 [512], replicated
- expand_weight_grad: float32 [512, 2048], replicated
- contract_weight_grad: float32 [2048, 512], replicated
- pooling_weight_grad: float32 [1536, 512], replicated
- coarse_gain_grad: float32 [512], replicated
- coarse_shift_grad: float32 [512], replicated
- coarse_query_grad: float32 [512, 512], P(None, 'head')
- coarse_key_grad: float32 [512, 512], P(None, 'head')
- coarse_value_grad: float32 [512, 512], P(None, 'head')
- coarse_output_grad: float32 [512, 512], P('head')
- widen_gain_grad: float32 [512], replicated
- widen_shift_grad: float32 [512], replicated
- coarse_expand_grad: float32 [512, 2048], P(None, 'head')
- coarse_contract_grad: float32 [2048, 512], P('head')
- upsample_weight_grad: float32 [512, 1536], replicated
The draws below stay inside these ranges and needn't reach their ends.
Inputs may be any that keep to these rules, and one draw needn't show every extreme that they name: `lengths`: every length is 1536 or 768, and both occur.
All inputs are finite; a program needn't handle non-finite values.
Results may differ from the reference program's by a relative error of at most 0.03.
Values may be sent and summed in bfloat16 or wider, within the bound.
A program may use at most 192 MiB of HBM per device.

```python
import math
import jax
import jax.numpy as jnp
from jax import lax

D = 512
HEADS = 8
FF = 2048
GROUP = 1536
POOLED = 513
GROUPS = 32
TOKENS = 49152


def draw_lengths(key, part):
    key = jax.random.fold_in(key, 7)
    flip_key, long_key, offset_key = jax.random.split(key, 3)
    coin_flips = jax.random.randint(flip_key, (GROUPS,), 0, 2)
    longest = jax.random.randint(long_key, (), 0, GROUPS)
    offset = jax.random.randint(offset_key, (), 1, GROUPS)
    shortest = (longest + offset) % GROUPS
    group_index = jnp.arange(GROUPS)
    coin_flips = jnp.where(group_index == longest, 1, jnp.where(group_index == shortest, 0, coin_flips))
    return jnp.where(coin_flips == 1, GROUP, GROUP // 2).astype(jnp.int32)


def shard_levels(own_key, dims, pieces, least, top_value):
    loudness, own = 1.0, jax.random.fold_in(own_key, 6)
    for position, shards_of in pieces:
        draws = jnp.exp(jax.random.uniform(jax.random.fold_in(own, position), (shards_of,), jnp.float32, least / len(pieces), top_value / len(pieces)))
        loudness = loudness * jnp.repeat(draws, dims[position] // shards_of).reshape([-1 if axis == position else 1 for axis in range(len(dims))])
    return loudness


def scatter_about(stream_key, shape, width, most, pieces=(), kind=jnp.bfloat16):
    values = jax.random.normal(stream_key, shape, jnp.float32) * width
    if len(pieces) > 0:
        values = shard_levels(stream_key, shape, pieces, -0.22, 0.18) * values
    return jnp.clip(values, min=-most, max=most).astype(kind)


def setup_inputs(seed: int = 0) -> dict:
    seeds = jax.random.split(jax.random.key(seed), 26)
    return {
        "inputs": scatter_about(seeds[0], (TOKENS, D), 1.0, 6.0, ((0, 128),)),
        "lengths": draw_lengths(jax.random.fold_in(seeds[25], 71), 0),
        "cotangent": scatter_about(seeds[2], (TOKENS, D), 1.0, 6.0, ((0, 128),)),
        "attention_gain": jnp.clip(1.0 + 0.1 * jax.random.normal(seeds[3], (D,), jnp.float32), 0.5, 1.5),
        "attention_shift": scatter_about(seeds[4], (D,), 0.3, 2.0, (), jnp.float32),
        "query_weight": scatter_about(seeds[5], (D, D), D ** -0.5, 0.25),
        "key_weight": scatter_about(seeds[6], (D, D), D ** -0.5, 0.25),
        "value_weight": scatter_about(seeds[7], (D, D), D ** -0.5, 0.25),
        "output_weight": scatter_about(seeds[8], (D, D), (D // 16) ** -0.5, 1.0),
        "feedforward_gain": jnp.clip(1.0 + 0.1 * jax.random.normal(seeds[9], (D,), jnp.float32), 0.5, 1.5),
        "feedforward_shift": scatter_about(seeds[10], (D,), 0.3, 2.0, (), jnp.float32),
        "expand_weight": scatter_about(seeds[11], (D, FF), D ** -0.5, 0.25),
        "contract_weight": scatter_about(seeds[12], (FF, D), FF ** -0.5, 0.125),
        "pooling_weight": scatter_about(seeds[13], (3 * D, D), (3 * D) ** -0.5, 0.15625),
        "coarse_gain": jnp.clip(1.0 + 0.1 * jax.random.normal(seeds[14], (D,), jnp.float32), 0.5, 1.5),
        "coarse_shift": scatter_about(seeds[15], (D,), 0.3, 2.0, (), jnp.float32),
        "coarse_query": scatter_about(seeds[16], (D, D), D ** -0.5, 0.25, ((1, 4),)),
        "coarse_key": scatter_about(seeds[17], (D, D), D ** -0.5, 0.25, ((1, 4),)),
        "coarse_value": scatter_about(seeds[18], (D, D), D ** -0.5, 0.25, ((1, 4),)),
        "coarse_output": scatter_about(seeds[19], (D, D), (D // 16) ** -0.5, 1.0, ((0, 4),)),
        "widen_gain": jnp.clip(1.0 + 0.1 * jax.random.normal(seeds[20], (D,), jnp.float32), 0.5, 1.5),
        "widen_shift": scatter_about(seeds[21], (D,), 0.3, 2.0, (), jnp.float32),
        "coarse_expand": scatter_about(seeds[22], (D, FF), D ** -0.5, 0.25, ((1, 4),)),
        "coarse_contract": scatter_about(seeds[23], (FF, D), FF ** -0.5, 0.125, ((0, 4),)),
        "upsample_weight": scatter_about(seeds[24], (D, 3 * D), D ** -0.5, 0.25),
    }


@jax.custom_vjp
def low(v):
    return lax.optimization_barrier(v.astype(jnp.bfloat16)).astype(jnp.float32)

@jax.custom_vjp
def low_back(v):
    return v

def low_keep(v):
    return (low(v), None)

def low_pass(kept, grad):
    return (grad,)

def back_keep(v):
    return (v, None)

def back_low(kept, grad):
    return (low(grad),)
low.defvjp(low_keep, low_pass)
low_back.defvjp(back_keep, back_low)
EPSILON = 1e-05

def matmul(left, right):
    return jnp.dot(left, right, precision=lax.Precision.HIGHEST, preferred_element_type=jnp.float32)

def layer_norm(values, norm_gain, norm_shift):
    centred = values - lax.optimization_barrier(jnp.mean(values, axis=-1, keepdims=True))
    spread = lax.optimization_barrier(jnp.mean(centred * centred, axis=-1, keepdims=True))
    return centred * lax.rsqrt(spread + EPSILON) * norm_gain + norm_shift

def rotate(values, positions, head_count):
    row_count = values.shape[0]
    head_width = values.shape[1] // head_count
    half_width = head_width // 2
    per_head = values.reshape(row_count, head_count, head_width)
    frequency = jnp.exp(jnp.arange(half_width, dtype=jnp.float32) * (-math.log(10000.0) / half_width))
    angles = positions[:, None] * frequency[None, :]
    cosine = jnp.cos(angles)[:, None, :]
    sine_part = jnp.sin(angles)[:, None, :]
    front_half = per_head[:, :, :half_width]
    back_half = per_head[:, :, half_width:]
    turned = jnp.concatenate([front_half * cosine - back_half * sine_part, front_half * sine_part + back_half * cosine], axis=-1)
    return turned.reshape(row_count, head_count * head_width)

def attend(normed, query_w, key_w, value_w, output_w, head_count):
    row_count = normed.shape[0]
    head_width = normed.shape[1] // head_count
    positions = jnp.arange(row_count, dtype=jnp.float32)
    queries = low(rotate(low_back(matmul(normed, query_w)), positions, head_count))
    key_rows = low(rotate(low_back(matmul(normed, key_w)), positions, head_count))
    value_rows = low(low_back(matmul(normed, value_w)))
    split_query = queries.reshape(row_count, head_count, head_width)
    split_key = key_rows.reshape(row_count, head_count, head_width)
    split_value = value_rows.reshape(row_count, head_count, head_width)
    scores = low_back(jnp.einsum('qhd,khd->hqk', split_query, split_key, precision=lax.Precision.HIGHEST) * (1.0 / math.sqrt(head_width)))
    order = jnp.arange(row_count, dtype=jnp.int32)
    causal = order[None, :] <= order[:, None]
    scores = jnp.where(causal[None], scores, -1e+30)
    row_max = lax.optimization_barrier(jnp.max(scores, axis=-1, keepdims=True))
    lifted_exp = jnp.exp(scores - row_max)
    attention_probs = low(lifted_exp / lax.optimization_barrier(jnp.sum(lifted_exp, axis=-1, keepdims=True)))
    blended = jnp.einsum('hqk,khd->qhd', attention_probs, split_value, precision=lax.Precision.HIGHEST)
    blended = blended.reshape(row_count, head_count * head_width)
    return low_back(matmul(low(low_back(blended)), output_w))

def group_forward(params, rows_in, valid_rows):
    att_gain, att_shift, query_w, key_w, value_w, output_w, ffn_gain, ffn_shift, expand_w, contract_w, pool_w, crs_gain, crs_shift, crs_query, crs_key, crs_value, crs_output, wide_gain, wide_shift, crs_expand, crs_contract, upsample_w = params
    normed = low(layer_norm(rows_in, att_gain, att_shift))
    hidden = rows_in + attend(normed, query_w, key_w, value_w, output_w, HEADS)
    widened = low(layer_norm(hidden, ffn_gain, ffn_shift))
    activated = low(jax.nn.gelu(low_back(matmul(widened, expand_w)), approximate=False))
    stream = hidden + low_back(matmul(activated, contract_w))
    masked = low(stream * valid_rows[:, None])
    padded = jnp.concatenate([jnp.zeros((2, D), jnp.float32), masked, jnp.zeros((3 * POOLED - GROUP - 2, D), jnp.float32)], axis=0)
    coarse_in = low_back(matmul(padded.reshape(POOLED, 3 * D), pool_w))
    coarse_normed = low(layer_norm(coarse_in, crs_gain, crs_shift))
    coarse_mid = coarse_in + attend(coarse_normed, crs_query, crs_key, crs_value, crs_output, HEADS)
    coarse_wide = low(layer_norm(coarse_mid, wide_gain, wide_shift))
    coarse_act = low(jax.nn.gelu(low_back(matmul(coarse_wide, crs_expand)), approximate=False))
    coarse_out = coarse_mid + low_back(matmul(coarse_act, crs_contract))
    coarse_top = low(coarse_out)
    lifted = low_back(matmul(coarse_top, upsample_w)).reshape(3 * POOLED, D)[:GROUP]
    return valid_rows[:, None] * (stream + lifted)

def reference(inputs, lengths, cotangent, attention_gain, attention_shift, query_weight, key_weight, value_weight, output_weight, feedforward_gain, feedforward_shift, expand_weight, contract_weight, pooling_weight, coarse_gain, coarse_shift, coarse_query, coarse_key, coarse_value, coarse_output, widen_gain, widen_shift, coarse_expand, coarse_contract, upsample_weight):
    params = tuple((weight.astype(jnp.float32) for weight in (attention_gain, attention_shift, query_weight, key_weight, value_weight, output_weight, feedforward_gain, feedforward_shift, expand_weight, contract_weight, pooling_weight, coarse_gain, coarse_shift, coarse_query, coarse_key, coarse_value, coarse_output, widen_gain, widen_shift, coarse_expand, coarse_contract, upsample_weight)))
    rows_all = inputs.astype(jnp.float32).reshape(GROUPS, GROUP, D)
    grads_all = cotangent.astype(jnp.float32).reshape(GROUPS, GROUP, D)

    def one_group(totals, packed):
        rows_in, grad_rows, length = packed
        valid_rows = (jnp.arange(GROUP, dtype=jnp.int32) < length).astype(jnp.float32)

        def forward(weights, stream_rows):
            return group_forward(weights, stream_rows, valid_rows)
        result, pullback = jax.vjp(forward, params, rows_in)
        param_grads, input_grads = pullback(grad_rows)
        totals = jax.tree.map(jnp.add, totals, param_grads)
        return (totals, (result.astype(jnp.bfloat16), input_grads))
    zero_grads = jax.tree.map(jnp.zeros_like, params)
    totals, outputs = lax.scan(one_group, zero_grads, (rows_all, grads_all, lengths))
    mixed = outputs[0].reshape(TOKENS, D)
    input_grad = outputs[1].reshape(TOKENS, D)
    return (mixed, input_grad, totals[0], totals[1], totals[2], totals[3], totals[4], totals[5], totals[6], totals[7], totals[8], totals[9], totals[10], totals[11], totals[12], totals[13], totals[14], totals[15], totals[16], totals[17], totals[18], totals[19], totals[20], totals[21])
```

```python
import functools
import math

import jax
import jax.numpy as jnp
import numpy as np
from jax import lax
from jax.experimental import pallas as pl
from jax.experimental.pallas import tpu as pltpu
from jax.sharding import PartitionSpec as P

MESH = pl.DeviceIdType.MESH
VMEM = pltpu.VMEM
LOW = jnp.bfloat16
WIDE = jnp.float32
EPSILON = 1e-05
OWN = 384
ROWS = 1536
WIDTH = 512
HIDDEN = 2048
SHORT = 528
PART = 144
SIZES = {"core": 2, "x": 4, "y": 4, "z": 4}


def turn_tables():
    frequency = np.exp(np.arange(32, dtype=np.float32) * np.float32(-math.log(10000.0) / 32))
    angles = np.arange(ROWS, dtype=np.float32)[:, None] * frequency.astype(np.float32)[None, :]
    cosine = np.cos(angles.astype(np.float64)).astype(np.float32)
    sine = np.sin(angles.astype(np.float64)).astype(np.float32)
    return np.tile(cosine, (1, 4)), np.concatenate([-sine, sine, -sine, sine], axis=1)


def my_coords():
    seq = lax.axis_index("seq")
    return {
        "core": lax.rem(seq, 2),
        "y": lax.rem(lax.div(seq, 2), 4),
        "x": lax.div(seq, 8),
        "z": lax.axis_index("head"),
    }


def moved(coords, axis, step):
    other = dict(coords)
    other[axis] = lax.rem(coords[axis] + step, SIZES[axis])
    return other


def device_of(coords):
    return {
        "seq": (coords["x"] * 4 + coords["y"]) * 2 + coords["core"],
        "head": coords["z"],
    }


def meet(coords, axes):
    barrier = pltpu.get_barrier_semaphore()
    count = 0
    for axis in axes:
        for step in range(1, SIZES[axis]):
            pl.semaphore_signal(
                barrier,
                inc=1,
                device_id=device_of(moved(coords, axis, step)),
                device_id_type=MESH,
            )
            count += 1
    pl.semaphore_wait(barrier, count)


def dot(left, right):
    return lax.dot_general(left, right, (((1,), (0,)), ((), ())), preferred_element_type=WIDE)


def dot_nt(left, right):
    return lax.dot_general(left, right, (((1,), (1,)), ((), ())), preferred_element_type=WIDE)


def dot_tn(left, right):
    return lax.dot_general(left, right, (((0,), (0,)), ((), ())), preferred_element_type=WIDE)


def lanes_iota(shape):
    return lax.broadcasted_iota(jnp.int32, shape, len(shape) - 1)


def rows_iota(shape):
    return lax.broadcasted_iota(jnp.int32, shape, 0)


def standard(values):
    centred = values - jnp.mean(values, axis=-1, keepdims=True)
    scale = lax.rsqrt(jnp.mean(centred * centred, axis=-1, keepdims=True) + EPSILON)
    return centred * scale, scale


def norm(values, gain, shift):
    return standard(values)[0] * gain + shift


def norm_back(values, gain, grad):
    unit, scale = standard(values)
    inner = grad * gain
    first = jnp.mean(inner, axis=-1, keepdims=True)
    second = jnp.mean(inner * unit, axis=-1, keepdims=True)
    return scale * (inner - first - unit * second), grad * unit


def turn(values, cosine, sine):
    lane = lanes_iota(values.shape)
    other = jnp.where(
        lax.rem(lane, 64) < 32, pltpu.roll(values, 96, 1), pltpu.roll(values, 32, 1)
    )
    return values * cosine + other * sine


def gelu_parts(values):
    half = 0.5 + 0.5 * lax.erf(values * math.sqrt(0.5))
    bell = jnp.exp(values * values * -0.5) * (1.0 / math.sqrt(2.0 * math.pi))
    return values * half, half + values * bell


def head_lanes(head, values):
    return jnp.where(lanes_iota(values.shape) // 64 == head, values, jnp.zeros_like(values))


def by_head(first, second):
    return jnp.where(lanes_iota(first.shape) < 64, first, second)


def head_rows(columns):
    shape = (8, 128)
    pick = (lanes_iota(shape) == rows_iota(shape) * 64).astype(WIDE)
    return lax.dot_general(
        pick,
        columns,
        (((1,), (1,)), ((), ())),
        precision=lax.Precision.HIGHEST,
        preferred_element_type=WIDE,
    )


def attend_tile(q_tile, k_ref, v_ref, lanes, before, width, offset, key_limit=None):
    outs, tops = [], []
    rows = q_tile.shape[0]
    for head in range(2):
        query = head_lanes(head, q_tile)
        last = pl.ds(before, width)
        near = dot_nt(query, k_ref[last, lanes])
        keep = lanes_iota(near.shape) <= rows_iota(near.shape) + offset
        near = jnp.where(keep, near, -1e30)
        top = jnp.max(near, axis=-1, keepdims=True)
        if before:
            far = dot_nt(query, k_ref[pl.ds(0, before), lanes])
            top = jnp.maximum(top, jnp.max(far, axis=-1, keepdims=True))
        near = jnp.exp(near - top)
        total = jnp.sum(near, axis=-1, keepdims=True)
        mixed = dot(near.astype(LOW), v_ref[last, lanes])
        if before:
            far = jnp.exp(far - top)
            total = total + jnp.sum(far, axis=-1, keepdims=True)
            mixed = mixed + dot(far.astype(LOW), v_ref[pl.ds(0, before), lanes])
        outs.append(mixed * (1.0 / total))
        tops.append(top + jnp.log(total))
    shape = (rows, 128)
    level = by_head(jnp.broadcast_to(tops[0], shape), jnp.broadcast_to(tops[1], shape))
    return by_head(outs[0], outs[1]), head_rows(level)


class Copies:
    def __init__(self, send_sem, recv_sem):
        self.send_sem, self.recv_sem, self.count, self.sent = send_sem, recv_sem, 0, []

    def remote(self, source, target, other):
        place = self.count
        self.count += 1
        move = pltpu.make_async_remote_copy(
            src_ref=source,
            dst_ref=target,
            send_sem=self.send_sem.at[place],
            recv_sem=self.recv_sem.at[place],
            device_id=device_of(other),
            device_id_type=MESH,
        )
        move.start()
        self.sent.append(move)
        return move

    def local(self, source, target):
        place = self.count
        self.count += 1
        move = pltpu.make_async_copy(source, target, self.recv_sem.at[place])
        move.start()
        return move

    def finish(self):
        for move in self.sent:
            move.wait_send()


def pair_sums(columns):
    shape = (8, 128)
    pick = (lanes_iota(shape) // 64 == rows_iota(shape)).astype(WIDE)
    return lax.dot_general(
        pick,
        columns,
        (((1,), (1,)), ((), ())),
        precision=lax.Precision.HIGHEST,
        preferred_element_type=WIDE,
    )


def attend_back_block(q_tile, d_tile, key, value, tops, deltas, offset):
    d_query = []
    d_key = d_value = None
    for head in range(2):
        query = head_lanes(head, q_tile)
        d_out = head_lanes(head, d_tile)
        probs = jnp.exp(dot_nt(key, query) - tops[head : head + 1])
        if offset is not None:
            probs = jnp.where(rows_iota(probs.shape) <= lanes_iota(probs.shape) + offset, probs, 0.0)
        d_score = (probs * (dot_nt(value, d_out) - deltas[head : head + 1])).astype(LOW)
        more_value = dot(probs.astype(LOW), d_out)
        more_key = dot(d_score, query)
        d_value = more_value if d_value is None else d_value + more_value
        d_key = more_key if d_key is None else d_key + more_key
        d_query.append(dot_tn(d_score, key))
    return by_head(*d_query) * 0.125, d_key, d_value


class Stream:
    def __init__(self, stack, low, high, axes, spread=False):
        self.stack, self.low, self.high, self.axes = stack, low, high, axes
        self.spread = spread
        self.levels = len(axes) + spread


def sum_kernel(streams, row_counts, *refs):
    stacks = len(row_counts)
    ins = refs[:stacks]
    outs = refs[stacks : 2 * stacks]
    totals = refs[2 * stacks : 3 * stacks]
    rest = refs[3 * stacks :]
    depth = max(s.levels for s in streams)
    landing = {}
    place = 0
    for number, stream in enumerate(streams):
        for level in range(1, len(stream.axes)):
            landing[number, level] = rest[place]
            place += 1
    send_sem, recv_sem = rest[place], rest[place + 1]
    coords = my_coords()
    meet(coords, ("core", "x", "y", "z"))

    def block(stream, level):
        rows = row_counts[stream.stack]
        start = 0
        for axis in stream.axes[:level]:
            rows = rows // SIZES[axis]
            start = start + coords[axis] * rows
        return start, rows

    def lanes(stream):
        return pl.ds(stream.low, stream.high - stream.low)

    def copy(number, phase, slot, source, target, other):
        return pltpu.make_async_remote_copy(
            src_ref=source,
            dst_ref=target,
            send_sem=send_sem.at[number, phase, slot],
            recv_sem=recv_sem.at[number, phase, slot],
            device_id=device_of(other),
            device_id_type=MESH,
        )

    sends = []
    pending = {}

    def start_down(number, level):
        stream = streams[number]
        axis = stream.axes[level]
        start, rows = block(stream, level)
        part = rows // SIZES[axis]
        source = ins[stream.stack] if level == 0 else totals[stream.stack]
        for step in range(1, SIZES[axis]):
            other = moved(coords, axis, step)
            where = pl.ds(pl.multiple_of(start + other[axis] * part, 16), part)
            if level == 0:
                mine = pl.ds(pl.multiple_of(start + coords[axis] * part, 16), part)
                target = totals[stream.stack].at[pl.ds(0, part), lanes(stream)]
            else:
                target = landing[number, level].at[step - 1]
            if level > 0:
                where = pl.ds(pl.multiple_of(where_in_half(stream, level, other), 16), part)
            move = copy(number, level, step - 1, source.at[where, lanes(stream)], target, other)
            move.start()
            sends.append(move)
            pending[number, level, step] = move

    def where_in_half(stream, level, who):
        rows = row_counts[stream.stack] // 2
        start = 0
        for axis in stream.axes[1:level]:
            rows = rows // SIZES[axis]
            start = start + coords[axis] * rows
        axis = stream.axes[level]
        return start + who[axis] * (rows // SIZES[axis])

    def add_down(number, level):
        stream = streams[number]
        axis = stream.axes[level]
        for step in range(1, SIZES[axis]):
            pending[number, level, step].wait_recv()
        rows = row_counts[stream.stack] // 2
        for other in stream.axes[1 : level + 1]:
            rows = rows // SIZES[other]
        total = totals[stream.stack]
        base = 0 if level == 0 else where_in_half(stream, level, coords)
        step_rows = min(rows, 32)

        def add(index, carry):
            at = pl.multiple_of(index * step_rows, 16)
            here = pl.ds(pl.multiple_of(base + at, 16), step_rows)
            value = total[here, lanes(stream)].astype(WIDE)
            if level == 0:
                own = pl.ds(pl.multiple_of(coords["core"] * rows + at, 16), step_rows)
                value = value + ins[stream.stack][own, lanes(stream)].astype(WIDE)
            else:
                for step in range(1, SIZES[axis]):
                    value = value + landing[number, level][
                        step - 1, pl.ds(at, step_rows), :
                    ].astype(WIDE)
            total[here, lanes(stream)] = value.astype(LOW)
            return carry

        lax.fori_loop(0, rows // step_rows, add, 0)

    def start_up(number, level):
        stream = streams[number]
        axis = (*stream.axes, "z")[level]
        start, rows = block(stream, level + 1)
        where = pl.ds(pl.multiple_of(start, 16), rows)
        phase = 2 * depth - 1 - level
        target = outs[stream.stack]
        if level == len(stream.axes):
            target = target.at[coords["z"], where, lanes(stream)]
        elif stream.spread:
            target = target.at[pl.ds(0, 4), where, lanes(stream)]
        else:
            target = target.at[where, lanes(stream)]
        for step in range(1, SIZES[axis]):
            move = copy(number, phase, step - 1, target, target, moved(coords, axis, step))
            move.start()
            sends.append(move)
            pending[number, phase, step] = move

    def end_up(number, level):
        phase = 2 * depth - 1 - level
        for step in range(1, SIZES[(*streams[number].axes, "z")[level]]):
            pending[number, phase, step].wait_recv()

    for level in range(depth):
        for number, stream in enumerate(streams):
            if level < len(stream.axes):
                if level > 0:
                    add_down(number, level - 1)
                start_down(number, level)
    for level in reversed(range(depth)):
        for number, stream in enumerate(streams):
            if level == stream.levels - 1:
                last = len(stream.axes) - 1
                add_down(number, last)
                start, rows = block(stream, last + 1)
                here = pl.ds(pl.multiple_of(start, 16), rows)
                there = pl.ds(pl.multiple_of(where_in_half(stream, last, coords), 16), rows)
                value = totals[stream.stack][there, lanes(stream)]
                if stream.spread:
                    outs[stream.stack][coords["z"], here, lanes(stream)] = value
                else:
                    outs[stream.stack][here, lanes(stream)] = value
                start_up(number, level)
            elif level < stream.levels - 1:
                end_up(number, level + 1)
                start_up(number, level)
    for number in range(len(streams)):
        end_up(number, 0)
    for move in sends:
        move.wait_send()


def sum_gradients(stacks, streams, collective_id):
    row_counts = [stack.shape[0] for stack in stacks]
    spread = {s.stack for s in streams if s.spread}
    depth = max(s.levels for s in streams)
    scratch = [VMEM((s.shape[0] // 2, s.shape[1]), LOW) for s in stacks]
    for stream in streams:
        rows = row_counts[stream.stack] // 2
        for axis in stream.axes[1:]:
            rows = rows // SIZES[axis]
            scratch.append(VMEM((3, rows, stream.high - stream.low), LOW))
    scratch.append(pltpu.SemaphoreType.DMA((len(streams), 2 * depth, 3)))
    scratch.append(pltpu.SemaphoreType.DMA((len(streams), 2 * depth, 3)))
    return pl.pallas_call(
        functools.partial(sum_kernel, streams, row_counts),
        out_shape=[
            jax.ShapeDtypeStruct((4, *s.shape) if number in spread else s.shape, s.dtype)
            for number, s in enumerate(stacks)
        ],
        in_specs=[pl.BlockSpec(memory_space=VMEM)] * len(stacks),
        out_specs=[pl.BlockSpec(memory_space=VMEM)] * len(stacks),
        scratch_shapes=scratch,
        compiler_params=pltpu.CompilerParams(
            collective_id=collective_id, has_side_effects=True, vmem_limit_bytes=56 * 2**20
        ),
    )(*stacks)


def forward_kernel(*refs):
    (lengths, x, cot, a_gain, a_shift, wq, wk, wv, wo_hbm, f_gain, f_shift, we_hbm, wc_hbm, wp_hbm,
     wu_hbm, cosine, sine, *shards) = refs[:23]
    (a1, q, k, v, o, level, o_own, h, a2, act, slope, s, m, c0g, dcg, fqkv, fo, fe, fc) = refs[23:42]
    (wo, we, wc, wp, wu, wqkv, landing, thin, send_sem, recv_sem) = refs[42:]
    fulls = [
        (fqkv, pl.ds(0, 128)),
        (fqkv, pl.ds(128, 128)),
        (fqkv, pl.ds(256, 128)),
        (fo, pl.ds(0, WIDTH)),
        (fe, pl.ds(0, WIDTH)),
        (fc, pl.ds(0, WIDTH)),
    ]
    coords = my_coords()
    z = coords["z"]
    core = coords["core"]
    right, left, far = (moved(coords, "z", step) for step in (1, 3, 2))
    copies = Copies(send_sem, recv_sem)
    loads = [
        copies.local(source, target)
        for source, target in ((wu_hbm, wu), (wo_hbm, wo), (we_hbm, we), (wc_hbm, wc), (wp_hbm, wp))
    ]
    own_weights = [
        copies.local(shard, full.at[z, pl.ds(0, shard.shape[0]), across])
        for shard, (full, across) in zip(shards, fulls)
    ]
    meet(coords, ("core", "z"))
    low, high = pl.ds(0, OWN // 2), pl.ds(OWN // 2, OWN // 2)
    to_right = copies.remote(x.at[low], landing.at[0, low], right)
    to_left = copies.remote(x.at[high], landing.at[1, high], left)
    to_right_more = copies.remote(x.at[high], landing.at[0, high], right)
    to_left_more = copies.remote(x.at[low], landing.at[1, low], left)

    lane = pl.ds(pl.multiple_of(z * 128, 128), 128)
    for place, weight in enumerate((wq, wk, wv)):
        wqkv[:, 128 * place : 128 * place + 128] = weight[:, lane]

    def project(block, index):
        start = pl.multiple_of(index * OWN, OWN)

        def rows_of(step, carry):
            here = pl.multiple_of(step * 128, 128)
            there = pl.ds(pl.multiple_of(start + here, 128), 128)
            values = block[pl.ds(here, 128), :].astype(WIDE)
            a1[there, :] = norm(values, a_gain[...], a_shift[...]).astype(LOW)
            return carry

        lax.fori_loop(0, OWN // 128, rows_of, 0)
        here = pl.ds(start, OWN)
        both = dot(a1[here, :], wqkv[...])
        cos, sin = cosine[here, :], sine[here, :]
        q[here, :] = (turn(both[:, :128], cos, sin) * 0.125).astype(LOW)
        k[here, :] = turn(both[:, 128:256], cos, sin).astype(LOW)
        v[here, :] = both[:, 256:].astype(LOW)

    project(x, z)
    to_right.wait_recv()
    far_right = copies.remote(landing.at[0, low], landing.at[2, low], right)
    to_left.wait_recv()
    far_left = copies.remote(landing.at[1, high], landing.at[2, high], left)

    valid = (rows_iota((OWN, 128)) + z * OWN < lengths[0]).astype(WIDE)
    for part in range(4):
        thin[part, pl.ds(0, 8), :] = jnp.zeros((8, 128), WIDE)
        thin[part, pl.ds(392, 48), :] = jnp.zeros((48, 128), WIDE)
        thin[part, pl.ds(8, OWN), :] = cot[:, 128 * part : 128 * part + 128].astype(WIDE) * valid

    def every_third(first, count):
        pieces = [thin[part, pl.ds(first, count, 3), :].astype(LOW) for part in range(4)]
        return jnp.concatenate(pieces, axis=1)

    loads[0].wait()
    lifted_back = sum(
        dot_nt(every_third(8 + r, 128), wu[:, 512 * r : 512 * r + 512]) for r in range(3)
    )
    dcg[z] = lifted_back.astype(LOW)

    to_right_more.wait_recv()
    project(landing.at[0], left["z"])
    to_left_more.wait_recv()
    project(landing.at[1], right["z"])
    far_right.wait_recv()
    far_left.wait_recv()
    project(landing.at[2], far["z"])

    dc_moves = [copies.remote(dcg.at[z], dcg.at[z], other) for other in (right, left, far)]
    weight_moves = {}
    for step, other in enumerate((right, left, far)):
        for place, (shard, (full, across)) in enumerate(zip(shards, fulls)):
            half = shard.shape[0] // 2
            mine = pl.ds(pl.multiple_of(core * half, 32), half)
            weight_moves[step, place] = copies.remote(
                shard.at[mine], full.at[z, mine, across], other
            )

    sent_blocks = send_sem.shape[0] - 4
    got_blocks = recv_sem.shape[0] - 4

    def block_move(target, source):
        return pltpu.make_async_remote_copy(
            src_ref=o.at[pl.ds(pl.multiple_of(target * OWN, OWN), OWN), :],
            dst_ref=o_own.at[:, pl.ds(pl.multiple_of(source * 128, 128), 128)],
            send_sem=send_sem.at[sent_blocks + target],
            recv_sem=recv_sem.at[got_blocks + source],
            device_id=device_of({**coords, "z": target}),
            device_id_type=MESH,
        )

    everything = pl.ds(0, 128)
    for block in reversed(range(4)):

        def tile(step, carry):
            start = pl.multiple_of(block * OWN + step * 128, 128)
            here = pl.ds(start, 128)
            mixed, tops = attend_tile(
                q[here, :], k, v, everything, block * OWN, OWN, step * 128
            )
            o[here, :] = mixed.astype(LOW)
            level[:, here] = tops
            return carry

        lax.fori_loop(0, 3, tile, 0)

        @pl.when(z != block)
        def send():
            block_move(block, z).start()

    o_own[:, lane] = o[pl.ds(pl.multiple_of(z * OWN, OWN), OWN), :]

    swaps = []
    sibling = moved(coords, "core", 1)
    for step, other in enumerate((left, right, far)):
        for place, (full, across) in enumerate(fulls):
            weight_moves[step, place].wait_recv()
            half = full.shape[1] // 2
            mine = pl.ds(pl.multiple_of(core * half, 32), half)
            part = full.at[other["z"], mine, across]
            swaps.append(copies.remote(part, part, sibling))
    for step in range(1, 4):
        other = lax.rem(z + step, 4)
        block_move(z, other).wait_recv()

    for load in loads[1:]:
        load.wait()

    def mix(step, carry):
        here = pl.ds(pl.multiple_of(step * 128, 128), 128)
        hidden = x[here, :].astype(WIDE) + dot(o_own[here, :], wo[...])
        h[here, :] = hidden
        a2[here, :] = norm(hidden, f_gain[...], f_shift[...]).astype(LOW)
        return carry

    lax.fori_loop(0, 3, mix, 0)

    def widen(step, carry):
        here = pl.ds(pl.multiple_of(step * 256, 256), 256)
        value, back = gelu_parts(dot(a2[...], we[:, here]))
        act[:, here] = value.astype(LOW)
        slope[:, here] = back.astype(LOW)
        return carry

    lax.fori_loop(0, HIDDEN // 256, widen, 0)

    for part in range(4):
        here = slice(128 * part, 128 * part + 128)
        if part % 2 == 0:
            wide = slice(256 * (part // 2), 256 * (part // 2) + 256)
            summed = h[:, wide] + dot(act[...], wc[:, wide])
            s[:, wide] = summed
        kept = (s[:, here] * valid).astype(LOW)
        m[:, here] = kept
        thin[part, pl.ds(8, OWN), :] = kept.astype(WIDE)
    pooled = sum(
        dot(every_third(6 + r, PART), wp[512 * r : 512 * r + 512, :]) for r in range(3)
    )
    c0g[z] = pooled.astype(LOW)
    c0_moves = [copies.remote(c0g.at[z], c0g.at[z], other) for other in (right, left, far)]

    for load in own_weights:
        load.wait()
    for move in dc_moves + swaps + c0_moves:
        move.wait_recv()
    copies.finish()
    for step in range(1, 4):
        block_move(lax.rem(z + step, 4), z).wait_send()


def forward(lengths, x, cot, gains, square, wo, we, wc, wp, wu, tables, shards):
    def shape(*dims, kind=LOW):
        return jax.ShapeDtypeStruct(dims, kind)

    outs = [
        shape(ROWS, WIDTH),
        shape(ROWS, 128),
        shape(ROWS, 128),
        shape(ROWS, 128),
        shape(ROWS, 128),
        shape(8, ROWS, kind=WIDE),
        shape(OWN, WIDTH),
        shape(OWN, WIDTH, kind=WIDE),
        shape(OWN, WIDTH),
        shape(OWN, HIDDEN),
        shape(OWN, HIDDEN),
        shape(OWN, WIDTH, kind=WIDE),
        shape(OWN, WIDTH),
        shape(4, PART, WIDTH),
        shape(4, 128, WIDTH),
        shape(4, WIDTH, OWN),
        shape(4, 128, WIDTH),
        shape(4, WIDTH, WIDTH),
        shape(4, WIDTH, WIDTH),
    ]
    vmem = pl.BlockSpec(memory_space=VMEM)
    hbm = pl.BlockSpec(memory_space=pl.ANY)
    copy_count = 5 + 6 + 4 + 2 + 3 + 18 + 18 + 3 + 4
    return pl.pallas_call(
        forward_kernel,
        out_shape=outs,
        in_specs=[pl.BlockSpec(memory_space=pltpu.SMEM)]
        + [vmem] * 7 + [hbm] + [vmem] * 2 + [hbm] * 4 + [vmem] * 2 + [hbm] * 6,
        out_specs=[vmem] * 15 + [hbm] * 4,
        scratch_shapes=[
            VMEM((WIDTH, WIDTH), LOW),
            VMEM((WIDTH, HIDDEN), LOW),
            VMEM((HIDDEN, WIDTH), LOW),
            VMEM((ROWS, WIDTH), LOW),
            VMEM((WIDTH, ROWS), LOW),
            VMEM((WIDTH, OWN), LOW),
            VMEM((3, OWN, WIDTH), LOW),
            VMEM((4, 440, 128), WIDE),
            pltpu.SemaphoreType.DMA((copy_count,)),
            pltpu.SemaphoreType.DMA((copy_count,)),
        ],
        compiler_params=pltpu.CompilerParams(
            collective_id=1, has_side_effects=True, vmem_limit_bytes=60 * 2**20
        ),
    )(lengths, x, cot, gains[0], gains[1], *square, wo, gains[2], gains[3], we, wc, wp, wu,
      *tables, *shards)


def coarse_kernel(*refs):
    (lengths, c0g, dcg, s, m, cot, c_gain, c_shift, w_gain, w_shift, fqkv, fo, fe, fc, wp, wu,
     cosine, sine) = refs[:18]
    (mixed, ds, pool_rows, lift_rows, stack) = refs[18:23]
    (c0, c1, b1, b2, dr, q, k, v, o, level, d_out, act, d_pre, total, top, d_pair, thin, kept_act,
     kept_pre) = refs[23:]
    z = lax.axis_index("head")
    own_lane = pl.ds(pl.multiple_of(z * 128, 128), 128)
    own_rows = pl.ds(pl.multiple_of(z * 128, 128), 128)

    def row_chunks(body):
        def run(step, carry):
            body(pl.ds(pl.multiple_of(step * 176, 16), 176))
            return carry

        lax.fori_loop(0, 3, run, 0)

    for part in range(4):
        base = 128 * part
        c0[pl.ds(base, 128), :] = c0g[part, pl.ds(0, 128), :].astype(WIDE)
        dr[pl.ds(base, 128), :] = dcg[part]
        if part:
            first = pl.ds(base, 1)
            c0[first, :] = c0[first, :] + c0g[part - 1, pl.ds(128, 16), :].astype(WIDE)[:1]
    c0[pl.ds(512, 16), :] = c0g[3, pl.ds(128, 16), :].astype(WIDE)
    dr[pl.ds(512, 16), :] = jnp.zeros((16, WIDTH), LOW)

    def first_norm(here):
        b1[here, :] = norm(c0[here, :], c_gain[...], c_shift[...]).astype(LOW)

    row_chunks(first_norm)
    for ref in (q, k, v):
        ref[pl.ds(SHORT, 640 - SHORT), :] = jnp.zeros((640 - SHORT, WIDTH), LOW)

    def attend(pair, carry):
        lane = pl.ds(pl.multiple_of(pair * 128, 128), 128)
        both = dot(b1[...], fqkv[pair])
        cos, sin = cosine[...], sine[...]
        rows = pl.ds(0, SHORT)
        q[rows, lane] = (turn(both[:, :128], cos, sin) * 0.125).astype(LOW)
        k[rows, lane] = turn(both[:, 128:256], cos, sin).astype(LOW)
        v[rows, lane] = both[:, 256:].astype(LOW)
        for tile in range(5):
            here = pl.ds(128 * tile, 128 if tile < 4 else 16)
            mixed_tile, tops = attend_tile(q[here, lane], k, v, lane, 128 * tile, 128, 0)
            o[here, lane] = mixed_tile.astype(LOW)
            level[pair, :, here] = tops
        return carry

    lax.fori_loop(0, 4, attend, 0)

    def second_norm(here):
        value = c0[here, :]
        for part in range(4):
            value = value + dot(o[here, 128 * part : 128 * part + 128], fo[part])
        c1[here, :] = value
        b2[here, :] = norm(value, w_gain[...], w_shift[...]).astype(LOW)

    row_chunks(second_norm)
    total[...] = jnp.zeros_like(total)
    top[...] = c1[own_rows, :]

    def widen(keep, step, carry):
        slot = lax.rem(z + step // 2, 4)
        lane = pl.ds(pl.multiple_of(lax.rem(step, 2) * 256, 256), 256)
        value, slope = gelu_parts(dot(b2[...], fe[slot, :, lane]))
        act[...] = value.astype(LOW)
        d_pre[...] = (slope * dot_nt(dr[...], fc[slot, lane, :])).astype(LOW)
        if keep:
            kept_act[:, lane] = act[...]
            kept_pre[:, lane] = d_pre[...]
        top[...] += dot(act[own_rows, :], fc[slot, lane, :])
        total[...] += dot_nt(d_pre[...], fe[slot, :, lane])
        return carry

    lax.fori_loop(0, 2, functools.partial(widen, True), 0)
    lax.fori_loop(2, 8, functools.partial(widen, False), 0)

    crest = top[...].astype(LOW)
    valid = (rows_iota((OWN, 128)) + z * OWN < lengths[0]).astype(WIDE)
    for r in range(3):
        lifted = dot(crest, wu[:, 512 * r : 512 * r + 512])
        for part in range(4):
            thin[part, pl.ds(8 + r, 128, 3), :] = lifted[:, 128 * part : 128 * part + 128]
    for part in range(4):
        lane = slice(128 * part, 128 * part + 128)
        mixed[:, lane] = (valid * (s[:, lane] + thin[part, pl.ds(8, OWN), :])).astype(LOW)
        thin[part, pl.ds(8, OWN), :] = cot[:, lane].astype(WIDE) * valid

    def every_third(first, count):
        pieces = [thin[part, pl.ds(first, count, 3), :].astype(LOW) for part in range(4)]
        return jnp.concatenate(pieces, axis=1)

    for r in range(3):
        lift_rows[512 * r : 512 * r + 512, :] = dot_tn(crest, every_third(8 + r, 128)).astype(LOW)

    stack[:, 512:1024] = dot_tn(b2[...], kept_pre[...]).astype(LOW)
    stack[:, 1024:1536] = dot_tn(kept_act[...], dr[...]).astype(LOW)
    sums = [jnp.zeros((1, WIDTH), WIDE) for _ in range(4)]
    for step in range(3):
        here = pl.ds(176 * step, 176)
        grad = total[here, :]
        back, unit_grad = norm_back(c1[here, :], w_gain[...], grad)
        sums[2] = sums[2] + jnp.sum(unit_grad, axis=0, keepdims=True)
        sums[3] = sums[3] + jnp.sum(grad, axis=0, keepdims=True)
        back = dr[here, :].astype(WIDE) + back
        c1[here, :] = back
        b2[here, :] = back.astype(LOW)
    output_grad = dot_tn(o[:, own_lane], b2[...]).astype(LOW)
    for part in range(4):
        stack[128 * part : 128 * part + 128, 384:512] = output_grad[:, 128 * part : 128 * part + 128]
    total[...] = jnp.zeros_like(total)

    def attend_back(pair, carry):
        lane = pl.ds(pl.multiple_of(pair * 128, 128), 128)
        d_out[...] = dot_nt(b2[...], fo[pair]).astype(LOW)
        deltas = pair_sums(d_out[...].astype(WIDE) * o[:, lane].astype(WIDE))
        d_pair[...] = jnp.zeros_like(d_pair)
        for tile in range(5):
            here = pl.ds(128 * tile, 128 if tile < 4 else 16)
            near = pl.ds(128 * tile, 128)
            tops = level[pair, :, here]
            delta = deltas[:, 128 * tile : 128 * tile + here.size]
            d_q, d_k, d_v = attend_back_block(
                q[here, lane], d_out[here, :], k[near, lane], v[near, lane], tops, delta, 0
            )
            d_pair[near, 128:256] = d_pair[near, 128:256] + d_k
            d_pair[near, 256:] = d_pair[near, 256:] + d_v
            if tile:
                past = pl.ds(0, 128 * tile)
                more, d_k, d_v = attend_back_block(
                    q[here, lane], d_out[here, :], k[past, lane], v[past, lane], tops, delta, None
                )
                d_q = d_q + more
                d_pair[past, 128:256] = d_pair[past, 128:256] + d_k
                d_pair[past, 256:] = d_pair[past, 256:] + d_v
            d_pair[here, :128] = d_q
        cos, sin = cosine[...], -sine[...]
        rows = pl.ds(0, SHORT)
        d_three = jnp.concatenate(
            [
                turn(d_pair[rows, :128], cos, sin).astype(LOW),
                turn(d_pair[rows, 128:256], cos, sin).astype(LOW),
                d_pair[rows, 256:].astype(LOW),
            ],
            axis=1,
        )
        total[...] += dot_nt(d_three, fqkv[pair])

        @pl.when(pair == z)
        def keep():
            stack[:, :384] = dot_tn(b1[...], d_three).astype(LOW)

        return carry

    lax.fori_loop(0, 4, attend_back, 0)

    for step in range(3):
        here = pl.ds(176 * step, 176)
        grad = total[here, :]
        back, unit_grad = norm_back(c0[here, :], c_gain[...], grad)
        sums[0] = sums[0] + jnp.sum(unit_grad, axis=0, keepdims=True)
        sums[1] = sums[1] + jnp.sum(grad, axis=0, keepdims=True)
        b1[here, :] = (c1[here, :] + back).astype(LOW)
    stack[:, 1536:] = jnp.zeros((WIDTH, WIDTH), LOW)
    stack[:16, 1536:] = jnp.concatenate(sums + [jnp.zeros((12, WIDTH), WIDE)], axis=0).astype(LOW)

    down = b1[pl.ds(pl.multiple_of(z * 128, 128), PART), :]
    for part in range(4):
        lane = slice(128 * part, 128 * part + 128)
        thin[part, pl.ds(0, 8), :] = jnp.zeros((8, 128), WIDE)
        thin[part, pl.ds(392, 48), :] = jnp.zeros((48, 128), WIDE)
        thin[part, pl.ds(8, OWN), :] = m[:, lane].astype(WIDE)
    for r in range(3):
        pool_rows[512 * r : 512 * r + 512, :] = dot_tn(every_third(6 + r, PART), down).astype(LOW)
    for r in range(3):
        back = dot_nt(down, wp[512 * r : 512 * r + 512, :])
        for part in range(4):
            thin[part, pl.ds(6 + r, PART, 3), :] = back[:, 128 * part : 128 * part + 128]
    for part in range(4):
        lane = slice(128 * part, 128 * part + 128)
        ds[:, lane] = valid * (cot[:, lane].astype(WIDE) + thin[part, pl.ds(8, OWN), :])


def coarse(lengths, c0g, dcg, s, m, cot, gains, fulls, wp, wu, tables):
    def shape(*dims, kind=LOW):
        return jax.ShapeDtypeStruct(dims, kind)

    vmem = pl.BlockSpec(memory_space=VMEM)
    return pl.pallas_call(
        coarse_kernel,
        out_shape=[
            shape(OWN, WIDTH),
            shape(OWN, WIDTH, kind=WIDE),
            shape(ROWS, WIDTH),
            shape(ROWS, WIDTH),
            shape(WIDTH, HIDDEN),
        ],
        in_specs=[pl.BlockSpec(memory_space=pltpu.SMEM)] + [vmem] * 17,
        out_specs=[vmem] * 5,
        scratch_shapes=[
            VMEM((SHORT, WIDTH), WIDE),
            VMEM((SHORT, WIDTH), WIDE),
            VMEM((SHORT, WIDTH), LOW),
            VMEM((SHORT, WIDTH), LOW),
            VMEM((SHORT, WIDTH), LOW),
            VMEM((640, WIDTH), LOW),
            VMEM((640, WIDTH), LOW),
            VMEM((640, WIDTH), LOW),
            VMEM((SHORT, WIDTH), LOW),
            VMEM((4, 8, 640), WIDE),
            VMEM((SHORT, 128), LOW),
            VMEM((SHORT, 256), LOW),
            VMEM((SHORT, 256), LOW),
            VMEM((SHORT, WIDTH), WIDE),
            VMEM((128, WIDTH), WIDE),
            VMEM((640, OWN), WIDE),
            VMEM((4, 440, 128), WIDE),
            VMEM((SHORT, WIDTH), LOW),
            VMEM((SHORT, WIDTH), LOW),
        ],
        compiler_params=pltpu.CompilerParams(vmem_limit_bytes=60 * 2**20),
    )(lengths, c0g, dcg, s, m, cot, *gains, *fulls, wp, wu, *tables)


def backward_kernel(*refs):
    (x, ds, h, a2, act, slope, o_own, a_row, a_gain, a_shift, f_gain, wq, wk, wv, wo, we, wc, a1, q, k, v,
     o, level, pool_rows, lift_rows, cosine, sine) = refs[:27]
    (x_grad, stack, late) = refs[27:30]
    (low, d_pre, dh, d_own, d_heads, d_three, turned, parts, landing, wqkv, send_sem, recv_sem) = refs[30:]
    coords = my_coords()
    z = coords["z"]
    others = [moved(coords, "z", step) for step in (1, 3, 2)]
    copies = Copies(send_sem, recv_sem)
    lane = pl.ds(pl.multiple_of(z * 128, 128), 128)
    meet(coords, ("z",))
    for place, weight in enumerate((wq, wk, wv)):
        wqkv[:, 128 * place : 128 * place + 128] = weight[:, lane]

    low[...] = ds[...].astype(LOW)

    def widen_back(step, carry):
        here = pl.ds(pl.multiple_of(step * 256, 256), 256)
        back = (slope[:, here].astype(WIDE) * dot_nt(low[...], wc[here, :])).astype(LOW)
        d_pre[:, here] = back
        stack[here, :512] = dot_tn(act[:, here], low[...]).astype(LOW)
        down = pl.ds(pl.multiple_of(lax.div(step, 2) * 512, 512), 512)
        across = pl.ds(pl.multiple_of(512 + lax.rem(step, 2) * 256, 256), 256)
        stack[down, across] = dot_tn(a2[...], back).astype(LOW)
        return carry

    lax.fori_loop(0, HIDDEN // 256, widen_back, 0)
    for part in range(2):
        here = slice(256 * part, 256 * part + 256)
        dh[:, here] = dot_nt(d_pre[...], we[here, :])
    sums = [jnp.zeros((1, WIDTH), WIDE) for _ in range(2)]
    for step in range(3):
        here = pl.ds(128 * step, 128)
        grad = dh[here, :]
        back, unit_grad = norm_back(h[here, :], f_gain[...], grad)
        sums[0] = sums[0] + jnp.sum(unit_grad, axis=0, keepdims=True)
        sums[1] = sums[1] + jnp.sum(grad, axis=0, keepdims=True)
        back = ds[here, :] + back
        dh[here, :] = back
        low[here, :] = back.astype(LOW)
    d_own[...] = dot_nt(low[...], wo[...]).astype(LOW)

    head_moves = [
        copies.remote(
            d_own.at[:, pl.ds(pl.multiple_of(other["z"] * 128, 128), 128)],
            d_heads.at[pl.ds(pl.multiple_of(z * OWN, OWN), OWN), :],
            other,
        )
        for other in others
    ]
    d_heads[pl.ds(pl.multiple_of(z * OWN, OWN), OWN), :] = d_own[:, lane]
    stack[1536:, 1024:1536] = dot_tn(o_own[...], low[...]).astype(LOW)
    stack[:1536, 1024:1536] = pool_rows[...]
    stack[:1536, 1536:] = lift_rows[...]
    stack[1536:, 1536:] = jnp.zeros((512, WIDTH), LOW)
    stack[1536:1552, 1536:] = jnp.concatenate(sums + [jnp.zeros((14, WIDTH), WIDE)], 0).astype(LOW)
    d_three[...] = jnp.zeros_like(d_three)
    for move in head_moves:
        move.wait_recv()

    for block in range(4):
        here = pl.ds(OWN * block, OWN)
        deltas = pair_sums(d_heads[here, :].astype(WIDE) * o[here, :].astype(WIDE))
        tops = level[:, here]

        def add_block(there, offset):
            d_q, d_k, d_v = attend_back_block(
                q[here, :], d_heads[here, :], k[there, :], v[there, :], tops, deltas, offset
            )
            d_three[here, :128] = d_three[here, :128] + d_q
            d_three[there, 128:256] = d_three[there, 128:256] + d_k
            d_three[there, 256:] = d_three[there, 256:] + d_v

        def past(step, carry):
            add_block(pl.ds(pl.multiple_of(step * OWN, OWN), OWN), None)
            return carry

        if block:
            lax.fori_loop(0, block, past, 0)
        add_block(here, 0)

    def finish_block(index):
        here = pl.ds(pl.multiple_of(index * OWN, OWN), OWN)
        cos, sin = cosine[here, :], -sine[here, :]
        turned[here, :128] = turn(d_three[here, :128], cos, sin).astype(LOW)
        turned[here, 128:256] = turn(d_three[here, 128:256], cos, sin).astype(LOW)
        turned[here, 256:] = d_three[here, 256:].astype(LOW)
        return dot_nt(turned[here, :], wqkv[...])

    part_moves = []
    for step, other in enumerate((others[2], others[0], others[1])):
        parts[step] = finish_block(other["z"]).astype(LOW)
        part_moves.append(copies.remote(parts.at[step], landing.at[step], other))
    grad_own = finish_block(z)
    d_weight = dot_tn(a1[...], turned[...])
    late[:, :OWN] = d_weight.astype(LOW)
    column_sums = jnp.sum(turned[...].astype(WIDE), axis=0, keepdims=True)
    weight = wqkv[...].astype(WIDE)
    shift_grad = jnp.sum(weight * column_sums, axis=1, keepdims=True)
    whole = jnp.sum(weight * d_weight, axis=1, keepdims=True)
    gain_grad = (whole - a_shift[...] * shift_grad) * (1.0 / a_gain[...])
    lanes = lanes_iota((WIDTH, 128))
    late[:, OWN:] = jnp.where(
        lanes == 0, gain_grad, jnp.where(lanes == 1, shift_grad, 0.0)
    ).astype(LOW)
    for move in part_moves:
        move.wait_recv()
    grad_own = grad_own + sum(landing[step].astype(WIDE) for step in range(3))
    x_grad[...] = grad_own
    for step in range(3):
        here = pl.ds(128 * step, 128)
        back, _ = norm_back(x[here, :].astype(WIDE), a_row[...], x_grad[here, :])
        x_grad[here, :] = dh[here, :] + back
    copies.finish()


def backward(x, ds, saved, gains, weights, attention, rows, tables):
    def shape(*dims, kind=LOW):
        return jax.ShapeDtypeStruct(dims, kind)

    vmem = pl.BlockSpec(memory_space=VMEM)
    operands = (x, ds, *saved, *gains, *weights, *attention, *rows, *tables)
    return pl.pallas_call(
        backward_kernel,
        out_shape=[
            shape(OWN, WIDTH, kind=WIDE),
            shape(HIDDEN, HIDDEN),
            shape(WIDTH, WIDTH),
        ],
        in_specs=[vmem] * len(operands),
        out_specs=[vmem] * 3,
        scratch_shapes=[
            VMEM((OWN, WIDTH), LOW),
            VMEM((OWN, HIDDEN), LOW),
            VMEM((OWN, WIDTH), WIDE),
            VMEM((OWN, WIDTH), LOW),
            VMEM((ROWS, 128), LOW),
            VMEM((ROWS, OWN), WIDE),
            VMEM((ROWS, OWN), LOW),
            VMEM((3, OWN, WIDTH), LOW),
            VMEM((3, OWN, WIDTH), LOW),
            VMEM((WIDTH, OWN), LOW),
            pltpu.SemaphoreType.DMA((6,)),
            pltpu.SemaphoreType.DMA((6,)),
        ],
        compiler_params=pltpu.CompilerParams(
            collective_id=2, has_side_effects=True, vmem_limit_bytes=60 * 2**20
        ),
    )(*operands)


def body(
    inputs,
    lengths,
    cotangent,
    attention_gain,
    attention_shift,
    query_weight,
    key_weight,
    value_weight,
    output_weight,
    feedforward_gain,
    feedforward_shift,
    expand_weight,
    contract_weight,
    pooling_weight,
    coarse_gain,
    coarse_shift,
    coarse_query,
    coarse_key,
    coarse_value,
    coarse_output,
    widen_gain,
    widen_shift,
    coarse_expand,
    coarse_contract,
    upsample_weight,
):
    def row(vector):
        return vector.reshape(1, -1)

    tables = turn_tables()
    square = (query_weight, key_weight, value_weight)
    (a1, q, k, v, o, level, o_own, h, a2, act, slope, s, m, c0g, dcg, *fulls) = forward(
        lengths,
        inputs,
        cotangent,
        (row(attention_gain), row(attention_shift), row(feedforward_gain), row(feedforward_shift)),
        square,
        output_weight,
        expand_weight,
        contract_weight,
        pooling_weight,
        upsample_weight,
        tables,
        (coarse_query, coarse_key, coarse_value, coarse_output, coarse_expand, coarse_contract),
    )
    mixed, ds, pool_rows, lift_rows, coarse_stack = coarse(
        lengths,
        c0g,
        dcg,
        s,
        m,
        cotangent,
        (row(coarse_gain), row(coarse_shift), row(widen_gain), row(widen_shift)),
        fulls,
        pooling_weight,
        upsample_weight,
        (tables[0][:SHORT], tables[1][:SHORT]),
    )
    input_grad, stack, late = backward(
        inputs,
        ds,
        (h, a2, act, slope, o_own),
        (
            row(attention_gain),
            attention_gain.reshape(-1, 1),
            attention_shift.reshape(-1, 1),
            row(feedforward_gain),
        ),
        (*square, output_weight, expand_weight, contract_weight),
        (a1, q, k, v, o, level),
        (pool_rows, lift_rows),
        tables,
    )
    streams = (
        Stream(0, 0, 768, ("core", "x", "y", "z")),
        Stream(0, 768, 1280, ("core", "y", "z", "x")),
        Stream(0, 1280, 2048, ("core", "z", "x", "y")),
        Stream(1, 0, 2048, ("core", "y", "x")),
        Stream(2, 0, 512, ("core", "x", "y"), True),
    )
    total, coarse_total, late_total = sum_gradients([stack, coarse_stack, late], streams, 0)
    total = total.astype(WIDE)
    coarse_total = coarse_total.astype(WIDE)
    late_total = late_total.astype(WIDE)
    squares = [
        jnp.concatenate([late_total[i, :, 128 * j : 128 * j + 128] for i in range(4)], axis=1)
        for j in range(3)
    ]
    vectors = jnp.sum(late_total[:, :, 384:386], axis=0)
    expand_total = jnp.concatenate(
        [total[512 * i : 512 * i + 512, 512:1024] for i in range(4)], axis=1
    )
    upsample_total = jnp.concatenate(
        [total[512 * i : 512 * i + 512, 1536:] for i in range(3)], axis=1
    )
    return (
        mixed,
        input_grad,
        vectors[:, 0],
        vectors[:, 1],
        *squares,
        total[1536:, 1024:1536],
        total[1536, 1536:],
        total[1537, 1536:],
        expand_total,
        total[:, :512],
        total[:1536, 1024:1536],
        coarse_total[0, 1536:],
        coarse_total[1, 1536:],
        coarse_total[:, :128],
        coarse_total[:, 128:256],
        coarse_total[:, 256:384],
        jnp.concatenate([coarse_total[128 * i : 128 * i + 128, 384:512] for i in range(4)], axis=1),
        coarse_total[2, 1536:],
        coarse_total[3, 1536:],
        coarse_total[:, 512:1024],
        coarse_total[:, 1024:1536],
        upsample_total,
    )


def solution(mesh):
    in_specs = (
        P(("seq", "head"), None),
        P("seq"),
        P(("seq", "head"), None),
        P(),
        P(),
        P(),
        P(),
        P(),
        P(),
        P(),
        P(),
        P(),
        P(),
        P(),
        P(),
        P(),
        P(None, "head"),
        P(None, "head"),
        P(None, "head"),
        P("head", None),
        P(),
        P(),
        P(None, "head"),
        P("head", None),
        P(),
    )
    out_specs = (
        P(("seq", "head"), None),
        P(("seq", "head"), None),
        P(),
        P(),
        P(),
        P(),
        P(),
        P(),
        P(),
        P(),
        P(),
        P(),
        P(),
        P(),
        P(),
        P(None, "head"),
        P(None, "head"),
        P(None, "head"),
        P("head", None),
        P(),
        P(),
        P(None, "head"),
        P("head", None),
        P(),
    )
    return jax.shard_map(body, mesh=mesh, in_specs=in_specs, out_specs=out_specs, check_vma=False)
```

```python
import functools
import math

import jax
import jax.numpy as jnp
import numpy as np
from jax import lax
from jax.experimental import pallas as pl
from jax.experimental.pallas import tpu as pltpu
from jax.sharding import PartitionSpec as P

MESH = pl.DeviceIdType.MESH
VMEM = pltpu.VMEM
LOW = jnp.bfloat16
WIDE = jnp.float32
EPSILON = 1e-05
OWN = 384
ROWS = 1536
WIDTH = 512
HIDDEN = 2048
SHORT = 528
PART = 144
SIZES = {"core": 2, "x": 4, "y": 4, "z": 4}


def turn_tables():
    frequency = np.exp(np.arange(32, dtype=np.float32) * np.float32(-math.log(10000.0) / 32))
    angles = np.arange(ROWS, dtype=np.float32)[:, None] * frequency.astype(np.float32)[None, :]
    cosine = np.cos(angles.astype(np.float64)).astype(np.float32)
    sine = np.sin(angles.astype(np.float64)).astype(np.float32)
    return np.tile(cosine, (1, 4)), np.concatenate([-sine, sine, -sine, sine], axis=1)


def my_coords():
    seq = lax.axis_index("seq")
    return {
        "core": lax.rem(seq, 2),
        "y": lax.rem(lax.div(seq, 2), 4),
        "x": lax.div(seq, 8),
        "z": lax.axis_index("head"),
    }


def moved(coords, axis, step):
    other = dict(coords)
    other[axis] = lax.rem(coords[axis] + step, SIZES[axis])
    return other


def device_of(coords):
    return {
        "seq": (coords["x"] * 4 + coords["y"]) * 2 + coords["core"],
        "head": coords["z"],
    }


def meet(coords, axes):
    barrier = pltpu.get_barrier_semaphore()
    count = 0
    for axis in axes:
        for step in range(1, SIZES[axis]):
            pl.semaphore_signal(
                barrier,
                inc=1,
                device_id=device_of(moved(coords, axis, step)),
                device_id_type=MESH,
            )
            count += 1
    pl.semaphore_wait(barrier, count)


def dot(left, right):
    return lax.dot_general(left, right, (((1,), (0,)), ((), ())), preferred_element_type=WIDE)


def dot_nt(left, right):
    return lax.dot_general(left, right, (((1,), (1,)), ((), ())), preferred_element_type=WIDE)


def dot_tn(left, right):
    return lax.dot_general(left, right, (((0,), (0,)), ((), ())), preferred_element_type=WIDE)


def lanes_iota(shape):
    return lax.broadcasted_iota(jnp.int32, shape, len(shape) - 1)


def rows_iota(shape):
    return lax.broadcasted_iota(jnp.int32, shape, 0)


def standard(values):
    centred = values - jnp.mean(values, axis=-1, keepdims=True)
    scale = lax.rsqrt(jnp.mean(centred * centred, axis=-1, keepdims=True) + EPSILON)
    return centred * scale, scale


def norm(values, gain, shift):
    return standard(values)[0] * gain + shift


def norm_back(values, gain, grad):
    unit, scale = standard(values)
    inner = grad * gain
    first = jnp.mean(inner, axis=-1, keepdims=True)
    second = jnp.mean(inner * unit, axis=-1, keepdims=True)
    return scale * (inner - first - unit * second), grad * unit


def turn(values, cosine, sine):
    lane = lanes_iota(values.shape)
    other = jnp.where(
        lax.rem(lane, 64) < 32, pltpu.roll(values, 96, 1), pltpu.roll(values, 32, 1)
    )
    return values * cosine + other * sine


def gelu_parts(values):
    half = 0.5 + 0.5 * lax.erf(values * math.sqrt(0.5))
    bell = jnp.exp(values * values * -0.5) * (1.0 / math.sqrt(2.0 * math.pi))
    return values * half, half + values * bell


def head_lanes(head, values):
    return jnp.where(lanes_iota(values.shape) // 64 == head, values, jnp.zeros_like(values))


def by_head(first, second):
    return jnp.where(lanes_iota(first.shape) < 64, first, second)


def head_rows(columns):
    shape = (8, 128)
    pick = (lanes_iota(shape) == rows_iota(shape) * 64).astype(WIDE)
    return lax.dot_general(
        pick,
        columns,
        (((1,), (1,)), ((), ())),
        precision=lax.Precision.HIGHEST,
        preferred_element_type=WIDE,
    )


def attend_tile(q_tile, k_ref, v_ref, lanes, before, width, offset, key_limit=None):
    outs, tops = [], []
    rows = q_tile.shape[0]
    for head in range(2):
        query = head_lanes(head, q_tile)
        last = pl.ds(before, width)
        near = dot_nt(query, k_ref[last, lanes])
        keep = lanes_iota(near.shape) <= rows_iota(near.shape) + offset
        near = jnp.where(keep, near, -1e30)
        top = jnp.max(near, axis=-1, keepdims=True)
        if before:
            far = dot_nt(query, k_ref[pl.ds(0, before), lanes])
            top = jnp.maximum(top, jnp.max(far, axis=-1, keepdims=True))
        near = jnp.exp(near - top)
        total = jnp.sum(near, axis=-1, keepdims=True)
        mixed = dot(near.astype(LOW), v_ref[last, lanes])
        if before:
            far = jnp.exp(far - top)
            total = total + jnp.sum(far, axis=-1, keepdims=True)
            mixed = mixed + dot(far.astype(LOW), v_ref[pl.ds(0, before), lanes])
        outs.append(mixed * (1.0 / total))
        tops.append(top + jnp.log(total))
    shape = (rows, 128)
    level = by_head(jnp.broadcast_to(tops[0], shape), jnp.broadcast_to(tops[1], shape))
    return by_head(outs[0], outs[1]), head_rows(level)


class Copies:
    def __init__(self, send_sem, recv_sem):
        self.send_sem, self.recv_sem, self.count, self.sent = send_sem, recv_sem, 0, []

    def remote(self, source, target, other):
        place = self.count
        self.count += 1
        move = pltpu.make_async_remote_copy(
            src_ref=source,
            dst_ref=target,
            send_sem=self.send_sem.at[place],
            recv_sem=self.recv_sem.at[place],
            device_id=device_of(other),
            device_id_type=MESH,
        )
        move.start()
        self.sent.append(move)
        return move

    def local(self, source, target):
        place = self.count
        self.count += 1
        move = pltpu.make_async_copy(source, target, self.recv_sem.at[place])
        move.start()
        return move

    def finish(self):
        for move in self.sent:
            move.wait_send()


def pair_sums(columns):
    shape = (8, 128)
    pick = (lanes_iota(shape) // 64 == rows_iota(shape)).astype(WIDE)
    return lax.dot_general(
        pick,
        columns,
        (((1,), (1,)), ((), ())),
        precision=lax.Precision.HIGHEST,
        preferred_element_type=WIDE,
    )


def attend_back_block(q_tile, d_tile, key, value, tops, deltas, offset):
    d_query = []
    d_key = d_value = None
    for head in range(2):
        query = head_lanes(head, q_tile)
        d_out = head_lanes(head, d_tile)
        probs = jnp.exp(dot_nt(key, query) - tops[head : head + 1])
        if offset is not None:
            probs = jnp.where(rows_iota(probs.shape) <= lanes_iota(probs.shape) + offset, probs, 0.0)
        d_score = (probs * (dot_nt(value, d_out) - deltas[head : head + 1])).astype(LOW)
        more_value = dot(probs.astype(LOW), d_out)
        more_key = dot(d_score, query)
        d_value = more_value if d_value is None else d_value + more_value
        d_key = more_key if d_key is None else d_key + more_key
        d_query.append(dot_tn(d_score, key))
    return by_head(*d_query) * 0.125, d_key, d_value


def attend_tiles(items, before, width, offset):
    last, first = pl.ds(before, width), pl.ds(0, before)
    chains = [(item, head) for item in items for head in range(2)]
    queries = [head_lanes(head, item[0]) for item, head in chains]
    near = [dot_nt(query, item[1][last, item[3]]) for query, (item, _) in zip(queries, chains)]
    keep = [
        lanes_iota(near[0].shape) <= rows_iota(near[0].shape) + shift
        for shift in (offset if isinstance(offset, tuple) else (offset,) * len(items))
    ]
    near = [jnp.where(keep[place // 2], scores, -1e30) for place, scores in enumerate(near)]
    tops = [jnp.max(scores, axis=-1, keepdims=True) for scores in near]
    if before:
        far = [dot_nt(query, item[1][first, item[3]]) for query, (item, _) in zip(queries, chains)]
        tops = [jnp.maximum(t, jnp.max(s, axis=-1, keepdims=True)) for t, s in zip(tops, far)]
        far = [jnp.exp(scores - t) for scores, t in zip(far, tops)]
    near = [jnp.exp(scores - t) for scores, t in zip(near, tops)]
    totals = [jnp.sum(probs, axis=-1, keepdims=True) for probs in near]
    mixed = [dot(probs.astype(LOW), item[2][last, item[3]]) for probs, (item, _) in zip(near, chains)]
    if before:
        totals = [t + jnp.sum(probs, axis=-1, keepdims=True) for t, probs in zip(totals, far)]
        mixed = [
            m + dot(probs.astype(LOW), item[2][first, item[3]])
            for m, probs, (item, _) in zip(mixed, far, chains)
        ]
    outs = [m * (1.0 / t) for m, t in zip(mixed, totals)]
    levels = [t + jnp.log(total) for t, total in zip(tops, totals)]
    shape = (items[0][0].shape[0], 128)
    results = []
    for place in range(len(items)):
        a, b = 2 * place, 2 * place + 1
        level = by_head(jnp.broadcast_to(levels[a], shape), jnp.broadcast_to(levels[b], shape))
        results.append((by_head(outs[a], outs[b]), head_rows(level)))
    return results


def attend_back_blocks(items, offset):
    chains = [(item, head) for item in items for head in range(2)]
    queries = [head_lanes(head, item[0]) for item, head in chains]
    d_outs = [head_lanes(head, item[1]) for item, head in chains]
    scores = [dot_nt(item[2], query) for query, (item, _) in zip(queries, chains)]
    d_probs = [dot_nt(item[3], d_out) for d_out, (item, _) in zip(d_outs, chains)]
    probs = [
        jnp.exp(score - item[4][head : head + 1]) for score, (item, head) in zip(scores, chains)
    ]
    if offset is not None:
        keep = rows_iota(probs[0].shape) <= lanes_iota(probs[0].shape) + offset
        probs = [jnp.where(keep, prob, 0.0) for prob in probs]
    d_scores = [
        (prob * (d_prob - item[5][head : head + 1])).astype(LOW)
        for prob, d_prob, (item, head) in zip(probs, d_probs, chains)
    ]
    d_values = [dot(prob.astype(LOW), d_out) for prob, d_out in zip(probs, d_outs)]
    d_keys = [dot(d_score, query) for d_score, query in zip(d_scores, queries)]
    d_queries = [dot_tn(d_score, item[2]) for d_score, (item, _) in zip(d_scores, chains)]
    return [
        (
            by_head(d_queries[i], d_queries[i + 1]) * 0.125,
            d_keys[i] + d_keys[i + 1],
            d_values[i] + d_values[i + 1],
        )
        for i in range(0, len(chains), 2)
    ]


def front_kernel(*refs):
    (lengths, x, cot, a_gain, a_shift, f_gain, f_shift, c_gain, c_shift, w_gain, w_shift) = refs[:11]
    (wq_hbm, wk_hbm, wv_hbm, wo_hbm, we_hbm, wc_hbm, wp_hbm, wu_hbm, cos_hbm, sin_hbm) = refs[11:21]
    shards = refs[21:27]
    out_refs = refs[27:43]
    (a1, q, k, v, o, level, o_own, h, a2, act, slope, wqkv, mixed, ds, early, stack) = refs[43:59]
    (wo, we, wc, wp, wu, cosine, sine, landing, thin, s, m, c0g, dcg, fqkv, fo, fe, fc) = refs[59:76]
    (c0, c1, b1, b2, dr, cq, ck, cv, co, clevel, d_out, c_act, d_pre, total, top, d_pair, d_three,
     kept_act, kept_pre, send_sem, recv_sem) = refs[76:]
    saved = {}

    def save(place, source):
        saved[place] = copies.local(source, out_refs[place])

    coords = my_coords()
    z = coords["z"]
    core = coords["core"]
    right, left, far = (moved(coords, "z", step) for step in (1, 3, 2))
    copies = Copies(send_sem, recv_sem)
    lane = pl.ds(pl.multiple_of(z * 128, 128), 128)
    first_loads = [
        copies.local(weight.at[:, lane], wqkv.at[:, pl.ds(128 * place, 128)])
        for place, weight in enumerate((wq_hbm, wk_hbm, wv_hbm))
    ] + [copies.local(cos_hbm, cosine), copies.local(sin_hbm, sine)]
    loads = [
        copies.local(source, target)
        for source, target in ((wu_hbm, wu), (wo_hbm, wo), (we_hbm, we), (wc_hbm, wc), (wp_hbm, wp))
    ]
    own_weights = [
        copies.local(shard, full)
        for shard, full in zip(
            shards,
            [fqkv.at[z, :, pl.ds(128 * place, 128)] for place in range(3)]
            + [fo.at[z], fe.at[z], fc.at[z]],
        )
    ]
    meet(coords, ("core", "x", "y", "z"))
    low, high = pl.ds(0, OWN // 2), pl.ds(OWN // 2, OWN // 2)
    to_right = copies.remote(x.at[low], landing.at[0, low], right)
    to_left = copies.remote(x.at[high], landing.at[1, high], left)
    to_right_more = copies.remote(x.at[high], landing.at[0, high], right)
    to_left_more = copies.remote(x.at[low], landing.at[1, low], left)

    def project(block, index):
        start = pl.multiple_of(index * OWN, OWN)

        def rows_of(step, carry):
            here = pl.multiple_of(step * 128, 128)
            there = pl.ds(pl.multiple_of(start + here, 128), 128)
            values = block[pl.ds(here, 128), :].astype(WIDE)
            a1[there, :] = norm(values, a_gain[...], a_shift[...]).astype(LOW)
            return carry

        lax.fori_loop(0, OWN // 128, rows_of, 0)
        here = pl.ds(start, OWN)
        both = dot(a1[here, :], wqkv[...])
        cos, sin = cosine[here, :], sine[here, :]
        q[here, :] = (turn(both[:, :128], cos, sin) * 0.125).astype(LOW)
        k[here, :] = turn(both[:, 128:256], cos, sin).astype(LOW)
        v[here, :] = both[:, 256:].astype(LOW)

    for load in first_loads:
        load.wait()
    project(x, z)
    to_right.wait_recv()
    far_right = copies.remote(landing.at[0, low], landing.at[2, low], right)
    to_left.wait_recv()
    far_left = copies.remote(landing.at[1, high], landing.at[2, high], left)

    valid = (rows_iota((OWN, 128)) + z * OWN < lengths[0]).astype(WIDE)
    for part in range(4):
        thin[part, pl.ds(0, 8), :] = jnp.zeros((8, 128), WIDE)
        thin[part, pl.ds(392, 48), :] = jnp.zeros((48, 128), WIDE)
        thin[part, pl.ds(8, OWN), :] = cot[:, 128 * part : 128 * part + 128].astype(WIDE) * valid

    def every_third(first, count):
        pieces = [thin[part, pl.ds(first, count, 3), :].astype(LOW) for part in range(4)]
        return jnp.concatenate(pieces, axis=1)

    loads[0].wait()
    lifted_back = sum(
        dot_nt(every_third(8 + r, 128), wu[:, 512 * r : 512 * r + 512]) for r in range(3)
    )
    dcg[z] = lifted_back.astype(LOW)

    to_right_more.wait_recv()
    project(landing.at[0], left["z"])
    to_left_more.wait_recv()
    project(landing.at[1], right["z"])
    far_right.wait_recv()
    far_left.wait_recv()
    project(landing.at[2], far["z"])

    for load in own_weights:
        load.wait()
    z_others = (right, left, far)
    z_sources = (left, right, far)
    pieces = {}
    for place, full in enumerate((fqkv, fe, fc)):
        for way, axis in enumerate(("x", "y")):
            rows = pl.ds(pl.multiple_of(core * 256 + way * 128 + coords[axis] * 32, 32), 32)
            for step, other in enumerate(z_others):
                pieces[place, way, step] = copies.remote(full.at[z, rows], full.at[z, rows], other)
    fo_rows = pl.ds(pl.multiple_of(core * 64, 64), 64)
    fo_moves = [copies.remote(fo.at[z, fo_rows], fo.at[z, fo_rows], other) for other in z_others]

    sent_blocks = send_sem.shape[0] - 4
    got_blocks = recv_sem.shape[0] - 4

    def block_move(target, source):
        return pltpu.make_async_remote_copy(
            src_ref=o.at[pl.ds(pl.multiple_of(target * OWN, OWN), OWN), :],
            dst_ref=o_own.at[:, pl.ds(pl.multiple_of(source * 128, 128), 128)],
            send_sem=send_sem.at[sent_blocks + target],
            recv_sem=recv_sem.at[got_blocks + source],
            device_id=device_of({**coords, "z": target}),
            device_id_type=MESH,
        )

    everything = pl.ds(0, 128)
    for block in reversed(range(4)):
        tiles = [pl.ds(OWN * block + 128 * step, 128) for step in range(3)]
        results = attend_tiles(
            [(q[here, :], k, v, everything) for here in tiles], OWN * block, OWN, (0, 128, 256)
        )
        for here, (mixed_tile, tops) in zip(tiles, results):
            o[here, :] = mixed_tile.astype(LOW)
            level[:, here] = tops

        @pl.when(z != block)
        def send():
            block_move(block, z).start()

    for place, ref in ((0, a1), (1, q), (2, k), (3, v), (4, o), (5, level), (11, wqkv)):
        save(place, ref)
    o_own[:, lane] = o[pl.ds(pl.multiple_of(z * OWN, OWN), OWN), :]

    spread = []
    for place, full in enumerate((fqkv, fe, fc)):
        for way, axis in enumerate(("x", "y")):
            rows = pl.ds(pl.multiple_of(core * 256 + way * 128 + coords[axis] * 32, 32), 32)
            for step, source in enumerate(z_sources):
                pieces[place, way, step].wait_recv()
                part = full.at[source["z"], rows]
                for far_step in range(1, 4):
                    spread.append(copies.remote(part, part, moved(coords, axis, far_step)))
    for step in range(1, 4):
        other = lax.rem(z + step, 4)
        block_move(z, other).wait_recv()
    save(6, o_own)

    for load in loads[1:]:
        load.wait()

    def mix(step, carry):
        here = pl.ds(pl.multiple_of(step * 128, 128), 128)
        hidden = x[here, :].astype(WIDE) + dot(o_own[here, :], wo[...])
        h[here, :] = hidden
        a2[here, :] = norm(hidden, f_gain[...], f_shift[...]).astype(LOW)
        return carry

    lax.fori_loop(0, 3, mix, 0)

    def widen(step, carry):
        here = pl.ds(pl.multiple_of(step * 256, 256), 256)
        value, back = gelu_parts(dot(a2[...], we[:, here]))
        act[:, here] = value.astype(LOW)
        slope[:, here] = back.astype(LOW)
        return carry

    lax.fori_loop(0, HIDDEN // 256, widen, 0)
    for place, ref in ((7, h), (8, a2), (9, act), (10, slope)):
        save(place, ref)

    for part in range(4):
        here = slice(128 * part, 128 * part + 128)
        if part % 2 == 0:
            wide = slice(256 * (part // 2), 256 * (part // 2) + 256)
            summed = h[:, wide] + dot(act[...], wc[:, wide])
            s[:, wide] = summed
        kept = (s[:, here] * valid).astype(LOW)
        m[:, here] = kept
        thin[part, pl.ds(8, OWN), :] = kept.astype(WIDE)
    pooled = sum(
        dot(every_third(6 + r, PART), wp[512 * r : 512 * r + 512, :]) for r in range(3)
    )
    c0g[z] = pooled.astype(LOW)
    c0_moves = [copies.remote(c0g.at[z], c0g.at[z], other) for other in z_others]
    dc_moves = [copies.remote(dcg.at[z], dcg.at[z], other) for other in z_others]
    sibling = moved(coords, "core", 1)
    swaps = []
    for step, source in enumerate(z_sources):
        fo_moves[step].wait_recv()
        part = fo.at[source["z"], fo_rows]
        swaps.append(copies.remote(part, part, sibling))
    for move in spread:
        move.wait_recv()
    half = pl.ds(pl.multiple_of(core * 256, 256), 256)
    for full in (fqkv, fe, fc):
        for source in z_sources:
            part = full.at[source["z"], half]
            swaps.append(copies.remote(part, part, sibling))
    for move in swaps + c0_moves + dc_moves:
        move.wait_recv()

    own_lane = pl.ds(pl.multiple_of(z * 128, 128), 128)
    own_rows = pl.ds(pl.multiple_of(z * 128, 128), 128)

    def row_chunks(body):
        def run(step, carry):
            body(pl.ds(pl.multiple_of(step * 176, 16), 176))
            return carry

        lax.fori_loop(0, 3, run, 0)

    for part in range(4):
        base = 128 * part
        c0[pl.ds(base, 128), :] = c0g[part, pl.ds(0, 128), :].astype(WIDE)
        dr[pl.ds(base, 128), :] = dcg[part]
        if part:
            first = pl.ds(base, 1)
            c0[first, :] = c0[first, :] + c0g[part - 1, pl.ds(128, 16), :].astype(WIDE)[:1]
    c0[pl.ds(512, 16), :] = c0g[3, pl.ds(128, 16), :].astype(WIDE)
    dr[pl.ds(512, 16), :] = jnp.zeros((16, WIDTH), LOW)

    def first_norm(here):
        b1[here, :] = norm(c0[here, :], c_gain[...], c_shift[...]).astype(LOW)

    row_chunks(first_norm)
    for ref in (cq, ck, cv):
        ref[pl.ds(SHORT, 640 - SHORT), :] = jnp.zeros((640 - SHORT, WIDTH), LOW)

    for pair in range(4):
        lane = pl.ds(pair * 128, 128)
        both = dot(b1[...], fqkv[pair])
        cos, sin = cosine[pl.ds(0, SHORT), :], sine[pl.ds(0, SHORT), :]
        rows = pl.ds(0, SHORT)
        cq[rows, lane] = (turn(both[:, :128], cos, sin) * 0.125).astype(LOW)
        ck[rows, lane] = turn(both[:, 128:256], cos, sin).astype(LOW)
        cv[rows, lane] = both[:, 256:].astype(LOW)
    for tile in range(5):
        here = pl.ds(128 * tile, 128 if tile < 4 else 16)
        for pair, (mixed_tile, tops) in enumerate(
            attend_tiles([(cq[here, pl.ds(128 * p, 128)], ck, cv, pl.ds(128 * p, 128)) for p in range(4)], 128 * tile, 128, 0)
        ):
            co[here, pl.ds(128 * pair, 128)] = mixed_tile.astype(LOW)
            clevel[pair, :, here] = tops

    def second_norm(here):
        value = c0[here, :]
        for part in range(4):
            value = value + dot(co[here, 128 * part : 128 * part + 128], fo[part])
        c1[here, :] = value
        b2[here, :] = norm(value, w_gain[...], w_shift[...]).astype(LOW)

    row_chunks(second_norm)
    total[...] = jnp.zeros_like(total)
    top[...] = c1[own_rows, :]

    def widen(keep, step, carry):
        slot = lax.rem(z + step // 2, 4)
        lane = pl.ds(pl.multiple_of(lax.rem(step, 2) * 256, 256), 256)
        value, slope = gelu_parts(dot(b2[...], fe[slot, :, lane]))
        c_act[...] = value.astype(LOW)
        d_pre[...] = (slope * dot_nt(dr[...], fc[slot, lane, :])).astype(LOW)
        if keep:
            kept_act[:, lane] = c_act[...]
            kept_pre[:, lane] = d_pre[...]
        top[...] += dot(c_act[own_rows, :], fc[slot, lane, :])
        total[...] += dot_nt(d_pre[...], fe[slot, :, lane])
        return carry

    lax.fori_loop(0, 2, functools.partial(widen, True), 0)
    lax.fori_loop(2, 8, functools.partial(widen, False), 0)

    def put_early(number, grad):
        for part in range(2):
            down, across = divmod(2 * number + part, 3)
            early[512 * down : 512 * down + 512, 256 * across : 256 * across + 256] = grad[
                :, 256 * part : 256 * part + 256
            ].astype(LOW)

    crest = top[...].astype(LOW)
    for r in range(3):
        lifted = dot(crest, wu[:, 512 * r : 512 * r + 512])
        for part in range(4):
            thin[part, pl.ds(8 + r, 128, 3), :] = lifted[:, 128 * part : 128 * part + 128]
    for part in range(4):
        lane = slice(128 * part, 128 * part + 128)
        mixed[:, lane] = (valid * (s[:, lane] + thin[part, pl.ds(8, OWN), :])).astype(LOW)
        thin[part, pl.ds(8, OWN), :] = cot[:, lane].astype(WIDE) * valid

    for r in range(3):
        put_early(3 + r, dot_tn(crest, every_third(8 + r, 128)))

    save(12, mixed)
    stack[:, 512:1024] = dot_tn(b2[...], kept_pre[...]).astype(LOW)
    stack[:, 1024:1536] = dot_tn(kept_act[...], dr[...]).astype(LOW)
    sums = [jnp.zeros((1, WIDTH), WIDE) for _ in range(4)]
    for step in range(3):
        here = pl.ds(176 * step, 176)
        grad = total[here, :]
        back, unit_grad = norm_back(c1[here, :], w_gain[...], grad)
        sums[2] = sums[2] + jnp.sum(unit_grad, axis=0, keepdims=True)
        sums[3] = sums[3] + jnp.sum(grad, axis=0, keepdims=True)
        back = dr[here, :].astype(WIDE) + back
        c1[here, :] = back
        b2[here, :] = back.astype(LOW)
    output_grad = dot_tn(co[:, own_lane], b2[...]).astype(LOW)
    for part in range(4):
        stack[128 * part : 128 * part + 128, 384:512] = output_grad[:, 128 * part : 128 * part + 128]
    for pair in range(4):
        d_out[:, pl.ds(128 * pair, 128)] = dot_nt(b2[...], fo[pair]).astype(LOW)
    lanes = [pl.ds(128 * pair, 128) for pair in range(4)]
    deltas = [
        pair_sums(d_out[:, lane].astype(WIDE) * co[:, lane].astype(WIDE)) for lane in lanes
    ]
    for tile in range(5):
        here = pl.ds(128 * tile, 128 if tile < 4 else 16)
        near, past = pl.ds(128 * tile, 128), pl.ds(0, 128 * tile)

        def items(there):
            return [
                (
                    cq[here, lane],
                    d_out[here, lane],
                    ck[there, lane],
                    cv[there, lane],
                    clevel[pair, :, here],
                    deltas[pair][:, 128 * tile : 128 * tile + here.size],
                )
                for pair, lane in enumerate(lanes)
            ]

        results = attend_back_blocks(items(near), 0)
        for pair, (d_q, d_k, d_v) in enumerate(results):
            d_pair[pair, here, :128] = d_q
            d_pair[pair, near, 128:256] = d_k
            d_pair[pair, near, 256:] = d_v
        if tile:
            results = attend_back_blocks(items(past), None)
            for pair, (d_q, d_k, d_v) in enumerate(results):
                d_pair[pair, here, :128] += d_q
                d_pair[pair, past, 128:256] += d_k
                d_pair[pair, past, 256:] += d_v
    for pair in range(4):
        cos, sin = cosine[pl.ds(0, SHORT), :], -sine[pl.ds(0, SHORT), :]
        rows = pl.ds(0, SHORT)
        d_three[pair, :, :128] = turn(d_pair[pair, rows, :128], cos, sin).astype(LOW)
        d_three[pair, :, 128:256] = turn(d_pair[pair, rows, 128:256], cos, sin).astype(LOW)
        d_three[pair, :, 256:] = d_pair[pair, rows, 256:].astype(LOW)
    total[...] = sum(dot_nt(d_three[pair], fqkv[pair]) for pair in range(4))
    stack[:, :384] = dot_tn(b1[...], d_three[z]).astype(LOW)

    for step in range(3):
        here = pl.ds(176 * step, 176)
        grad = total[here, :]
        back, unit_grad = norm_back(c0[here, :], c_gain[...], grad)
        sums[0] = sums[0] + jnp.sum(unit_grad, axis=0, keepdims=True)
        sums[1] = sums[1] + jnp.sum(grad, axis=0, keepdims=True)
        b1[here, :] = (c1[here, :] + back).astype(LOW)
    stack[:, 1536:] = jnp.zeros((WIDTH, WIDTH), LOW)
    stack[:16, 1536:] = jnp.concatenate(sums + [jnp.zeros((12, WIDTH), WIDE)], axis=0).astype(LOW)

    save(15, stack)
    down = b1[pl.ds(pl.multiple_of(z * 128, 128), PART), :]
    for part in range(4):
        lane = slice(128 * part, 128 * part + 128)
        thin[part, pl.ds(0, 8), :] = jnp.zeros((8, 128), WIDE)
        thin[part, pl.ds(392, 48), :] = jnp.zeros((48, 128), WIDE)
        thin[part, pl.ds(8, OWN), :] = m[:, lane].astype(WIDE)
    for r in range(3):
        put_early(r, dot_tn(every_third(6 + r, PART), down))
    for r in range(3):
        back = dot_nt(down, wp[512 * r : 512 * r + 512, :])
        for part in range(4):
            thin[part, pl.ds(6 + r, PART, 3), :] = back[:, 128 * part : 128 * part + 128]
    for part in range(4):
        lane = slice(128 * part, 128 * part + 128)
        ds[:, lane] = valid * (cot[:, lane].astype(WIDE) + thin[part, pl.ds(8, OWN), :])
    save(13, ds)
    save(14, early)
    copies.finish()
    for step in range(1, 4):
        block_move(lax.rem(z + step, 4), z).wait_send()
    for move in saved.values():
        move.wait()


def front(lengths, x, cot, gains, weights, tables, shards):
    def shape(*dims, kind=LOW):
        return (dims, kind)

    outs = [
        shape(ROWS, WIDTH),
        shape(ROWS, 128),
        shape(ROWS, 128),
        shape(ROWS, 128),
        shape(ROWS, 128),
        shape(8, ROWS, kind=WIDE),
        shape(OWN, WIDTH),
        shape(OWN, WIDTH, kind=WIDE),
        shape(OWN, WIDTH),
        shape(OWN, HIDDEN),
        shape(OWN, HIDDEN),
        shape(WIDTH, OWN),
        shape(OWN, WIDTH),
        shape(OWN, WIDTH, kind=WIDE),
        shape(HIDDEN, 768),
        shape(WIDTH, HIDDEN),
    ]
    scratch = [
        shape(WIDTH, WIDTH),
        shape(WIDTH, HIDDEN),
        shape(HIDDEN, WIDTH),
        shape(ROWS, WIDTH),
        shape(WIDTH, ROWS),
        shape(ROWS, 128, kind=WIDE),
        shape(ROWS, 128, kind=WIDE),
        shape(3, OWN, WIDTH),
        shape(4, 440, 128, kind=WIDE),
        shape(OWN, WIDTH, kind=WIDE),
        shape(OWN, WIDTH),
        shape(4, PART, WIDTH),
        shape(4, 128, WIDTH),
        shape(4, WIDTH, OWN),
        shape(4, 128, WIDTH),
        shape(4, WIDTH, WIDTH),
        shape(4, WIDTH, WIDTH),
        shape(SHORT, WIDTH, kind=WIDE),
        shape(SHORT, WIDTH, kind=WIDE),
        shape(SHORT, WIDTH),
        shape(SHORT, WIDTH),
        shape(SHORT, WIDTH),
        shape(640, WIDTH),
        shape(640, WIDTH),
        shape(640, WIDTH),
        shape(SHORT, WIDTH),
        shape(4, 8, 640, kind=WIDE),
        shape(SHORT, WIDTH),
        shape(SHORT, 256),
        shape(SHORT, 256),
        shape(SHORT, WIDTH, kind=WIDE),
        shape(128, WIDTH, kind=WIDE),
        shape(4, 640, OWN, kind=WIDE),
        shape(4, SHORT, OWN),
        shape(SHORT, WIDTH),
        shape(SHORT, WIDTH),
    ]
    vmem = pl.BlockSpec(memory_space=VMEM)
    hbm = pl.BlockSpec(memory_space=pl.ANY)
    copy_count = 160
    return pl.pallas_call(
        front_kernel,
        out_shape=[jax.ShapeDtypeStruct(*out) for out in outs],
        in_specs=[pl.BlockSpec(memory_space=pltpu.SMEM)] + [vmem] * 10 + [hbm] * 16,
        out_specs=[hbm] * len(outs),
        scratch_shapes=[VMEM(*out) for out in outs + scratch]
        + [pltpu.SemaphoreType.DMA((copy_count,)), pltpu.SemaphoreType.DMA((copy_count,))],
        compiler_params=pltpu.CompilerParams(
            collective_id=1, has_side_effects=True, vmem_limit_bytes=60 * 2**20
        ),
    )(lengths, x, cot, *gains, *weights, *tables, *shards)


class Stream:
    def __init__(self, stack, low, high, axes, spread=False):
        self.stack, self.lanes = stack, pl.ds(low, high - low)
        self.axes = axes
        self.levels = (*axes, "z") if spread else axes
        self.spread = spread

    def landing_shapes(self, row_counts):
        rows = row_counts[self.stack] // 2
        shapes = []
        for axis in self.axes[1:]:
            rows = rows // SIZES[axis]
            shapes.append((3, rows, self.lanes.size))
        return shapes


STREAMS = (
    Stream(0, 0, 384, ("core", "z", "x", "y")),
    Stream(0, 384, 768, ("core", "y", "z", "x")),
    Stream(1, 0, 2048, ("core", "x", "y")),
    Stream(2, 0, 512, ("core", "x", "y", "z")),
    Stream(2, 512, 1024, ("core", "y", "z", "x")),
    Stream(2, 1024, 1152, ("core", "z", "x", "y")),
    Stream(3, 0, 512, ("core", "x", "y"), True),
)
STACK_SHAPES = ((HIDDEN, 768), (WIDTH, HIDDEN), (HIDDEN, 1152), (WIDTH, WIDTH))
STACK_ROWS = tuple(shape[0] for shape in STACK_SHAPES)


class Summing:
    def __init__(self, stream, source, total, out, landings, copies, coords):
        self.stream, self.source, self.total, self.out = stream, source, total, out
        self.landings, self.copies, self.coords = landings, copies, coords
        self.pending = []
        self.tick_count = 0

    def rows_at(self, level, who, whole):
        rows = STACK_ROWS[self.stream.stack]
        start = 0
        for axis in self.stream.axes[:level]:
            rows = rows // SIZES[axis]
            if whole or axis != "core":
                start = start + who[axis] * rows
        return pl.ds(pl.multiple_of(start, 16), rows)

    def start_down(self, level):
        axis = self.stream.axes[level]
        lanes = self.stream.lanes
        self.pending = []
        for step in range(1, SIZES[axis]):
            other = moved(self.coords, axis, step)
            where = self.rows_at(level + 1, other, level == 0)
            if level == 0:
                source = self.source.at[where, lanes]
                target = self.total.at[pl.ds(0, where.size), lanes]
            else:
                source = self.total.at[where, lanes]
                target = self.landings[level - 1].at[step - 1]
            self.pending.append(self.copies.remote(source, target, other))

    def add_down(self, level):
        lanes = self.stream.lanes
        for move in self.pending:
            move.wait_recv()
        here = self.rows_at(level + 1, self.coords, False)
        mine = self.rows_at(1, self.coords, True)
        step_rows = min(here.size, 32)

        def add(index, carry):
            at = pl.multiple_of(index * step_rows, 16)
            part = pl.ds(pl.multiple_of(here.start + at, 16), step_rows)
            value = self.total[part, lanes].astype(WIDE)
            if level == 0:
                own = pl.ds(pl.multiple_of(mine.start + at, 16), step_rows)
                value = value + self.source[own, lanes].astype(WIDE)
            else:
                for slot in range(3):
                    landed = self.landings[level - 1][slot, pl.ds(at, step_rows), :]
                    value = value + landed.astype(WIDE)
            self.total[part, lanes] = value.astype(LOW)
            return carry

        lax.fori_loop(0, here.size // step_rows, add, 0)

    def start_up(self, level):
        axes = self.stream.axes
        where = self.rows_at(min(level + 1, len(axes)), self.coords, True)
        if level == len(axes):
            part = self.out.at[self.coords["z"], where, self.stream.lanes]
        elif self.stream.spread:
            part = self.out.at[pl.ds(0, 4), where, self.stream.lanes]
        else:
            part = self.out.at[where, self.stream.lanes]
        axis = self.stream.levels[level]
        self.pending = [
            self.copies.remote(part, part, moved(self.coords, axis, step))
            for step in range(1, SIZES[axis])
        ]

    def tick(self):
        now = self.tick_count
        self.tick_count += 1
        down, depth = len(self.stream.axes), len(self.stream.levels)
        if now < down:
            if now:
                self.add_down(now - 1)
            self.start_down(now)
        elif now == down:
            self.add_down(down - 1)
            last = self.rows_at(down, self.coords, True)
            value = self.total[self.rows_at(down, self.coords, False), self.stream.lanes]
            if self.stream.spread:
                self.out[self.coords["z"], last, self.stream.lanes] = value
            else:
                self.out[last, self.stream.lanes] = value
            self.start_up(depth - 1)
        elif now <= down + depth:
            for move in self.pending:
                move.wait_recv()
            if now < down + depth:
                self.start_up(depth - 1 - (now - down))

    def done(self):
        return self.tick_count > len(self.stream.axes) + len(self.stream.levels)


def back_kernel(*refs):
    inputs = refs[:22]
    (x_hbm, ds_hbm, h_hbm, a2_hbm, act_hbm, slope_hbm, o_own_hbm, wqkv_hbm, wq_hbm, wk_hbm, wv_hbm,
     wo_hbm, we_hbm, wc_hbm, a1_hbm, q_hbm, k_hbm, v_hbm, o_hbm, level_hbm, early_hbm, coarse_hbm) = inputs
    (cos_hbm, sin_hbm, a_row, a_gain, a_shift, f_gain) = refs[22:28]
    x_out, *total_outs = refs[28:33]
    (x, ds, h, a2, act, slope, o_own, wqkv, wo, we, wc, a1, q, k, v, o, level, early, coarse, cosine,
     sine, wall, low, d_pre, dh, d_own, d_heads, d_acc, turned, d_rows, d_weight, middle, late) = refs[33:66]
    totals, outs = refs[66:70], refs[70:74]
    *landings, send_sem, recv_sem = refs[74:]
    coords = my_coords()
    z = coords["z"]
    others = [moved(coords, "z", step) for step in (1, 3, 2)]
    copies = Copies(send_sem, recv_sem)
    lane = pl.ds(pl.multiple_of(z * 128, 128), 128)
    own = pl.ds(pl.multiple_of(z * OWN, OWN), OWN)
    loads = {}

    def load(name, source, target):
        loads.setdefault(name, []).append(copies.local(source, target))

    def loaded(*names):
        for name in names:
            for move in loads.pop(name):
                move.wait()

    load("first", ds_hbm, ds)
    load("first", wc_hbm, wc)
    load("first", slope_hbm, slope)
    load("first", act_hbm, act)
    load("first", a2_hbm, a2)
    load("early", early_hbm, early)
    load("early", coarse_hbm, coarse)
    load("second", we_hbm, we)
    load("second", h_hbm, h)
    load("second", wo_hbm, wo)
    load("second", o_own_hbm, o_own)
    for source, target in ((q_hbm, q), (k_hbm, k), (v_hbm, v), (o_hbm, o), (level_hbm, level)):
        load("third", source, target)
    for source, target in ((cos_hbm, cosine), (sin_hbm, sine), (a1_hbm, a1)):
        load("fourth", source, target)
    load("fifth", wqkv_hbm, wqkv)
    load("fifth", x_hbm, x)
    for group in range(4):
        for place, weight in enumerate((wq_hbm, wk_hbm, wv_hbm)):
            load(
                "fifth",
                weight.at[:, pl.ds(128 * group, 128)],
                wall.at[:, pl.ds(OWN * group + 128 * place, 128)],
            )
    meet(coords, ("core", "x", "y", "z"))

    sources = (early, coarse, middle, late)
    streams = []
    for stream in STREAMS:
        count = len(stream.axes) - 1
        streams.append(
            Summing(
                stream,
                sources[stream.stack],
                totals[stream.stack],
                outs[stream.stack],
                landings[:count],
                copies,
                coords,
            )
        )
        landings = landings[count:]

    def tick(*numbers):
        for number in numbers:
            if not streams[number].done():
                streams[number].tick()

    loaded("early")
    tick(0, 1, 2)
    loaded("first")
    low[...] = ds[...].astype(LOW)

    def widen_back(step, carry):
        here = pl.ds(pl.multiple_of(step * 256, 256), 256)
        back = (slope[:, here].astype(WIDE) * dot_nt(low[...], wc[here, :])).astype(LOW)
        d_pre[:, here] = back
        middle[here, :512] = dot_tn(act[:, here], low[...]).astype(LOW)
        down = pl.ds(pl.multiple_of(lax.div(step, 2) * 512, 512), 512)
        across = pl.ds(pl.multiple_of(512 + lax.rem(step, 2) * 256, 256), 256)
        middle[down, across] = dot_tn(a2[...], back).astype(LOW)
        return carry

    lax.fori_loop(0, 4, widen_back, 0)
    tick(0, 1, 2)
    lax.fori_loop(4, 8, widen_back, 0)
    tick(3, 4)
    loaded("second")
    for part in range(2):
        here = slice(256 * part, 256 * part + 256)
        dh[:, here] = dot_nt(d_pre[...], we[here, :])
    sums = [jnp.zeros((1, WIDTH), WIDE) for _ in range(2)]
    for step in range(3):
        here = pl.ds(128 * step, 128)
        grad = dh[here, :]
        back, unit_grad = norm_back(h[here, :], f_gain[...], grad)
        sums[0] = sums[0] + jnp.sum(unit_grad, axis=0, keepdims=True)
        sums[1] = sums[1] + jnp.sum(grad, axis=0, keepdims=True)
        back = ds[here, :] + back
        dh[here, :] = back
        low[here, :] = back.astype(LOW)
    d_own[...] = dot_nt(low[...], wo[...]).astype(LOW)
    head_moves = [
        copies.remote(
            d_own.at[:, pl.ds(pl.multiple_of(other["z"] * 128, 128), 128)], d_heads.at[own, :], other
        )
        for other in others
    ]
    d_heads[own, :] = d_own[:, lane]
    output_grad = dot_tn(o_own[...], low[...]).astype(LOW)
    for part in range(4):
        middle[512 * part : 512 * part + 512, 1024:] = output_grad[:, 128 * part : 128 * part + 128]
    tick(5, 3, 4)
    late_columns = jnp.transpose(
        jnp.concatenate(sums + [jnp.zeros((126, WIDTH), WIDE)], axis=0)
    )
    d_acc[...] = jnp.zeros_like(d_acc)
    d_weight[...] = jnp.zeros_like(d_weight)
    loaded("third")
    for move in head_moves:
        move.wait_recv()
    loaded("fourth", "fifth")
    tick(0, 1, 2)

    sent_blocks = send_sem.shape[0] - 4
    got_blocks = recv_sem.shape[0] - 4

    def rows_move(target, source):
        return pltpu.make_async_remote_copy(
            src_ref=turned.at[pl.ds(pl.multiple_of(target * OWN, OWN), OWN), :],
            dst_ref=d_rows.at[:, pl.ds(pl.multiple_of(source * OWN, 128), OWN)],
            send_sem=send_sem.at[sent_blocks + target],
            recv_sem=recv_sem.at[got_blocks + source],
            device_id=device_of({**coords, "z": target}),
            device_id_type=MESH,
        )

    hooks = iter(
        (
            (5, 3, 4),
            (0, 1, 2),
            (3, 4, 5),
            (0, 1, 2),
            (3, 4, 5),
            (0, 1, 2),
            (3, 4, 5),
            (0, 1, 2),
            (3, 4, 5),
            (0, 1, 2),
        )
    )
    column_sums = jnp.zeros((1, OWN), WIDE)
    for block in reversed(range(4)):
        here = pl.ds(OWN * block, OWN)
        deltas = pair_sums(d_heads[here, :].astype(WIDE) * o[here, :].astype(WIDE))
        for past in reversed(range(block + 1)):
            there = pl.ds(OWN * past, OWN)
            ((d_q, d_k, d_v),) = attend_back_blocks(
                [(q[here, :], d_heads[here, :], k[there, :], v[there, :], level[:, here], deltas)],
                0 if past == block else None,
            )
            d_acc[here, :128] += d_q
            d_acc[there, 128:256] += d_k
            d_acc[there, 256:] += d_v
            tick(*next(hooks))
        cos, sin = cosine[here, :], -sine[here, :]
        turned[here, :128] = turn(d_acc[here, :128], cos, sin).astype(LOW)
        turned[here, 128:256] = turn(d_acc[here, 128:256], cos, sin).astype(LOW)
        turned[here, 256:] = d_acc[here, 256:].astype(LOW)

        @pl.when(z != block)
        def send():
            rows_move(block, z).start()

        d_weight[...] += dot_tn(a1[here, :], turned[here, :])
        column_sums = column_sums + jnp.sum(turned[here, :].astype(WIDE), axis=0, keepdims=True)

    weight = wqkv[...].astype(WIDE)
    late[:, :OWN] = d_weight[...].astype(LOW)
    shift_grad = jnp.sum(weight * column_sums, axis=1, keepdims=True)
    whole = jnp.sum(weight * d_weight[...], axis=1, keepdims=True)
    gain_grad = (whole - a_shift[...] * shift_grad) * (1.0 / a_gain[...])
    lanes = lanes_iota((WIDTH, 128))
    columns = jnp.where(
        lanes == 2, gain_grad, jnp.where(lanes == 3, shift_grad, late_columns)
    )
    late[:, OWN:] = columns.astype(LOW)
    tick(6)
    tick(3, 4, 5)
    tick(6)
    d_rows[:, pl.ds(pl.multiple_of(z * OWN, 128), OWN)] = turned[own, :]
    for step in range(1, 4):
        rows_move(z, lax.rem(z + step, 4)).wait_recv()
    x_grad = dot_nt(d_rows[...], wall[...])
    ds[...] = x_grad
    for step in range(3):
        here = pl.ds(128 * step, 128)
        back, _ = norm_back(x[here, :].astype(WIDE), a_row[...], ds[here, :])
        dh[here, :] = dh[here, :] + back
    writes = [copies.local(dh, x_out)]
    tick(6)
    while not all(stream.done() for stream in streams):
        tick(*range(7))
    for out, target in zip(outs, total_outs):
        writes.append(copies.local(out, target))
    copies.finish()
    for step in range(1, 4):
        rows_move(lax.rem(z + step, 4), z).wait_send()
    for move in writes:
        move.wait()


def back(operands, tables, gains):
    def shape(*dims, kind=LOW):
        return (dims, kind)

    outs = [shape(OWN, WIDTH, kind=WIDE)] + [shape(*dims) for dims in STACK_SHAPES[:3]]
    outs.append(shape(4, WIDTH, WIDTH))
    scratch = [
        shape(OWN, WIDTH),
        shape(OWN, WIDTH, kind=WIDE),
        shape(OWN, WIDTH, kind=WIDE),
        shape(OWN, WIDTH),
        shape(OWN, HIDDEN),
        shape(OWN, HIDDEN),
        shape(OWN, WIDTH),
        shape(WIDTH, OWN),
        shape(WIDTH, WIDTH),
        shape(WIDTH, HIDDEN),
        shape(HIDDEN, WIDTH),
        shape(ROWS, WIDTH),
        shape(ROWS, 128),
        shape(ROWS, 128),
        shape(ROWS, 128),
        shape(ROWS, 128),
        shape(8, ROWS, kind=WIDE),
        shape(*STACK_SHAPES[0]),
        shape(*STACK_SHAPES[1]),
        shape(ROWS, 128, kind=WIDE),
        shape(ROWS, 128, kind=WIDE),
        shape(WIDTH, ROWS),
        shape(OWN, WIDTH),
        shape(OWN, HIDDEN),
        shape(OWN, WIDTH, kind=WIDE),
        shape(OWN, WIDTH),
        shape(ROWS, 128),
        shape(ROWS, OWN, kind=WIDE),
        shape(ROWS, OWN),
        shape(OWN, ROWS),
        shape(WIDTH, OWN, kind=WIDE),
        shape(*STACK_SHAPES[2]),
        shape(*STACK_SHAPES[3]),
    ]
    scratch += [shape(rows // 2, lanes) for rows, lanes in STACK_SHAPES]
    scratch += outs[1:]
    for stream in STREAMS:
        scratch += [shape(*dims) for dims in stream.landing_shapes(STACK_ROWS)]
    vmem = pl.BlockSpec(memory_space=VMEM)
    hbm = pl.BlockSpec(memory_space=pl.ANY)
    copy_count = 200
    return pl.pallas_call(
        back_kernel,
        out_shape=[jax.ShapeDtypeStruct(*out) for out in outs],
        in_specs=[hbm] * (len(operands) + 2) + [vmem] * 4,
        out_specs=[hbm] * len(outs),
        scratch_shapes=[VMEM(*part) for part in scratch]
        + [pltpu.SemaphoreType.DMA((copy_count,)), pltpu.SemaphoreType.DMA((copy_count,))],
        compiler_params=pltpu.CompilerParams(
            collective_id=2, has_side_effects=True, vmem_limit_bytes=63 * 2**20
        ),
    )(*operands, *tables, *gains)


def halves(early, number):
    parts = [divmod(2 * number + part, 3) for part in range(2)]
    return jnp.concatenate(
        [early[512 * down : 512 * down + 512, 256 * across : 256 * across + 256] for down, across in parts],
        axis=1,
    )


def body(
    inputs,
    lengths,
    cotangent,
    attention_gain,
    attention_shift,
    query_weight,
    key_weight,
    value_weight,
    output_weight,
    feedforward_gain,
    feedforward_shift,
    expand_weight,
    contract_weight,
    pooling_weight,
    coarse_gain,
    coarse_shift,
    coarse_query,
    coarse_key,
    coarse_value,
    coarse_output,
    widen_gain,
    widen_shift,
    coarse_expand,
    coarse_contract,
    upsample_weight,
):
    def row(vector):
        return vector.reshape(1, -1)

    tables = turn_tables()
    square = (query_weight, key_weight, value_weight)
    (a1, q, k, v, o, level, o_own, h, a2, act, slope, wqkv, mixed, ds, early, coarse_stack) = front(
        lengths,
        inputs,
        cotangent,
        [
            row(vector)
            for vector in (
                attention_gain,
                attention_shift,
                feedforward_gain,
                feedforward_shift,
                coarse_gain,
                coarse_shift,
                widen_gain,
                widen_shift,
            )
        ],
        (*square, output_weight, expand_weight, contract_weight, pooling_weight, upsample_weight),
        tables,
        (coarse_query, coarse_key, coarse_value, coarse_output, coarse_expand, coarse_contract),
    )
    input_grad, early, coarse_total, middle, late = back(
        (
            inputs,
            ds,
            h,
            a2,
            act,
            slope,
            o_own,
            wqkv,
            *square,
            output_weight,
            expand_weight,
            contract_weight,
            a1,
            q,
            k,
            v,
            o,
            level,
            early,
            coarse_stack,
        ),
        tables,
        (
            row(attention_gain),
            attention_gain.reshape(-1, 1),
            attention_shift.reshape(-1, 1),
            row(feedforward_gain),
        ),
    )
    early, coarse_total, middle, late = (
        total.astype(WIDE) for total in (early, coarse_total, middle, late)
    )
    squares = [
        jnp.concatenate([late[i, :, 128 * j : 128 * j + 128] for i in range(4)], axis=1)
        for j in range(3)
    ]
    vectors = jnp.sum(late[:, :, 384:388], axis=0)
    return (
        mixed,
        input_grad,
        vectors[:, 2],
        vectors[:, 3],
        *squares,
        jnp.concatenate([middle[512 * i : 512 * i + 512, 1024:] for i in range(4)], axis=1),
        vectors[:, 0],
        vectors[:, 1],
        jnp.concatenate([middle[512 * i : 512 * i + 512, 512:1024] for i in range(4)], axis=1),
        middle[:, :512],
        jnp.concatenate([halves(early, i) for i in range(3)], axis=0),
        coarse_total[0, 1536:],
        coarse_total[1, 1536:],
        coarse_total[:, :128],
        coarse_total[:, 128:256],
        coarse_total[:, 256:384],
        jnp.concatenate([coarse_total[128 * i : 128 * i + 128, 384:512] for i in range(4)], axis=1),
        coarse_total[2, 1536:],
        coarse_total[3, 1536:],
        coarse_total[:, 512:1024],
        coarse_total[:, 1024:1536],
        jnp.concatenate([halves(early, 3 + i) for i in range(3)], axis=1),
    )


def solution(mesh):
    in_specs = (
        P(("seq", "head"), None),
        P("seq"),
        P(("seq", "head"), None),
        P(),
        P(),
        P(),
        P(),
        P(),
        P(),
        P(),
        P(),
        P(),
        P(),
        P(),
        P(),
        P(),
        P(None, "head"),
        P(None, "head"),
        P(None, "head"),
        P("head", None),
        P(),
        P(),
        P(None, "head"),
        P("head", None),
        P(),
    )
    out_specs = (
        P(("seq", "head"), None),
        P(("seq", "head"), None),
        P(),
        P(),
        P(),
        P(),
        P(),
        P(),
        P(),
        P(),
        P(),
        P(),
        P(),
        P(),
        P(),
        P(None, "head"),
        P(None, "head"),
        P(None, "head"),
        P("head", None),
        P(),
        P(),
        P(None, "head"),
        P("head", None),
        P(),
    )
    return jax.shard_map(body, mesh=mesh, in_specs=in_specs, out_specs=out_specs, check_vma=False)
```

```python
import functools
import math

import jax
import jax.numpy as jnp
import numpy as np
from jax import lax
from jax.experimental import pallas as pl
from jax.experimental.pallas import tpu as pltpu
from jax.sharding import PartitionSpec as P

MESH = pl.DeviceIdType.MESH
VMEM = pltpu.VMEM
LOW = jnp.bfloat16
WIDE = jnp.float32
EPSILON = 1e-05
OWN = 384
ROWS = 1536
WIDTH = 512
HIDDEN = 2048
SHORT = 528
PART = 144
SIZES = {"core": 2, "x": 4, "y": 4, "z": 4}


def my_coords():
    seq = lax.axis_index("seq")
    return {
        "core": lax.rem(seq, 2),
        "y": lax.rem(lax.div(seq, 2), 4),
        "x": lax.div(seq, 8),
        "z": lax.axis_index("head"),
    }


def moved(coords, axis, step):
    other = dict(coords)
    other[axis] = lax.rem(coords[axis] + step, SIZES[axis])
    return other


def device_of(coords):
    return {
        "seq": (coords["x"] * 4 + coords["y"]) * 2 + coords["core"],
        "head": coords["z"],
    }


def meet(coords, axes):
    barrier = pltpu.get_barrier_semaphore()
    count = 0
    for axis in axes:
        for step in range(1, SIZES[axis]):
            pl.semaphore_signal(
                barrier,
                inc=1,
                device_id=device_of(moved(coords, axis, step)),
                device_id_type=MESH,
            )
            count += 1
    pl.semaphore_wait(barrier, count)


def dot(left, right):
    return lax.dot_general(left, right, (((1,), (0,)), ((), ())), preferred_element_type=WIDE)


def dot_nt(left, right):
    return lax.dot_general(left, right, (((1,), (1,)), ((), ())), preferred_element_type=WIDE)


def dot_tn(left, right):
    return lax.dot_general(left, right, (((0,), (0,)), ((), ())), preferred_element_type=WIDE)


def lanes_iota(shape):
    return lax.broadcasted_iota(jnp.int32, shape, len(shape) - 1)


def rows_iota(shape):
    return lax.broadcasted_iota(jnp.int32, shape, 0)


def standard(values):
    centred = values - jnp.mean(values, axis=-1, keepdims=True)
    scale = lax.rsqrt(jnp.mean(centred * centred, axis=-1, keepdims=True) + EPSILON)
    return centred * scale, scale


def norm(values, gain, shift):
    return standard(values)[0] * gain + shift


def norm_back(values, gain, grad):
    unit, scale = standard(values)
    inner = grad * gain
    first = jnp.mean(inner, axis=-1, keepdims=True)
    second = jnp.mean(inner * unit, axis=-1, keepdims=True)
    return scale * (inner - first - unit * second), grad * unit


def turn(values, cosine, sine):
    lane = lanes_iota(values.shape)
    other = jnp.where(
        lax.rem(lane, 64) < 32, pltpu.roll(values, 96, 1), pltpu.roll(values, 32, 1)
    )
    return values * cosine + other * sine


def gelu_parts(values):
    half = 0.5 + 0.5 * lax.erf(values * math.sqrt(0.5))
    bell = jnp.exp(values * values * -0.5) * (1.0 / math.sqrt(2.0 * math.pi))
    return values * half, half + values * bell


def head_lanes(head, values):
    return jnp.where(lanes_iota(values.shape) // 64 == head, values, jnp.zeros_like(values))


def by_head(first, second):
    return jnp.where(lanes_iota(first.shape) < 64, first, second)


def head_rows(columns):
    shape = (8, 128)
    pick = (lanes_iota(shape) == rows_iota(shape) * 64).astype(WIDE)
    return lax.dot_general(
        pick,
        columns,
        (((1,), (1,)), ((), ())),
        precision=lax.Precision.HIGHEST,
        preferred_element_type=WIDE,
    )


def frequency_row():
    frequency = np.exp(np.arange(32, dtype=np.float32) * np.float32(-math.log(10000.0) / 32))
    return np.tile(frequency.astype(np.float32), 4)[None, :]


def fill_tables(frequency, cosine, sine):
    coarse = rows_iota((24, 128)).astype(WIDE) * 64.0 * frequency
    fine = rows_iota((64, 128)).astype(WIDE) * frequency
    sign = jnp.where(lax.rem(lanes_iota((64, 128)), 64) < 32, -1.0, 1.0)
    coarse_cos, coarse_sin = jnp.cos(coarse), jnp.sin(coarse)
    fine_cos, fine_sin = jnp.cos(fine), jnp.sin(fine)
    for place in range(24):
        one_cos, one_sin = coarse_cos[place : place + 1], coarse_sin[place : place + 1]
        here = pl.ds(64 * place, 64)
        cosine[here, :] = one_cos * fine_cos - one_sin * fine_sin
        sine[here, :] = (one_sin * fine_cos + one_cos * fine_sin) * sign


def as_columns(vectors):
    filler = jnp.zeros((128 - len(vectors), WIDTH), WIDE)
    return jnp.transpose(jnp.concatenate(vectors + [filler], axis=0))


class Copies:
    def __init__(self, send_sem, recv_sem):
        self.send_sem, self.recv_sem, self.count, self.sent = send_sem, recv_sem, 0, []

    def remote(self, source, target, other):
        place = self.count
        self.count += 1
        move = pltpu.make_async_remote_copy(
            src_ref=source,
            dst_ref=target,
            send_sem=self.send_sem.at[place],
            recv_sem=self.recv_sem.at[place],
            device_id=device_of(other),
            device_id_type=MESH,
        )
        move.start()
        self.sent.append(move)
        return move

    def local(self, source, target):
        place = self.count
        self.count += 1
        move = pltpu.make_async_copy(source, target, self.recv_sem.at[place])
        move.start()
        return move

    def finish(self):
        for move in self.sent:
            move.wait_send()


def pair_sums(columns):
    shape = (8, 128)
    pick = (lanes_iota(shape) // 64 == rows_iota(shape)).astype(WIDE)
    return lax.dot_general(
        pick,
        columns,
        (((1,), (1,)), ((), ())),
        precision=lax.Precision.HIGHEST,
        preferred_element_type=WIDE,
    )


def attend_tiles(items, before, width, offset):
    last, first = pl.ds(before, width), pl.ds(0, before)
    chains = [(item, head) for item in items for head in range(2)]
    queries = [head_lanes(head, item[0]) for item, head in chains]
    near = [dot_nt(query, item[1][last, item[3]]) for query, (item, _) in zip(queries, chains)]
    keep = [
        lanes_iota(near[0].shape) <= rows_iota(near[0].shape) + shift
        for shift in (offset if isinstance(offset, tuple) else (offset,) * len(items))
    ]
    near = [jnp.where(keep[place // 2], scores, -1e30) for place, scores in enumerate(near)]
    tops = [jnp.max(scores, axis=-1, keepdims=True) for scores in near]
    if before:
        far = [dot_nt(query, item[1][first, item[3]]) for query, (item, _) in zip(queries, chains)]
        tops = [jnp.maximum(t, jnp.max(s, axis=-1, keepdims=True)) for t, s in zip(tops, far)]
        far = [jnp.exp(scores - t) for scores, t in zip(far, tops)]
    near = [jnp.exp(scores - t) for scores, t in zip(near, tops)]
    totals = [jnp.sum(probs, axis=-1, keepdims=True) for probs in near]
    mixed = [dot(probs.astype(LOW), item[2][last, item[3]]) for probs, (item, _) in zip(near, chains)]
    if before:
        totals = [t + jnp.sum(probs, axis=-1, keepdims=True) for t, probs in zip(totals, far)]
        mixed = [
            m + dot(probs.astype(LOW), item[2][first, item[3]])
            for m, probs, (item, _) in zip(mixed, far, chains)
        ]
    outs = [m * (1.0 / t) for m, t in zip(mixed, totals)]
    levels = [t + jnp.log(total) for t, total in zip(tops, totals)]
    shape = (items[0][0].shape[0], 128)
    results = []
    for place in range(len(items)):
        a, b = 2 * place, 2 * place + 1
        level = by_head(jnp.broadcast_to(levels[a], shape), jnp.broadcast_to(levels[b], shape))
        results.append((by_head(outs[a], outs[b]), head_rows(level)))
    return results


def attend_back_blocks(items, offset):
    chains = [(item, head) for item in items for head in range(2)]
    queries = [head_lanes(head, item[0]) for item, head in chains]
    d_outs = [head_lanes(head, item[1]) for item, head in chains]
    scores = [dot_nt(item[2], query) for query, (item, _) in zip(queries, chains)]
    d_probs = [dot_nt(item[3], d_out) for d_out, (item, _) in zip(d_outs, chains)]
    probs = [
        jnp.exp(score - item[4][head : head + 1]) for score, (item, head) in zip(scores, chains)
    ]
    if offset is not None:
        keep = rows_iota(probs[0].shape) <= lanes_iota(probs[0].shape) + offset
        probs = [jnp.where(keep, prob, 0.0) for prob in probs]
    d_scores = [
        (prob * (d_prob - item[5][head : head + 1])).astype(LOW)
        for prob, d_prob, (item, head) in zip(probs, d_probs, chains)
    ]
    d_values = [dot(prob.astype(LOW), d_out) for prob, d_out in zip(probs, d_outs)]
    d_keys = [dot(d_score, query) for d_score, query in zip(d_scores, queries)]
    d_queries = [dot_tn(d_score, item[2]) for d_score, (item, _) in zip(d_scores, chains)]
    return [
        (
            by_head(d_queries[i], d_queries[i + 1]) * 0.125,
            d_keys[i] + d_keys[i + 1],
            d_values[i] + d_values[i + 1],
        )
        for i in range(0, len(chains), 2)
    ]


COARSE_STACK = (WIDTH, 1664)


def front_kernel(*refs):
    (lengths, x, cot, a_gain, a_shift, f_gain, f_shift, c_gain, c_shift, w_gain, w_shift) = refs[:11]
    (frequency, wq_hbm, wk_hbm, wv_hbm, wo_hbm, we_hbm, wc_hbm, wp_hbm, wu_hbm) = refs[11:20]
    shards = refs[20:26]
    out_refs = refs[26:42]
    (a1, q, k, v, o, level, o_own, h, a2, act, slope, wqkv, mixed, ds, early, stack) = refs[42:58]
    (wo, we, wc, wp, wu, cosine, sine, landing, thin, s, m, c0g, dcg, fqkv, fo, fe, fc) = refs[58:75]
    (c0, c1, b1, b2, dr, cq, ck, cv, co, clevel, d_out, c_act, d_pre, total, top, d_pair, d_three,
     kept_act, kept_pre, send_sem, recv_sem) = refs[75:]
    saved = {}

    def save(place, source):
        saved[place] = copies.local(source, out_refs[place])

    coords = my_coords()
    z = coords["z"]
    core = coords["core"]
    right, left, far = (moved(coords, "z", step) for step in (1, 3, 2))
    copies = Copies(send_sem, recv_sem)
    lane = pl.ds(pl.multiple_of(z * 128, 128), 128)
    first_loads = [
        copies.local(weight.at[:, lane], wqkv.at[:, pl.ds(128 * place, 128)])
        for place, weight in enumerate((wq_hbm, wk_hbm, wv_hbm))
    ]
    loads = [
        copies.local(source, target)
        for source, target in ((wu_hbm, wu), (wo_hbm, wo), (we_hbm, we), (wc_hbm, wc), (wp_hbm, wp))
    ]
    own_weights = [
        copies.local(shard, full)
        for shard, full in zip(
            shards,
            [fqkv.at[z, :, pl.ds(128 * place, 128)] for place in range(3)]
            + [fo.at[z], fe.at[z], fc.at[z]],
        )
    ]
    meet(coords, ("core", "x", "y", "z"))
    low, high = pl.ds(0, OWN // 2), pl.ds(OWN // 2, OWN // 2)
    to_right = copies.remote(x.at[low], landing.at[0, low], right)
    to_left = copies.remote(x.at[high], landing.at[1, high], left)
    to_right_more = copies.remote(x.at[high], landing.at[0, high], right)
    to_left_more = copies.remote(x.at[low], landing.at[1, low], left)

    def project(block, index):
        start = pl.multiple_of(index * OWN, OWN)

        def rows_of(step, carry):
            here = pl.multiple_of(step * 128, 128)
            there = pl.ds(pl.multiple_of(start + here, 128), 128)
            values = block[pl.ds(here, 128), :].astype(WIDE)
            a1[there, :] = norm(values, a_gain[...], a_shift[...]).astype(LOW)
            return carry

        lax.fori_loop(0, OWN // 128, rows_of, 0)
        here = pl.ds(start, OWN)
        both = dot(a1[here, :], wqkv[...])
        cos, sin = cosine[here, :], sine[here, :]
        q[here, :] = (turn(both[:, :128], cos, sin) * 0.125).astype(LOW)
        k[here, :] = turn(both[:, 128:256], cos, sin).astype(LOW)
        v[here, :] = both[:, 256:].astype(LOW)

    fill_tables(frequency[...], cosine, sine)
    for load in first_loads:
        load.wait()
    project(x, z)
    to_right.wait_recv()
    far_right = copies.remote(landing.at[0, low], landing.at[2, low], right)
    to_left.wait_recv()
    far_left = copies.remote(landing.at[1, high], landing.at[2, high], left)

    valid = (rows_iota((OWN, 128)) + z * OWN < lengths[0]).astype(WIDE)
    for part in range(4):
        thin[part, pl.ds(0, 8), :] = jnp.zeros((8, 128), WIDE)
        thin[part, pl.ds(392, 48), :] = jnp.zeros((48, 128), WIDE)
        thin[part, pl.ds(8, OWN), :] = cot[:, 128 * part : 128 * part + 128].astype(WIDE) * valid

    def every_third(first, count):
        pieces = [thin[part, pl.ds(first, count, 3), :].astype(LOW) for part in range(4)]
        return jnp.concatenate(pieces, axis=1)

    loads[0].wait()
    lifted_back = sum(
        dot_nt(every_third(8 + r, 128), wu[:, 512 * r : 512 * r + 512]) for r in range(3)
    )
    dcg[z] = lifted_back.astype(LOW)

    to_right_more.wait_recv()
    project(landing.at[0], left["z"])
    to_left_more.wait_recv()
    project(landing.at[1], right["z"])
    far_right.wait_recv()
    far_left.wait_recv()
    project(landing.at[2], far["z"])

    for load in own_weights:
        load.wait()
    z_others = (right, left, far)
    z_sources = (left, right, far)
    pieces = {}
    for place, full in enumerate((fqkv, fe, fc)):
        for way, axis in enumerate(("x", "y")):
            rows = pl.ds(pl.multiple_of(core * 256 + way * 128 + coords[axis] * 32, 32), 32)
            for step, other in enumerate(z_others):
                pieces[place, way, step] = copies.remote(full.at[z, rows], full.at[z, rows], other)
    fo_rows = pl.ds(pl.multiple_of(core * 64, 64), 64)
    fo_moves = [copies.remote(fo.at[z, fo_rows], fo.at[z, fo_rows], other) for other in z_others]

    sent_blocks = send_sem.shape[0] - 4
    got_blocks = recv_sem.shape[0] - 4

    def block_move(target, source):
        return pltpu.make_async_remote_copy(
            src_ref=o.at[pl.ds(pl.multiple_of(target * OWN, OWN), OWN), :],
            dst_ref=o_own.at[:, pl.ds(pl.multiple_of(source * 128, 128), 128)],
            send_sem=send_sem.at[sent_blocks + target],
            recv_sem=recv_sem.at[got_blocks + source],
            device_id=device_of({**coords, "z": target}),
            device_id_type=MESH,
        )

    everything = pl.ds(0, 128)
    for block in reversed(range(4)):
        tiles = [pl.ds(OWN * block + 128 * step, 128) for step in range(3)]
        results = attend_tiles(
            [(q[here, :], k, v, everything) for here in tiles], OWN * block, OWN, (0, 128, 256)
        )
        for here, (mixed_tile, tops) in zip(tiles, results):
            o[here, :] = mixed_tile.astype(LOW)
            level[:, here] = tops

        @pl.when(z != block)
        def send():
            block_move(block, z).start()

    for place, ref in ((0, a1), (1, q), (2, k), (3, v), (4, o), (5, level), (11, wqkv)):
        save(place, ref)
    o_own[:, lane] = o[pl.ds(pl.multiple_of(z * OWN, OWN), OWN), :]

    spread = []
    for place, full in enumerate((fqkv, fe, fc)):
        for way, axis in enumerate(("x", "y")):
            rows = pl.ds(pl.multiple_of(core * 256 + way * 128 + coords[axis] * 32, 32), 32)
            for step, source in enumerate(z_sources):
                pieces[place, way, step].wait_recv()
                part = full.at[source["z"], rows]
                for far_step in range(1, 4):
                    spread.append(copies.remote(part, part, moved(coords, axis, far_step)))
    for step in range(1, 4):
        other = lax.rem(z + step, 4)
        block_move(z, other).wait_recv()
    save(6, o_own)

    for load in loads[1:]:
        load.wait()

    def mix(step, carry):
        here = pl.ds(pl.multiple_of(step * 128, 128), 128)
        hidden = x[here, :].astype(WIDE) + dot(o_own[here, :], wo[...])
        h[here, :] = hidden
        a2[here, :] = norm(hidden, f_gain[...], f_shift[...]).astype(LOW)
        return carry

    lax.fori_loop(0, 3, mix, 0)

    def widen(step, carry):
        here = pl.ds(pl.multiple_of(step * 256, 256), 256)
        value, back = gelu_parts(dot(a2[...], we[:, here]))
        act[:, here] = value.astype(LOW)
        slope[:, here] = back.astype(LOW)
        return carry

    lax.fori_loop(0, HIDDEN // 256, widen, 0)
    for place, ref in ((7, h), (8, a2), (9, act), (10, slope)):
        save(place, ref)

    for part in range(4):
        here = slice(128 * part, 128 * part + 128)
        if part % 2 == 0:
            wide = slice(256 * (part // 2), 256 * (part // 2) + 256)
            summed = h[:, wide] + dot(act[...], wc[:, wide])
            s[:, wide] = summed
        kept = (s[:, here] * valid).astype(LOW)
        m[:, here] = kept
        thin[part, pl.ds(8, OWN), :] = kept.astype(WIDE)
    pooled = sum(
        dot(every_third(6 + r, PART), wp[512 * r : 512 * r + 512, :]) for r in range(3)
    )
    c0g[z] = pooled.astype(LOW)
    c0_moves = [copies.remote(c0g.at[z], c0g.at[z], other) for other in z_others]
    dc_moves = [copies.remote(dcg.at[z], dcg.at[z], other) for other in z_others]
    sibling = moved(coords, "core", 1)
    swaps = []
    for step, source in enumerate(z_sources):
        fo_moves[step].wait_recv()
        part = fo.at[source["z"], fo_rows]
        swaps.append(copies.remote(part, part, sibling))
    for move in spread:
        move.wait_recv()
    half = pl.ds(pl.multiple_of(core * 256, 256), 256)
    for full in (fqkv, fe, fc):
        for source in z_sources:
            part = full.at[source["z"], half]
            swaps.append(copies.remote(part, part, sibling))
    for move in swaps + c0_moves + dc_moves:
        move.wait_recv()

    own_lane = pl.ds(pl.multiple_of(z * 128, 128), 128)
    own_rows = pl.ds(pl.multiple_of(z * 128, 128), 128)

    def row_chunks(body):
        def run(step, carry):
            body(pl.ds(pl.multiple_of(step * 176, 16), 176))
            return carry

        lax.fori_loop(0, 3, run, 0)

    for part in range(4):
        base = 128 * part
        c0[pl.ds(base, 128), :] = c0g[part, pl.ds(0, 128), :].astype(WIDE)
        dr[pl.ds(base, 128), :] = dcg[part]
        if part:
            first = pl.ds(base, 1)
            c0[first, :] = c0[first, :] + c0g[part - 1, pl.ds(128, 16), :].astype(WIDE)[:1]
    c0[pl.ds(512, 16), :] = c0g[3, pl.ds(128, 16), :].astype(WIDE)
    dr[pl.ds(512, 16), :] = jnp.zeros((16, WIDTH), LOW)

    def first_norm(here):
        b1[here, :] = norm(c0[here, :], c_gain[...], c_shift[...]).astype(LOW)

    row_chunks(first_norm)
    for ref in (cq, ck, cv):
        ref[pl.ds(SHORT, 640 - SHORT), :] = jnp.zeros((640 - SHORT, WIDTH), LOW)

    for pair in range(4):
        lane = pl.ds(pair * 128, 128)
        both = dot(b1[...], fqkv[pair])
        cos, sin = cosine[pl.ds(0, SHORT), :], sine[pl.ds(0, SHORT), :]
        rows = pl.ds(0, SHORT)
        cq[rows, lane] = (turn(both[:, :128], cos, sin) * 0.125).astype(LOW)
        ck[rows, lane] = turn(both[:, 128:256], cos, sin).astype(LOW)
        cv[rows, lane] = both[:, 256:].astype(LOW)
    for tile in range(5):
        here = pl.ds(128 * tile, 128 if tile < 4 else 16)
        for pair, (mixed_tile, tops) in enumerate(
            attend_tiles([(cq[here, pl.ds(128 * p, 128)], ck, cv, pl.ds(128 * p, 128)) for p in range(4)], 128 * tile, 128, 0)
        ):
            co[here, pl.ds(128 * pair, 128)] = mixed_tile.astype(LOW)
            clevel[pair, :, here] = tops

    def second_norm(here):
        value = c0[here, :]
        for part in range(4):
            value = value + dot(co[here, 128 * part : 128 * part + 128], fo[part])
        c1[here, :] = value
        b2[here, :] = norm(value, w_gain[...], w_shift[...]).astype(LOW)

    row_chunks(second_norm)
    total[...] = jnp.zeros_like(total)
    top[...] = c1[own_rows, :]

    def widen(keep, step, carry):
        slot = lax.rem(z + step // 2, 4)
        lane = pl.ds(pl.multiple_of(lax.rem(step, 2) * 256, 256), 256)
        value, slope = gelu_parts(dot(b2[...], fe[slot, :, lane]))
        c_act[...] = value.astype(LOW)
        d_pre[...] = (slope * dot_nt(dr[...], fc[slot, lane, :])).astype(LOW)
        if keep:
            kept_act[:, lane] = c_act[...]
            kept_pre[:, lane] = d_pre[...]
        top[...] += dot(c_act[own_rows, :], fc[slot, lane, :])
        total[...] += dot_nt(d_pre[...], fe[slot, :, lane])
        return carry

    lax.fori_loop(0, 2, functools.partial(widen, True), 0)
    lax.fori_loop(2, 8, functools.partial(widen, False), 0)

    def put_early(number, grad):
        for part in range(2):
            down, across = divmod(2 * number + part, 3)
            early[512 * down : 512 * down + 512, 256 * across : 256 * across + 256] = grad[
                :, 256 * part : 256 * part + 256
            ].astype(LOW)

    crest = top[...].astype(LOW)
    for r in range(3):
        lifted = dot(crest, wu[:, 512 * r : 512 * r + 512])
        for part in range(4):
            thin[part, pl.ds(8 + r, 128, 3), :] = lifted[:, 128 * part : 128 * part + 128]
    for part in range(4):
        lane = slice(128 * part, 128 * part + 128)
        mixed[:, lane] = (valid * (s[:, lane] + thin[part, pl.ds(8, OWN), :])).astype(LOW)
        thin[part, pl.ds(8, OWN), :] = cot[:, lane].astype(WIDE) * valid

    for r in range(3):
        put_early(3 + r, dot_tn(crest, every_third(8 + r, 128)))

    save(12, mixed)
    stack[:, :512] = dot_tn(b2[...], kept_pre[...]).astype(LOW)
    stack[:, 512:1024] = dot_tn(kept_act[...], dr[...]).astype(LOW)
    sums = [jnp.zeros((1, WIDTH), WIDE) for _ in range(4)]
    for step in range(3):
        here = pl.ds(176 * step, 176)
        grad = total[here, :]
        back, unit_grad = norm_back(c1[here, :], w_gain[...], grad)
        sums[2] = sums[2] + jnp.sum(unit_grad, axis=0, keepdims=True)
        sums[3] = sums[3] + jnp.sum(grad, axis=0, keepdims=True)
        back = dr[here, :].astype(WIDE) + back
        c1[here, :] = back
        b2[here, :] = back.astype(LOW)
    output_grad = dot_tn(co[:, own_lane], b2[...]).astype(LOW)
    for part in range(4):
        stack[128 * part : 128 * part + 128, 1408:1536] = output_grad[:, 128 * part : 128 * part + 128]
    for pair in range(4):
        d_out[:, pl.ds(128 * pair, 128)] = dot_nt(b2[...], fo[pair]).astype(LOW)
    lanes = [pl.ds(128 * pair, 128) for pair in range(4)]
    deltas = [
        pair_sums(d_out[:, lane].astype(WIDE) * co[:, lane].astype(WIDE)) for lane in lanes
    ]
    for tile in range(5):
        here = pl.ds(128 * tile, 128 if tile < 4 else 16)
        near, past = pl.ds(128 * tile, 128), pl.ds(0, 128 * tile)

        def items(there):
            return [
                (
                    cq[here, lane],
                    d_out[here, lane],
                    ck[there, lane],
                    cv[there, lane],
                    clevel[pair, :, here],
                    deltas[pair][:, 128 * tile : 128 * tile + here.size],
                )
                for pair, lane in enumerate(lanes)
            ]

        results = attend_back_blocks(items(near), 0)
        for pair, (d_q, d_k, d_v) in enumerate(results):
            d_pair[pair, here, :128] = d_q
            d_pair[pair, near, 128:256] = d_k
            d_pair[pair, near, 256:] = d_v
        if tile:
            results = attend_back_blocks(items(past), None)
            for pair, (d_q, d_k, d_v) in enumerate(results):
                d_pair[pair, here, :128] += d_q
                d_pair[pair, past, 128:256] += d_k
                d_pair[pair, past, 256:] += d_v
    for pair in range(4):
        cos, sin = cosine[pl.ds(0, SHORT), :], -sine[pl.ds(0, SHORT), :]
        rows = pl.ds(0, SHORT)
        d_three[pair, :, :128] = turn(d_pair[pair, rows, :128], cos, sin).astype(LOW)
        d_three[pair, :, 128:256] = turn(d_pair[pair, rows, 128:256], cos, sin).astype(LOW)
        d_three[pair, :, 256:] = d_pair[pair, rows, 256:].astype(LOW)
    total[...] = sum(dot_nt(d_three[pair], fqkv[pair]) for pair in range(4))
    stack[:, 1024:1408] = dot_tn(b1[...], d_three[z]).astype(LOW)

    for step in range(3):
        here = pl.ds(176 * step, 176)
        grad = total[here, :]
        back, unit_grad = norm_back(c0[here, :], c_gain[...], grad)
        sums[0] = sums[0] + jnp.sum(unit_grad, axis=0, keepdims=True)
        sums[1] = sums[1] + jnp.sum(grad, axis=0, keepdims=True)
        b1[here, :] = (c1[here, :] + back).astype(LOW)
    stack[:, 1536:] = as_columns(sums).astype(LOW)

    save(15, stack)
    down = b1[pl.ds(pl.multiple_of(z * 128, 128), PART), :]
    for part in range(4):
        lane = slice(128 * part, 128 * part + 128)
        thin[part, pl.ds(0, 8), :] = jnp.zeros((8, 128), WIDE)
        thin[part, pl.ds(392, 48), :] = jnp.zeros((48, 128), WIDE)
        thin[part, pl.ds(8, OWN), :] = m[:, lane].astype(WIDE)
    for r in range(3):
        put_early(r, dot_tn(every_third(6 + r, PART), down))
    for r in range(3):
        back = dot_nt(down, wp[512 * r : 512 * r + 512, :])
        for part in range(4):
            thin[part, pl.ds(6 + r, PART, 3), :] = back[:, 128 * part : 128 * part + 128]
    for part in range(4):
        lane = slice(128 * part, 128 * part + 128)
        ds[:, lane] = valid * (cot[:, lane].astype(WIDE) + thin[part, pl.ds(8, OWN), :])
    save(13, ds)
    save(14, early)
    copies.finish()
    for step in range(1, 4):
        block_move(lax.rem(z + step, 4), z).wait_send()
    for move in saved.values():
        move.wait()


def front(lengths, x, cot, gains, frequency, weights, shards):
    def shape(*dims, kind=LOW):
        return (dims, kind)

    outs = [
        shape(ROWS, WIDTH),
        shape(ROWS, 128),
        shape(ROWS, 128),
        shape(ROWS, 128),
        shape(ROWS, 128),
        shape(8, ROWS, kind=WIDE),
        shape(OWN, WIDTH),
        shape(OWN, WIDTH, kind=WIDE),
        shape(OWN, WIDTH),
        shape(OWN, HIDDEN),
        shape(OWN, HIDDEN),
        shape(WIDTH, OWN),
        shape(OWN, WIDTH),
        shape(OWN, WIDTH, kind=WIDE),
        shape(HIDDEN, 768),
        shape(*COARSE_STACK),
    ]
    scratch = [
        shape(WIDTH, WIDTH),
        shape(WIDTH, HIDDEN),
        shape(HIDDEN, WIDTH),
        shape(ROWS, WIDTH),
        shape(WIDTH, ROWS),
        shape(ROWS, 128, kind=WIDE),
        shape(ROWS, 128, kind=WIDE),
        shape(3, OWN, WIDTH),
        shape(4, 440, 128, kind=WIDE),
        shape(OWN, WIDTH, kind=WIDE),
        shape(OWN, WIDTH),
        shape(4, PART, WIDTH),
        shape(4, 128, WIDTH),
        shape(4, WIDTH, OWN),
        shape(4, 128, WIDTH),
        shape(4, WIDTH, WIDTH),
        shape(4, WIDTH, WIDTH),
        shape(SHORT, WIDTH, kind=WIDE),
        shape(SHORT, WIDTH, kind=WIDE),
        shape(SHORT, WIDTH),
        shape(SHORT, WIDTH),
        shape(SHORT, WIDTH),
        shape(640, WIDTH),
        shape(640, WIDTH),
        shape(640, WIDTH),
        shape(SHORT, WIDTH),
        shape(4, 8, 640, kind=WIDE),
        shape(SHORT, WIDTH),
        shape(SHORT, 256),
        shape(SHORT, 256),
        shape(SHORT, WIDTH, kind=WIDE),
        shape(128, WIDTH, kind=WIDE),
        shape(4, 640, OWN, kind=WIDE),
        shape(4, SHORT, OWN),
        shape(SHORT, WIDTH),
        shape(SHORT, WIDTH),
    ]
    vmem = pl.BlockSpec(memory_space=VMEM)
    hbm = pl.BlockSpec(memory_space=pl.ANY)
    copy_count = 160
    return pl.pallas_call(
        front_kernel,
        out_shape=[jax.ShapeDtypeStruct(*out) for out in outs],
        in_specs=[pl.BlockSpec(memory_space=pltpu.SMEM)] + [vmem] * 11 + [hbm] * 14,
        out_specs=[hbm] * len(outs),
        scratch_shapes=[VMEM(*out) for out in outs + scratch]
        + [pltpu.SemaphoreType.DMA((copy_count,)), pltpu.SemaphoreType.DMA((copy_count,))],
        compiler_params=pltpu.CompilerParams(
            collective_id=1, has_side_effects=True, vmem_limit_bytes=60 * 2**20
        ),
    )(lengths, x, cot, *gains, frequency, *weights, *shards)


class Stream:
    def __init__(self, stack, low, high, axes, spread=False):
        self.stack, self.lanes = stack, pl.ds(low, high - low)
        self.axes = axes
        self.levels = (*axes, "z") if spread else axes
        self.spread = spread

    def landing_shapes(self, row_counts):
        rows = row_counts[self.stack] // 2
        shapes = []
        for axis in self.axes[1:]:
            rows = rows // SIZES[axis]
            shapes.append((3, rows, self.lanes.size))
        return shapes


STREAMS = (
    Stream(0, 0, 384, ("core", "z", "y", "x")),
    Stream(0, 384, 768, ("core", "x", "z", "y")),
    Stream(1, 0, 768, ("core", "x", "y")),
    Stream(1, 768, 1664, ("core", "y", "x")),
    Stream(2, 0, 384, ("core", "y", "x", "z")),
    Stream(2, 384, 768, ("core", "z", "x", "y")),
    Stream(2, 768, 1024, ("core", "y", "x", "z")),
    Stream(2, 1024, 1152, ("core", "z", "x", "y")),
    Stream(3, 0, 256, ("core", "x", "y"), True),
    Stream(3, 256, 512, ("core", "x", "y"), True),
)
STACK_SHAPES = ((HIDDEN, 768), COARSE_STACK, (HIDDEN, 1152), (WIDTH, WIDTH))
STACK_ROWS = tuple(shape[0] for shape in STACK_SHAPES)
ORDER = (
    -1, 0, 1, 2, 3, -1, -1, -1, -1, 0, 1, 2, 3, -1, -1, -1, -1, 4, 5, 6, -1, -1, 7, 4, 5, 6, 7, 3, 0, 1, -1,
    -1, 2, -1, 3, -1, -1, -1, 4, -1, -1, -1, 3, -1, 5, -1, 6, -1, 7, 4, -1, 0, -1, 1, 2, -1, 9, 8, 5, 9, 8, 6,
    7, 0, 3, 1, 2, 5, 3, 7, 9, 4, 8, 1, 0, 5, 7, 6, 9, 4, 8, 2, 1, 0, 2, 6, 9, 5, -1, 7, 8, 4, 9, 8, 1, 0, 6,
    1, 0, 4, 9, 4, 5, 9, 6, 5, 7, 8, 6, 7, 8,
)


ROWS_AT_ONCE = {128: 256, 256: 128, 384: 64, 512: 64, 640: 32, 768: 32, 896: 32, 1024: 32}


class Summing:
    def __init__(self, stream, source, total, out, landings, copies, coords):
        self.stream, self.source, self.total, self.out = stream, source, total, out
        self.landings, self.copies, self.coords = landings, copies, coords
        self.pending = []
        self.tick_count = 0

    def rows_at(self, level, who, whole):
        rows = STACK_ROWS[self.stream.stack]
        start = 0
        for axis in self.stream.axes[:level]:
            rows = rows // SIZES[axis]
            if whole or axis != "core":
                start = start + who[axis] * rows
        return pl.ds(pl.multiple_of(start, 16), rows)

    def start_down(self, level):
        axis = self.stream.axes[level]
        lanes = self.stream.lanes
        self.pending = []
        for step in range(1, SIZES[axis]):
            other = moved(self.coords, axis, step)
            where = self.rows_at(level + 1, other, level == 0)
            if level == 0:
                source = self.source.at[where, lanes]
                target = self.total.at[pl.ds(0, where.size), lanes]
            else:
                source = self.total.at[where, lanes]
                target = self.landings[level - 1].at[step - 1]
            self.pending.append(self.copies.remote(source, target, other))

    def add_down(self, level):
        lanes = self.stream.lanes
        for move in self.pending:
            move.wait_recv()
        here = self.rows_at(level + 1, self.coords, False)
        mine = self.rows_at(1, self.coords, True)
        step_rows = min(here.size, ROWS_AT_ONCE[lanes.size])

        def add(index, carry):
            at = pl.multiple_of(index * step_rows, 16)
            part = pl.ds(pl.multiple_of(here.start + at, 16), step_rows)
            value = self.total[part, lanes].astype(WIDE)
            if level == 0:
                own = pl.ds(pl.multiple_of(mine.start + at, 16), step_rows)
                value = value + self.source[own, lanes].astype(WIDE)
            else:
                for slot in range(3):
                    landed = self.landings[level - 1][slot, pl.ds(at, step_rows), :]
                    value = value + landed.astype(WIDE)
            self.total[part, lanes] = value.astype(LOW)
            return carry

        lax.fori_loop(0, here.size // step_rows, add, 0)

    def start_up(self, level):
        axes = self.stream.axes
        where = self.rows_at(min(level + 1, len(axes)), self.coords, True)
        if level == len(axes):
            part = self.out.at[self.coords["z"], where, self.stream.lanes]
        elif self.stream.spread:
            part = self.out.at[pl.ds(0, 4), where, self.stream.lanes]
        else:
            part = self.out.at[where, self.stream.lanes]
        axis = self.stream.levels[level]
        self.pending = [
            self.copies.remote(part, part, moved(self.coords, axis, step))
            for step in range(1, SIZES[axis])
        ]

    def tick(self):
        now = self.tick_count
        self.tick_count += 1
        down, depth = len(self.stream.axes), len(self.stream.levels)
        if now < down:
            if now:
                self.add_down(now - 1)
            self.start_down(now)
        elif now == down:
            self.add_down(down - 1)
            last = self.rows_at(down, self.coords, True)
            value = self.total[self.rows_at(down, self.coords, False), self.stream.lanes]
            if self.stream.spread:
                self.out[self.coords["z"], last, self.stream.lanes] = value
            else:
                self.out[last, self.stream.lanes] = value
            self.start_up(depth - 1)
        elif now <= down + depth:
            for move in self.pending:
                move.wait_recv()
            if now < down + depth:
                self.start_up(depth - 1 - (now - down))

    def done(self):
        return self.tick_count > len(self.stream.axes) + len(self.stream.levels)


def back_kernel(*refs):
    (x_hbm, ds_hbm, h_hbm, a2_hbm, act_hbm, slope_hbm, o_own_hbm, wqkv_hbm, wq_hbm, wk_hbm, wv_hbm,
     wo_hbm, we_hbm, wc_hbm, a1_hbm, q_hbm, k_hbm, v_hbm, o_hbm, level_hbm, early_hbm,
     coarse_hbm) = refs[:22]
    (frequency, a_gain, a_shift, f_gain) = refs[22:26]
    x_out, *total_outs = refs[26:31]
    (x, ds, h, a2, act, slope, o_own, wqkv, wo, we, wc, a1, q, k, v, o, level, early, coarse, cosine,
     sine, wall, low, d_pre, dh, d_own, d_heads, d_acc, turned, d_rows, d_weight, middle, late) = refs[31:64]
    totals, outs = refs[64:68], refs[68:72]
    *landings, send_sem, recv_sem = refs[72:]
    coords = my_coords()
    z = coords["z"]
    others = [moved(coords, "z", step) for step in (1, 3, 2)]
    copies = Copies(send_sem, recv_sem)
    lane = pl.ds(pl.multiple_of(z * 128, 128), 128)
    own = pl.ds(pl.multiple_of(z * OWN, OWN), OWN)
    loads, writes = {}, []

    def load(name, *pairs):
        loads[name] = [copies.local(source, target) for source, target in pairs]

    def loaded(name):
        for move in loads.pop(name):
            move.wait()

    load("early", (early_hbm, early), (coarse_hbm, coarse))
    load("first", (ds_hbm, ds), (wc_hbm, wc), (slope_hbm, slope), (act_hbm, act), (a2_hbm, a2))
    meet(coords, ("core", "x", "y", "z"))

    sources = (early, coarse, middle, late)
    streams = []
    for stream in STREAMS:
        count = len(stream.axes) - 1
        streams.append(
            Summing(
                stream,
                sources[stream.stack],
                totals[stream.stack],
                outs[stream.stack],
                landings[:count],
                copies,
                coords,
            )
        )
        landings = landings[count:]

    def tick(number):
        streams[number].tick()
        if streams[number].done():
            stack, lanes = streams[number].stream.stack, streams[number].stream.lanes
            part = (slice(None),) * (len(outs[stack].shape) - 1) + (lanes,)
            writes.append(copies.local(outs[stack].at[part], total_outs[stack].at[part]))

    def widen_back(index):
        here = pl.ds(256 * index, 256)
        back = (slope[:, here].astype(WIDE) * dot_nt(low[...], wc[here, :])).astype(LOW)
        d_pre[:, here] = back
        middle[here, :512] = dot_tn(act[:, here], low[...]).astype(LOW)
        down = pl.ds(512 * (index // 2), 512)
        across = pl.ds(512 + 256 * (index % 2), 256)
        middle[down, across] = dot_tn(a2[...], back).astype(LOW)

    sent_blocks = send_sem.shape[0] - 4
    got_blocks = recv_sem.shape[0] - 4

    def rows_move(target, source):
        return pltpu.make_async_remote_copy(
            src_ref=turned.at[pl.ds(pl.multiple_of(target * OWN, OWN), OWN), :],
            dst_ref=d_rows.at[:, pl.ds(pl.multiple_of(source * OWN, 128), OWN)],
            send_sem=send_sem.at[sent_blocks + target],
            recv_sem=recv_sem.at[got_blocks + source],
            device_id=device_of({**coords, "z": target}),
            device_id_type=MESH,
        )

    def steps():
        loaded("first")
        low[...] = ds[...].astype(LOW)
        load("second", (we_hbm, we), (h_hbm, h), (wo_hbm, wo), (o_own_hbm, o_own))
        yield
        for index in range(8):
            widen_back(index)
            yield
        load(
            "third",
            (q_hbm, q),
            (k_hbm, k),
            (v_hbm, v),
            (o_hbm, o),
            (level_hbm, level),
            (a1_hbm, a1),
            (wqkv_hbm, wqkv),
            (x_hbm, x),
            *(
                (
                    weight.at[:, pl.ds(128 * group, 128)],
                    wall.at[:, pl.ds(OWN * group + 128 * place, 128)],
                )
                for group in range(4)
                for place, weight in enumerate((wq_hbm, wk_hbm, wv_hbm))
            ),
        )
        loaded("second")
        for part in range(2):
            here = slice(256 * part, 256 * part + 256)
            dh[:, here] = dot_nt(d_pre[...], we[here, :])
        sums = [jnp.zeros((1, WIDTH), WIDE) for _ in range(2)]
        for step in range(3):
            here = pl.ds(128 * step, 128)
            grad = dh[here, :]
            back, unit_grad = norm_back(h[here, :], f_gain[...], grad)
            sums[0] = sums[0] + jnp.sum(unit_grad, axis=0, keepdims=True)
            sums[1] = sums[1] + jnp.sum(grad, axis=0, keepdims=True)
            back = ds[here, :] + back
            dh[here, :] = back
            low[here, :] = back.astype(LOW)
        d_own[...] = dot_nt(low[...], wo[...]).astype(LOW)
        head_moves = [
            copies.remote(
                d_own.at[:, pl.ds(pl.multiple_of(other["z"] * 128, 128), 128)],
                d_heads.at[own, :],
                other,
            )
            for other in others
        ]
        d_heads[own, :] = d_own[:, lane]
        yield
        output_grad = dot_tn(o_own[...], low[...]).astype(LOW)
        for part in range(4):
            middle[512 * part : 512 * part + 512, 1024:] = output_grad[
                :, 128 * part : 128 * part + 128
            ]
        late_columns = as_columns(sums)
        fill_tables(frequency[...], cosine, sine)
        d_acc[...] = jnp.zeros_like(d_acc)
        d_weight[...] = jnp.zeros_like(d_weight)
        yield
        loaded("third")
        for move in head_moves:
            move.wait_recv()
        column_sums = jnp.zeros((1, OWN), WIDE)
        for block in reversed(range(4)):
            here = pl.ds(OWN * block, OWN)
            deltas = pair_sums(d_heads[here, :].astype(WIDE) * o[here, :].astype(WIDE))
            for past in reversed(range(block + 1)):
                there = pl.ds(OWN * past, OWN)
                ((d_q, d_k, d_v),) = attend_back_blocks(
                    [
                        (
                            q[here, :],
                            d_heads[here, :],
                            k[there, :],
                            v[there, :],
                            level[:, here],
                            deltas,
                        )
                    ],
                    0 if past == block else None,
                )
                d_acc[here, :128] += d_q
                d_acc[there, 128:256] += d_k
                d_acc[there, 256:] += d_v
                yield
            cos, sin = cosine[here, :], -sine[here, :]
            turned[here, :128] = turn(d_acc[here, :128], cos, sin).astype(LOW)
            turned[here, 128:256] = turn(d_acc[here, 128:256], cos, sin).astype(LOW)
            turned[here, 256:] = d_acc[here, 256:].astype(LOW)

            @pl.when(z != block)
            def send():
                rows_move(block, z).start()

            d_weight[...] += dot_tn(a1[here, :], turned[here, :])
            column_sums = column_sums + jnp.sum(
                turned[here, :].astype(WIDE), axis=0, keepdims=True
            )
            yield
        weight = wqkv[...].astype(WIDE)
        late[:, :OWN] = d_weight[...].astype(LOW)
        shift_grad = jnp.sum(weight * column_sums, axis=1, keepdims=True)
        whole = jnp.sum(weight * d_weight[...], axis=1, keepdims=True)
        columns = as_columns([a_gain[...], a_shift[...]])
        gain_grad = (whole - columns[:, 1:2] * shift_grad) * (1.0 / columns[:, 0:1])
        lanes = lanes_iota((WIDTH, 128))
        columns = jnp.where(lanes == 2, gain_grad, jnp.where(lanes == 3, shift_grad, late_columns))
        late[:, OWN:] = columns.astype(LOW)
        yield
        d_rows[:, pl.ds(pl.multiple_of(z * OWN, 128), OWN)] = turned[own, :]
        for step in range(1, 4):
            rows_move(z, lax.rem(z + step, 4)).wait_recv()
        ds[...] = dot_nt(d_rows[...], wall[...])
        for step in range(3):
            here = pl.ds(128 * step, 128)
            back, _ = norm_back(x[here, :].astype(WIDE), a_gain[...], ds[here, :])
            dh[here, :] = dh[here, :] + back
        writes.append(copies.local(dh, x_out))
        yield

    loaded("early")
    walk = steps()
    for number in ORDER:
        if number < 0:
            next(walk)
        else:
            tick(number)
    copies.finish()
    for step in range(1, 4):
        rows_move(lax.rem(z + step, 4), z).wait_send()
    for move in writes:
        move.wait()


def back(operands, frequency, gains):
    def shape(*dims, kind=LOW):
        return (dims, kind)

    outs = [shape(OWN, WIDTH, kind=WIDE)] + [shape(*dims) for dims in STACK_SHAPES[:3]]
    outs.append(shape(4, WIDTH, WIDTH))
    scratch = [
        shape(OWN, WIDTH),
        shape(OWN, WIDTH, kind=WIDE),
        shape(OWN, WIDTH, kind=WIDE),
        shape(OWN, WIDTH),
        shape(OWN, HIDDEN),
        shape(OWN, HIDDEN),
        shape(OWN, WIDTH),
        shape(WIDTH, OWN),
        shape(WIDTH, WIDTH),
        shape(WIDTH, HIDDEN),
        shape(HIDDEN, WIDTH),
        shape(ROWS, WIDTH),
        shape(ROWS, 128),
        shape(ROWS, 128),
        shape(ROWS, 128),
        shape(ROWS, 128),
        shape(8, ROWS, kind=WIDE),
        shape(*STACK_SHAPES[0]),
        shape(*STACK_SHAPES[1]),
        shape(ROWS, 128, kind=WIDE),
        shape(ROWS, 128, kind=WIDE),
        shape(WIDTH, ROWS),
        shape(OWN, WIDTH),
        shape(OWN, HIDDEN),
        shape(OWN, WIDTH, kind=WIDE),
        shape(OWN, WIDTH),
        shape(ROWS, 128),
        shape(ROWS, OWN, kind=WIDE),
        shape(ROWS, OWN),
        shape(OWN, ROWS),
        shape(WIDTH, OWN, kind=WIDE),
        shape(*STACK_SHAPES[2]),
        shape(*STACK_SHAPES[3]),
    ]
    scratch += [shape(rows // 2, lanes) for rows, lanes in STACK_SHAPES]
    scratch += outs[1:]
    for stream in STREAMS:
        scratch += [shape(*dims) for dims in stream.landing_shapes(STACK_ROWS)]
    vmem = pl.BlockSpec(memory_space=VMEM)
    hbm = pl.BlockSpec(memory_space=pl.ANY)
    copy_count = 280
    return pl.pallas_call(
        back_kernel,
        out_shape=[jax.ShapeDtypeStruct(*out) for out in outs],
        in_specs=[hbm] * len(operands) + [vmem] * 4,
        out_specs=[hbm] * len(outs),
        scratch_shapes=[VMEM(*part) for part in scratch]
        + [pltpu.SemaphoreType.DMA((copy_count,)), pltpu.SemaphoreType.DMA((copy_count,))],
        compiler_params=pltpu.CompilerParams(
            collective_id=2, has_side_effects=True, vmem_limit_bytes=63 * 2**20
        ),
    )(*operands, frequency, *gains)


def unstack_kernel(*refs):
    stacks_hbm, (vectors_out, *outs_hbm) = refs[:4], refs[4:19]
    stacks, wides, sems = refs[19:23], refs[23:37], refs[37]
    loads = [
        pltpu.make_async_copy(source, target, sems.at[place])
        for place, (source, target) in enumerate(zip(stacks_hbm, stacks))
    ]
    for place in (2, 0, 1, 3):
        loads[place].start()
    early, coarse, middle, late = stacks
    (wq, wk, wv, wo, we, wc, wp, cq, ck, cv, co, ce, cc, wu) = wides
    writes = []

    def write(place):
        move = pltpu.make_async_copy(wides[place], outs_hbm[place], sems.at[4 + place])
        move.start()
        writes.append(move)

    loads[2].wait()
    for step in range(4):
        here = slice(512 * step, 512 * step + 512)
        wc[here, :] = middle[here, :512].astype(WIDE)
    write(5)
    for part in range(4):
        here = slice(512 * part, 512 * part + 512)
        we[:, here] = middle[here, 512:1024].astype(WIDE)
        wo[:, 128 * part : 128 * part + 128] = middle[here, 1024:].astype(WIDE)
    write(4)
    write(3)
    loads[0].wait()
    for number in range(6):
        for part in range(2):
            down, across = divmod(2 * number + part, 3)
            block = early[512 * down : 512 * down + 512, 256 * across : 256 * across + 256].astype(WIDE)
            inside = 256 * part
            if number < 3:
                wp[512 * number : 512 * number + 512, inside : inside + 256] = block
            else:
                start = 512 * (number - 3) + inside
                wu[:, start : start + 256] = block
        if number == 2:
            write(6)
    write(13)
    loads[1].wait()
    ce[...] = coarse[:, :512].astype(WIDE)
    write(11)
    cc[...] = coarse[:, 512:1024].astype(WIDE)
    write(12)
    for place, ref in enumerate((cq, ck, cv)):
        ref[...] = coarse[:, 1024 + 128 * place : 1152 + 128 * place].astype(WIDE)
        write(7 + place)
    for part in range(4):
        here = slice(128 * part, 128 * part + 128)
        co[:, here] = coarse[here, 1408:1536].astype(WIDE)
    write(10)
    loads[3].wait()
    for place, ref in enumerate((wq, wk, wv)):
        for group in range(4):
            ref[:, 128 * group : 128 * group + 128] = late[
                group, :, 128 * place : 128 * place + 128
            ].astype(WIDE)
        write(place)
    columns = sum(late[group, :, OWN:].astype(WIDE) for group in range(4))
    vectors_out[:8, :] = jnp.transpose(columns)[:8]
    vectors_out[8:, :] = jnp.transpose(coarse[:, 1536:].astype(WIDE))[:8]
    for move in writes:
        move.wait()


def unstack(stacks):
    shapes = (
        [(WIDTH, WIDTH)] * 4
        + [(WIDTH, HIDDEN), (HIDDEN, WIDTH), (ROWS, WIDTH)]
        + [(WIDTH, 128)] * 3
        + [(128, WIDTH), (WIDTH, WIDTH), (WIDTH, WIDTH), (WIDTH, ROWS)]
    )
    vmem = pl.BlockSpec(memory_space=VMEM)
    hbm = pl.BlockSpec(memory_space=pl.ANY)
    return pl.pallas_call(
        unstack_kernel,
        out_shape=[jax.ShapeDtypeStruct(shape, WIDE) for shape in [(16, WIDTH)] + shapes],
        in_specs=[hbm] * 4,
        out_specs=[vmem] + [hbm] * len(shapes),
        scratch_shapes=[VMEM(stack.shape, LOW) for stack in stacks]
        + [VMEM(shape, WIDE) for shape in shapes]
        + [pltpu.SemaphoreType.DMA((4 + len(shapes),))],
        compiler_params=pltpu.CompilerParams(vmem_limit_bytes=60 * 2**20),
    )(*stacks)


def body(
    inputs,
    lengths,
    cotangent,
    attention_gain,
    attention_shift,
    query_weight,
    key_weight,
    value_weight,
    output_weight,
    feedforward_gain,
    feedforward_shift,
    expand_weight,
    contract_weight,
    pooling_weight,
    coarse_gain,
    coarse_shift,
    coarse_query,
    coarse_key,
    coarse_value,
    coarse_output,
    widen_gain,
    widen_shift,
    coarse_expand,
    coarse_contract,
    upsample_weight,
):
    def row(vector):
        return vector.reshape(1, -1)

    frequency = jnp.asarray(frequency_row())
    square = (query_weight, key_weight, value_weight)
    (a1, q, k, v, o, level, o_own, h, a2, act, slope, wqkv, mixed, ds, early, coarse_stack) = front(
        lengths,
        inputs,
        cotangent,
        [
            row(vector)
            for vector in (
                attention_gain,
                attention_shift,
                feedforward_gain,
                feedforward_shift,
                coarse_gain,
                coarse_shift,
                widen_gain,
                widen_shift,
            )
        ],
        frequency,
        (*square, output_weight, expand_weight, contract_weight, pooling_weight, upsample_weight),
        (coarse_query, coarse_key, coarse_value, coarse_output, coarse_expand, coarse_contract),
    )
    input_grad, *stacks = back(
        (
            inputs,
            ds,
            h,
            a2,
            act,
            slope,
            o_own,
            wqkv,
            *square,
            output_weight,
            expand_weight,
            contract_weight,
            a1,
            q,
            k,
            v,
            o,
            level,
            early,
            coarse_stack,
        ),
        frequency,
        (
            row(attention_gain),
            row(attention_shift),
            row(feedforward_gain),
        ),
    )
    vectors, wq, wk, wv, wo, we, wc, wp, cq, ck, cv, co, ce, cc, wu = unstack(stacks)
    return (
        mixed,
        input_grad,
        vectors[2],
        vectors[3],
        wq,
        wk,
        wv,
        wo,
        vectors[0],
        vectors[1],
        we,
        wc,
        wp,
        vectors[8],
        vectors[9],
        cq,
        ck,
        cv,
        co,
        vectors[10],
        vectors[11],
        ce,
        cc,
        wu,
    )


def solution(mesh):
    in_specs = (
        P(("seq", "head"), None),
        P("seq"),
        P(("seq", "head"), None),
        P(),
        P(),
        P(),
        P(),
        P(),
        P(),
        P(),
        P(),
        P(),
        P(),
        P(),
        P(),
        P(),
        P(None, "head"),
        P(None, "head"),
        P(None, "head"),
        P("head", None),
        P(),
        P(),
        P(None, "head"),
        P("head", None),
        P(),
    )
    out_specs = (
        P(("seq", "head"), None),
        P(("seq", "head"), None),
        P(),
        P(),
        P(),
        P(),
        P(),
        P(),
        P(),
        P(),
        P(),
        P(),
        P(),
        P(),
        P(),
        P(None, "head"),
        P(None, "head"),
        P(None, "head"),
        P("head", None),
        P(),
        P(),
        P(None, "head"),
        P("head", None),
        P(),
    )
    return jax.shard_map(body, mesh=mesh, in_specs=in_specs, out_specs=out_specs, check_vma=False)
```

```python
import functools
import math

import jax
import jax.numpy as jnp
import numpy as np
from jax import lax
from jax.experimental import pallas as pl
from jax.experimental.pallas import tpu as pltpu
from jax.sharding import PartitionSpec as P

MESH = pl.DeviceIdType.MESH
VMEM = pltpu.VMEM
LOW = jnp.bfloat16
WIDE = jnp.float32
EPSILON = 1e-05
OWN = 384
ROWS = 1536
WIDTH = 512
HIDDEN = 2048
SHORT = 528
PART = 144
SIZES = {"core": 2, "x": 4, "y": 4, "z": 4}


def my_coords():
    seq = lax.axis_index("seq")
    return {
        "core": lax.rem(seq, 2),
        "y": lax.rem(lax.div(seq, 2), 4),
        "x": lax.div(seq, 8),
        "z": lax.axis_index("head"),
    }


def moved(coords, axis, step):
    other = dict(coords)
    other[axis] = lax.rem(coords[axis] + step, SIZES[axis])
    return other


def device_of(coords):
    return {
        "seq": (coords["x"] * 4 + coords["y"]) * 2 + coords["core"],
        "head": coords["z"],
    }


def meet(coords, axes):
    barrier = pltpu.get_barrier_semaphore()
    count = 0
    for axis in axes:
        for step in range(1, SIZES[axis]):
            pl.semaphore_signal(
                barrier,
                inc=1,
                device_id=device_of(moved(coords, axis, step)),
                device_id_type=MESH,
            )
            count += 1
    pl.semaphore_wait(barrier, count)


def dot(left, right):
    return lax.dot_general(left, right, (((1,), (0,)), ((), ())), preferred_element_type=WIDE)


def dot_nt(left, right):
    return lax.dot_general(left, right, (((1,), (1,)), ((), ())), preferred_element_type=WIDE)


def dot_tn(left, right):
    return lax.dot_general(left, right, (((0,), (0,)), ((), ())), preferred_element_type=WIDE)


def lanes_iota(shape):
    return lax.broadcasted_iota(jnp.int32, shape, len(shape) - 1)


def rows_iota(shape):
    return lax.broadcasted_iota(jnp.int32, shape, 0)


def standard(values):
    centred = values - jnp.mean(values, axis=-1, keepdims=True)
    scale = lax.rsqrt(jnp.mean(centred * centred, axis=-1, keepdims=True) + EPSILON)
    return centred * scale, scale


def norm(values, gain, shift):
    return standard(values)[0] * gain + shift


def norm_back(values, gain, grad):
    unit, scale = standard(values)
    inner = grad * gain
    first = jnp.mean(inner, axis=-1, keepdims=True)
    second = jnp.mean(inner * unit, axis=-1, keepdims=True)
    return scale * (inner - first - unit * second), grad * unit


def turn(values, cosine, sine):
    lane = lanes_iota(values.shape)
    other = jnp.where(
        lax.rem(lane, 64) < 32, pltpu.roll(values, 96, 1), pltpu.roll(values, 32, 1)
    )
    return values * cosine + other * sine


def gelu_parts(values):
    half = 0.5 + 0.5 * lax.erf(values * math.sqrt(0.5))
    bell = jnp.exp(values * values * -0.5) * (1.0 / math.sqrt(2.0 * math.pi))
    return values * half, half + values * bell


def head_lanes(head, values):
    return jnp.where(lanes_iota(values.shape) // 64 == head, values, jnp.zeros_like(values))


def by_head(first, second):
    return jnp.where(lanes_iota(first.shape) < 64, first, second)


def head_rows(columns):
    shape = (8, 128)
    pick = (lanes_iota(shape) == rows_iota(shape) * 64).astype(WIDE)
    return lax.dot_general(
        pick,
        columns,
        (((1,), (1,)), ((), ())),
        precision=lax.Precision.HIGHEST,
        preferred_element_type=WIDE,
    )


def frequency_row():
    frequency = np.exp(np.arange(32, dtype=np.float32) * np.float32(-math.log(10000.0) / 32))
    return np.tile(frequency.astype(np.float32), 4)[None, :]


def fill_tables(frequency, cosine, sine):
    coarse = rows_iota((24, 128)).astype(WIDE) * 64.0 * frequency
    fine = rows_iota((64, 128)).astype(WIDE) * frequency
    sign = jnp.where(lax.rem(lanes_iota((64, 128)), 64) < 32, -1.0, 1.0)
    coarse_cos, coarse_sin = jnp.cos(coarse), jnp.sin(coarse)
    fine_cos, fine_sin = jnp.cos(fine), jnp.sin(fine)
    for place in range(24):
        one_cos, one_sin = coarse_cos[place : place + 1], coarse_sin[place : place + 1]
        here = pl.ds(64 * place, 64)
        cosine[here, :] = one_cos * fine_cos - one_sin * fine_sin
        sine[here, :] = (one_sin * fine_cos + one_cos * fine_sin) * sign


def as_columns(vectors):
    filler = jnp.zeros((128 - len(vectors), WIDTH), WIDE)
    return jnp.transpose(jnp.concatenate(vectors + [filler], axis=0))


class Copies:
    def __init__(self, send_sem, recv_sem):
        self.send_sem, self.recv_sem, self.count, self.sent = send_sem, recv_sem, 0, []

    def remote(self, source, target, other):
        place = self.count
        self.count += 1
        move = pltpu.make_async_remote_copy(
            src_ref=source,
            dst_ref=target,
            send_sem=self.send_sem.at[place],
            recv_sem=self.recv_sem.at[place],
            device_id=device_of(other),
            device_id_type=MESH,
        )
        move.start()
        self.sent.append(move)
        return move

    def local(self, source, target):
        place = self.count
        self.count += 1
        move = pltpu.make_async_copy(source, target, self.recv_sem.at[place])
        move.start()
        return move

    def finish(self):
        for move in self.sent:
            move.wait_send()


def pair_sums(columns):
    shape = (8, 128)
    pick = (lanes_iota(shape) // 64 == rows_iota(shape)).astype(WIDE)
    return lax.dot_general(
        pick,
        columns,
        (((1,), (1,)), ((), ())),
        precision=lax.Precision.HIGHEST,
        preferred_element_type=WIDE,
    )


def attend_tiles(items, before, width, offset):
    last, first = pl.ds(before, width), pl.ds(0, before)
    chains = [(item, head) for item in items for head in range(2)]
    queries = [head_lanes(head, item[0]) for item, head in chains]
    near = [dot_nt(query, item[1][last, item[3]]) for query, (item, _) in zip(queries, chains)]
    keep = [
        lanes_iota(near[0].shape) <= rows_iota(near[0].shape) + shift
        for shift in (offset if isinstance(offset, tuple) else (offset,) * len(items))
    ]
    near = [jnp.where(keep[place // 2], scores, -1e30) for place, scores in enumerate(near)]
    tops = [jnp.max(scores, axis=-1, keepdims=True) for scores in near]
    if before:
        far = [dot_nt(query, item[1][first, item[3]]) for query, (item, _) in zip(queries, chains)]
        tops = [jnp.maximum(t, jnp.max(s, axis=-1, keepdims=True)) for t, s in zip(tops, far)]
        far = [jnp.exp(scores - t) for scores, t in zip(far, tops)]
    near = [jnp.exp(scores - t) for scores, t in zip(near, tops)]
    totals = [jnp.sum(probs, axis=-1, keepdims=True) for probs in near]
    mixed = [dot(probs.astype(LOW), item[2][last, item[3]]) for probs, (item, _) in zip(near, chains)]
    if before:
        totals = [t + jnp.sum(probs, axis=-1, keepdims=True) for t, probs in zip(totals, far)]
        mixed = [
            m + dot(probs.astype(LOW), item[2][first, item[3]])
            for m, probs, (item, _) in zip(mixed, far, chains)
        ]
    outs = [m * (1.0 / t) for m, t in zip(mixed, totals)]
    levels = [t + jnp.log(total) for t, total in zip(tops, totals)]
    shape = (items[0][0].shape[0], 128)
    results = []
    for place in range(len(items)):
        a, b = 2 * place, 2 * place + 1
        level = by_head(jnp.broadcast_to(levels[a], shape), jnp.broadcast_to(levels[b], shape))
        results.append((by_head(outs[a], outs[b]), head_rows(level)))
    return results


def attend_back_blocks(items, offset):
    chains = [(item, head) for item in items for head in range(2)]
    queries = [head_lanes(head, item[0]) for item, head in chains]
    d_outs = [head_lanes(head, item[1]) for item, head in chains]
    scores = [dot_nt(item[2], query) for query, (item, _) in zip(queries, chains)]
    d_probs = [dot_nt(item[3], d_out) for d_out, (item, _) in zip(d_outs, chains)]
    probs = [
        jnp.exp(score - item[4][head : head + 1]) for score, (item, head) in zip(scores, chains)
    ]
    if offset is not None:
        keep = rows_iota(probs[0].shape) <= lanes_iota(probs[0].shape) + offset
        probs = [jnp.where(keep, prob, 0.0) for prob in probs]
    d_scores = [
        (prob * (d_prob - item[5][head : head + 1])).astype(LOW)
        for prob, d_prob, (item, head) in zip(probs, d_probs, chains)
    ]
    d_values = [dot(prob.astype(LOW), d_out) for prob, d_out in zip(probs, d_outs)]
    d_keys = [dot(d_score, query) for d_score, query in zip(d_scores, queries)]
    d_queries = [dot_tn(d_score, item[2]) for d_score, (item, _) in zip(d_scores, chains)]
    return [
        (
            by_head(d_queries[i], d_queries[i + 1]) * 0.125,
            d_keys[i] + d_keys[i + 1],
            d_values[i] + d_values[i + 1],
        )
        for i in range(0, len(chains), 2)
    ]


COARSE_STACK = (WIDTH, 1664)
COARSE_TILES = ((0, 256, 256), (256, 256, 256), (512, 16, 128))


def front_kernel(*refs):
    (lengths, x, cot, a_gain, a_shift, f_gain, f_shift, c_gain, c_shift, w_gain, w_shift) = refs[:11]
    (frequency, wq_hbm, wk_hbm, wv_hbm, wo_hbm, we_hbm, wc_hbm, wp_hbm, wu_hbm) = refs[11:20]
    shards = refs[20:26]
    out_refs = refs[26:42]
    (a1, q, k, v, o, level, o_own, h, a2, act, slope, wqkv, mixed, ds, early, stack) = refs[42:58]
    (wo, we, wc, wp, wu, cosine, sine, landing, thin, s, m, c0g, dcg, fqkv, fo, fe, fc) = refs[58:75]
    (c0, c1, b1, b2, dr, cq, ck, cv, co, clevel, d_out, c_act, d_pre, total, top, d_pair, d_three,
     kept_act, kept_pre, send_sem, recv_sem) = refs[75:]
    saved = {}

    def save(key, source, part=None, place=None):
        target = out_refs[key if place is None else place]
        saved[key] = copies.local(source, target if part is None else target.at[part])

    coords = my_coords()
    z = coords["z"]
    core = coords["core"]
    right, left, far = (moved(coords, "z", step) for step in (1, 3, 2))
    copies = Copies(send_sem, recv_sem)
    lane = pl.ds(pl.multiple_of(z * 128, 128), 128)
    first_loads = [
        copies.local(weight.at[:, lane], wqkv.at[:, pl.ds(128 * place, 128)])
        for place, weight in enumerate((wq_hbm, wk_hbm, wv_hbm))
    ]
    loads = [
        copies.local(source, target)
        for source, target in ((wu_hbm, wu), (wo_hbm, wo), (we_hbm, we), (wc_hbm, wc), (wp_hbm, wp))
    ]
    own_weights = [
        copies.local(shard, full)
        for shard, full in zip(
            shards,
            [fqkv.at[z, :, pl.ds(128 * place, 128)] for place in range(3)]
            + [fo.at[z], fe.at[z], fc.at[z]],
        )
    ]
    meet(coords, ("core", "x", "y", "z"))
    low, high = pl.ds(0, OWN // 2), pl.ds(OWN // 2, OWN // 2)
    to_right = copies.remote(x.at[low], landing.at[0, low], right)
    to_left = copies.remote(x.at[high], landing.at[1, high], left)
    to_right_more = copies.remote(x.at[high], landing.at[0, high], right)
    to_left_more = copies.remote(x.at[low], landing.at[1, low], left)

    def project(block, index):
        start = pl.multiple_of(index * OWN, OWN)

        def rows_of(step, carry):
            here = pl.multiple_of(step * 128, 128)
            there = pl.ds(pl.multiple_of(start + here, 128), 128)
            values = block[pl.ds(here, 128), :].astype(WIDE)
            a1[there, :] = norm(values, a_gain[...], a_shift[...]).astype(LOW)
            return carry

        lax.fori_loop(0, OWN // 128, rows_of, 0)
        here = pl.ds(start, OWN)
        both = dot(a1[here, :], wqkv[...])
        cos, sin = cosine[here, :], sine[here, :]
        q[here, :] = (turn(both[:, :128], cos, sin) * 0.125).astype(LOW)
        k[here, :] = turn(both[:, 128:256], cos, sin).astype(LOW)
        v[here, :] = both[:, 256:].astype(LOW)

    fill_tables(frequency[...], cosine, sine)
    for load in first_loads:
        load.wait()
    project(x, z)
    to_right.wait_recv()
    far_right = copies.remote(landing.at[0, low], landing.at[2, low], right)
    to_left.wait_recv()
    far_left = copies.remote(landing.at[1, high], landing.at[2, high], left)

    valid = (rows_iota((OWN, 128)) + z * OWN < lengths[0]).astype(WIDE)
    for part in range(4):
        thin[part, pl.ds(0, 8), :] = jnp.zeros((8, 128), WIDE)
        thin[part, pl.ds(392, 48), :] = jnp.zeros((48, 128), WIDE)
        thin[part, pl.ds(8, OWN), :] = cot[:, 128 * part : 128 * part + 128].astype(WIDE) * valid

    def every_third(first, count):
        pieces = [thin[part, pl.ds(first, count, 3), :].astype(LOW) for part in range(4)]
        return jnp.concatenate(pieces, axis=1)

    loads[0].wait()
    lifted_back = sum(
        dot_nt(every_third(8 + r, 128), wu[:, 512 * r : 512 * r + 512]) for r in range(3)
    )
    dcg[z] = lifted_back.astype(LOW)

    to_right_more.wait_recv()
    project(landing.at[0], left["z"])
    to_left_more.wait_recv()
    project(landing.at[1], right["z"])
    far_right.wait_recv()
    far_left.wait_recv()
    project(landing.at[2], far["z"])

    for load in own_weights:
        load.wait()
    z_others = (right, left, far)
    z_sources = (left, right, far)
    pieces = {}
    def first_pieces(place, full):
        for way, axis in enumerate(("x", "y")):
            rows = pl.ds(pl.multiple_of(core * 256 + way * 128 + coords[axis] * 32, 32), 32)
            for step, other in enumerate(z_others):
                pieces[place, way, step] = copies.remote(full.at[z, rows], full.at[z, rows], other)
    first_pieces(0, fqkv)
    fo_rows = pl.ds(pl.multiple_of(core * 64, 64), 64)
    fo_moves = [copies.remote(fo.at[z, fo_rows], fo.at[z, fo_rows], other) for other in z_others]

    sent_blocks = send_sem.shape[0] - 4
    got_blocks = recv_sem.shape[0] - 4

    def block_move(target, source):
        return pltpu.make_async_remote_copy(
            src_ref=o.at[pl.ds(pl.multiple_of(target * OWN, OWN), OWN), :],
            dst_ref=o_own.at[:, pl.ds(pl.multiple_of(source * 128, 128), 128)],
            send_sem=send_sem.at[sent_blocks + target],
            recv_sem=recv_sem.at[got_blocks + source],
            device_id=device_of({**coords, "z": target}),
            device_id_type=MESH,
        )

    everything = pl.ds(0, 128)
    for block in reversed(range(4)):
        tiles = [pl.ds(OWN * block + 128 * step, 128) for step in range(3)]
        results = attend_tiles(
            [(q[here, :], k, v, everything) for here in tiles], OWN * block, OWN, (0, 128, 256)
        )
        for here, (mixed_tile, tops) in zip(tiles, results):
            o[here, :] = mixed_tile.astype(LOW)
            level[:, here] = tops

        @pl.when(z != block)
        def send():
            block_move(block, z).start()

        if block == 2:
            first_pieces(1, fe)
            first_pieces(2, fc)

    for place, ref in ((0, a1), (1, q), (2, k), (3, v), (4, o), (5, level), (11, wqkv)):
        save(place, ref)
    o_own[:, lane] = o[pl.ds(pl.multiple_of(z * OWN, OWN), OWN), :]

    spread, swaps = {0: [], 1: [], 2: []}, {0: [], 1: [], 2: []}
    whole = (fqkv, fe, fc)
    sibling = moved(coords, "core", 1)

    def spread_out(place):
        for way, axis in enumerate(("x", "y")):
            rows = pl.ds(pl.multiple_of(core * 256 + way * 128 + coords[axis] * 32, 32), 32)
            for step, source in enumerate(z_sources):
                pieces[place, way, step].wait_recv()
                part = whole[place].at[source["z"], rows]
                for far_step in range(1, 4):
                    spread[place].append(copies.remote(part, part, moved(coords, axis, far_step)))

    def swap(place):
        for move in spread[place]:
            move.wait_recv()
        half = pl.ds(pl.multiple_of(core * 256, 256), 256)
        for source in z_sources:
            part = whole[place].at[source["z"], half]
            swaps[place].append(copies.remote(part, part, sibling))

    spread_out(0)
    for step in range(1, 4):
        other = lax.rem(z + step, 4)
        block_move(z, other).wait_recv()
    dc_moves = [copies.remote(dcg.at[z], dcg.at[z], other) for other in z_others]
    save(6, o_own)

    for load in loads[1:]:
        load.wait()

    def mix(step, carry):
        here = pl.ds(pl.multiple_of(step * 128, 128), 128)
        hidden = x[here, :].astype(WIDE) + dot(o_own[here, :], wo[...])
        h[here, :] = hidden
        a2[here, :] = norm(hidden, f_gain[...], f_shift[...]).astype(LOW)
        return carry

    lax.fori_loop(0, 3, mix, 0)

    def widen(step, carry):
        here = pl.ds(pl.multiple_of(step * 256, 256), 256)
        value, back = gelu_parts(dot(a2[...], we[:, here]))
        act[:, here] = value.astype(LOW)
        slope[:, here] = back.astype(LOW)
        return carry

    lax.fori_loop(0, HIDDEN // 256, widen, 0)
    spread_out(1)
    spread_out(2)
    for place, ref in ((7, h), (8, a2), (9, act), (10, slope)):
        save(place, ref)

    for part in range(4):
        here = slice(128 * part, 128 * part + 128)
        if part % 2 == 0:
            wide = slice(256 * (part // 2), 256 * (part // 2) + 256)
            summed = h[:, wide] + dot(act[...], wc[:, wide])
            s[:, wide] = summed
        kept = (s[:, here] * valid).astype(LOW)
        m[:, here] = kept
        thin[part, pl.ds(8, OWN), :] = kept.astype(WIDE)
    pooled = sum(
        dot(every_third(6 + r, PART), wp[512 * r : 512 * r + 512, :]) for r in range(3)
    )
    c0g[z] = pooled.astype(LOW)
    c0_moves = [copies.remote(c0g.at[z], c0g.at[z], other) for other in z_others]
    fo_swaps = []
    for step, source in enumerate(z_sources):
        fo_moves[step].wait_recv()
        part = fo.at[source["z"], fo_rows]
        fo_swaps.append(copies.remote(part, part, sibling))
    swap(0)
    for move in c0_moves:
        move.wait_recv()

    own_lane = pl.ds(pl.multiple_of(z * 128, 128), 128)
    own_rows = pl.ds(pl.multiple_of(z * 128, 128), 128)

    def row_chunks(body):
        def run(step, carry):
            body(pl.ds(pl.multiple_of(step * 176, 16), 176))
            return carry

        lax.fori_loop(0, 3, run, 0)

    for part in range(4):
        base = 128 * part
        c0[pl.ds(base, 128), :] = c0g[part, pl.ds(0, 128), :].astype(WIDE)
        if part:
            first = pl.ds(base, 1)
            c0[first, :] = c0[first, :] + c0g[part - 1, pl.ds(128, 16), :].astype(WIDE)[:1]
    c0[pl.ds(512, 16), :] = c0g[3, pl.ds(128, 16), :].astype(WIDE)

    def first_norm(here):
        b1[here, :] = norm(c0[here, :], c_gain[...], c_shift[...]).astype(LOW)

    row_chunks(first_norm)
    for move in swaps[0]:
        move.wait_recv()
    for ref in (cq, ck, cv):
        ref[pl.ds(SHORT, 640 - SHORT), :] = jnp.zeros((640 - SHORT, WIDTH), LOW)

    for pair in range(4):
        lane = pl.ds(pair * 128, 128)
        both = dot(b1[...], fqkv[pair])
        cos, sin = cosine[pl.ds(0, SHORT), :], sine[pl.ds(0, SHORT), :]
        rows = pl.ds(0, SHORT)
        cq[rows, lane] = (turn(both[:, :128], cos, sin) * 0.125).astype(LOW)
        ck[rows, lane] = turn(both[:, 128:256], cos, sin).astype(LOW)
        cv[rows, lane] = both[:, 256:].astype(LOW)
    for first, count, width in COARSE_TILES:
        here = pl.ds(first, count)
        for pair, (mixed_tile, tops) in enumerate(
            attend_tiles([(cq[here, pl.ds(128 * p, 128)], ck, cv, pl.ds(128 * p, 128)) for p in range(4)], first, width, 0)
        ):
            co[here, pl.ds(128 * pair, 128)] = mixed_tile.astype(LOW)
            clevel[pair, :, here] = tops

    swap(1)
    swap(2)
    for move in dc_moves + fo_swaps:
        move.wait_recv()
    for part in range(4):
        dr[pl.ds(128 * part, 128), :] = dcg[part]
    dr[pl.ds(512, 16), :] = jnp.zeros((16, WIDTH), LOW)

    def second_norm(here):
        value = c0[here, :]
        for part in range(4):
            value = value + dot(co[here, 128 * part : 128 * part + 128], fo[part])
        c1[here, :] = value
        b2[here, :] = norm(value, w_gain[...], w_shift[...]).astype(LOW)

    row_chunks(second_norm)
    for move in swaps[1] + swaps[2]:
        move.wait_recv()
    total[...] = jnp.zeros_like(total)
    top[...] = c1[own_rows, :]

    def widen(keep, step, carry):
        slot = lax.rem(z + step // 2, 4)
        lane = pl.ds(pl.multiple_of(lax.rem(step, 2) * 256, 256), 256)
        value, slope = gelu_parts(dot(b2[...], fe[slot, :, lane]))
        c_act[...] = value.astype(LOW)
        d_pre[...] = (slope * dot_nt(dr[...], fc[slot, lane, :])).astype(LOW)
        if keep:
            kept_act[:, lane] = c_act[...]
            kept_pre[:, lane] = d_pre[...]
        top[...] += dot(c_act[own_rows, :], fc[slot, lane, :])
        total[...] += dot_nt(d_pre[...], fe[slot, :, lane])
        return carry

    lax.fori_loop(0, 2, functools.partial(widen, True), 0)
    lax.fori_loop(2, 8, functools.partial(widen, False), 0)

    def put_early(number, grad):
        for part in range(2):
            down, across = divmod(2 * number + part, 3)
            early[512 * down : 512 * down + 512, 256 * across : 256 * across + 256] = grad[
                :, 256 * part : 256 * part + 256
            ].astype(LOW)

    crest = top[...].astype(LOW)
    for r in range(3):
        lifted = dot(crest, wu[:, 512 * r : 512 * r + 512])
        for part in range(4):
            thin[part, pl.ds(8 + r, 128, 3), :] = lifted[:, 128 * part : 128 * part + 128]
    for part in range(4):
        lane = slice(128 * part, 128 * part + 128)
        mixed[:, lane] = (valid * (s[:, lane] + thin[part, pl.ds(8, OWN), :])).astype(LOW)
        thin[part, pl.ds(8, OWN), :] = cot[:, lane].astype(WIDE) * valid

    for r in range(3):
        put_early(3 + r, dot_tn(crest, every_third(8 + r, 128)))

    save(12, mixed)
    save(16, early.at[pl.ds(1024, 1024)], (pl.ds(1024, 1024),), 14)
    stack[:, :512] = dot_tn(b2[...], kept_pre[...]).astype(LOW)
    stack[:, 512:1024] = dot_tn(kept_act[...], dr[...]).astype(LOW)
    sums = [jnp.zeros((1, WIDTH), WIDE) for _ in range(4)]
    for step in range(3):
        here = pl.ds(176 * step, 176)
        grad = total[here, :]
        back, unit_grad = norm_back(c1[here, :], w_gain[...], grad)
        sums[2] = sums[2] + jnp.sum(unit_grad, axis=0, keepdims=True)
        sums[3] = sums[3] + jnp.sum(grad, axis=0, keepdims=True)
        back = dr[here, :].astype(WIDE) + back
        c1[here, :] = back
        b2[here, :] = back.astype(LOW)
    output_grad = dot_tn(co[:, own_lane], b2[...]).astype(LOW)
    for part in range(4):
        stack[128 * part : 128 * part + 128, 1408:1536] = output_grad[:, 128 * part : 128 * part + 128]
    for pair in range(4):
        d_out[:, pl.ds(128 * pair, 128)] = dot_nt(b2[...], fo[pair]).astype(LOW)
    lanes = [pl.ds(128 * pair, 128) for pair in range(4)]
    deltas = [
        pair_sums(d_out[:, lane].astype(WIDE) * co[:, lane].astype(WIDE)) for lane in lanes
    ]
    for first, count, width in COARSE_TILES:
        here = pl.ds(first, count)
        near, past = pl.ds(first, width), pl.ds(0, first)

        def items(there):
            return [
                (
                    cq[here, lane],
                    d_out[here, lane],
                    ck[there, lane],
                    cv[there, lane],
                    clevel[pair, :, here],
                    deltas[pair][:, first : first + count],
                )
                for pair, lane in enumerate(lanes)
            ]

        results = attend_back_blocks(items(near), 0)
        for pair, (d_q, d_k, d_v) in enumerate(results):
            d_pair[pair, here, :128] = d_q
            d_pair[pair, near, 128:256] = d_k
            d_pair[pair, near, 256:] = d_v
        if first:
            results = attend_back_blocks(items(past), None)
            for pair, (d_q, d_k, d_v) in enumerate(results):
                d_pair[pair, here, :128] += d_q
                d_pair[pair, past, 128:256] += d_k
                d_pair[pair, past, 256:] += d_v
    for pair in range(4):
        cos, sin = cosine[pl.ds(0, SHORT), :], -sine[pl.ds(0, SHORT), :]
        rows = pl.ds(0, SHORT)
        d_three[pair, :, :128] = turn(d_pair[pair, rows, :128], cos, sin).astype(LOW)
        d_three[pair, :, 128:256] = turn(d_pair[pair, rows, 128:256], cos, sin).astype(LOW)
        d_three[pair, :, 256:] = d_pair[pair, rows, 256:].astype(LOW)
    total[...] = sum(dot_nt(d_three[pair], fqkv[pair]) for pair in range(4))
    stack[:, 1024:1408] = dot_tn(b1[...], d_three[z]).astype(LOW)

    for step in range(3):
        here = pl.ds(176 * step, 176)
        grad = total[here, :]
        back, unit_grad = norm_back(c0[here, :], c_gain[...], grad)
        sums[0] = sums[0] + jnp.sum(unit_grad, axis=0, keepdims=True)
        sums[1] = sums[1] + jnp.sum(grad, axis=0, keepdims=True)
        b1[here, :] = (c1[here, :] + back).astype(LOW)
    stack[:, 1536:] = as_columns(sums).astype(LOW)

    save(15, stack)
    down = b1[pl.ds(pl.multiple_of(z * 128, 128), PART), :]
    for part in range(4):
        lane = slice(128 * part, 128 * part + 128)
        thin[part, pl.ds(0, 8), :] = jnp.zeros((8, 128), WIDE)
        thin[part, pl.ds(392, 48), :] = jnp.zeros((48, 128), WIDE)
        thin[part, pl.ds(8, OWN), :] = m[:, lane].astype(WIDE)
    for r in range(3):
        put_early(r, dot_tn(every_third(6 + r, PART), down))
    for r in range(3):
        back = dot_nt(down, wp[512 * r : 512 * r + 512, :])
        for part in range(4):
            thin[part, pl.ds(6 + r, PART, 3), :] = back[:, 128 * part : 128 * part + 128]
    for part in range(4):
        lane = slice(128 * part, 128 * part + 128)
        ds[:, lane] = valid * (cot[:, lane].astype(WIDE) + thin[part, pl.ds(8, OWN), :])
    save(13, ds)
    save(14, early.at[pl.ds(0, 1024)], (pl.ds(0, 1024),))
    copies.finish()
    for step in range(1, 4):
        block_move(lax.rem(z + step, 4), z).wait_send()
    for move in saved.values():
        move.wait()


def front(lengths, x, cot, gains, frequency, weights, shards):
    def shape(*dims, kind=LOW):
        return (dims, kind)

    outs = [
        shape(ROWS, WIDTH),
        shape(ROWS, 128),
        shape(ROWS, 128),
        shape(ROWS, 128),
        shape(ROWS, 128),
        shape(8, ROWS, kind=WIDE),
        shape(OWN, WIDTH),
        shape(OWN, WIDTH, kind=WIDE),
        shape(OWN, WIDTH),
        shape(OWN, HIDDEN),
        shape(OWN, HIDDEN),
        shape(WIDTH, OWN),
        shape(OWN, WIDTH),
        shape(OWN, WIDTH, kind=WIDE),
        shape(HIDDEN, 768),
        shape(*COARSE_STACK),
    ]
    scratch = [
        shape(WIDTH, WIDTH),
        shape(WIDTH, HIDDEN),
        shape(HIDDEN, WIDTH),
        shape(ROWS, WIDTH),
        shape(WIDTH, ROWS),
        shape(ROWS, 128, kind=WIDE),
        shape(ROWS, 128, kind=WIDE),
        shape(3, OWN, WIDTH),
        shape(4, 440, 128, kind=WIDE),
        shape(OWN, WIDTH, kind=WIDE),
        shape(OWN, WIDTH),
        shape(4, PART, WIDTH),
        shape(4, 128, WIDTH),
        shape(4, WIDTH, OWN),
        shape(4, 128, WIDTH),
        shape(4, WIDTH, WIDTH),
        shape(4, WIDTH, WIDTH),
        shape(SHORT, WIDTH, kind=WIDE),
        shape(SHORT, WIDTH, kind=WIDE),
        shape(SHORT, WIDTH),
        shape(SHORT, WIDTH),
        shape(SHORT, WIDTH),
        shape(640, WIDTH),
        shape(640, WIDTH),
        shape(640, WIDTH),
        shape(SHORT, WIDTH),
        shape(4, 8, 640, kind=WIDE),
        shape(SHORT, WIDTH),
        shape(SHORT, 256),
        shape(SHORT, 256),
        shape(SHORT, WIDTH, kind=WIDE),
        shape(128, WIDTH, kind=WIDE),
        shape(4, 640, OWN, kind=WIDE),
        shape(4, SHORT, OWN),
        shape(SHORT, WIDTH),
        shape(SHORT, WIDTH),
    ]
    vmem = pl.BlockSpec(memory_space=VMEM)
    hbm = pl.BlockSpec(memory_space=pl.ANY)
    copy_count = 160
    return pl.pallas_call(
        front_kernel,
        out_shape=[jax.ShapeDtypeStruct(*out) for out in outs],
        in_specs=[pl.BlockSpec(memory_space=pltpu.SMEM)] + [vmem] * 11 + [hbm] * 14,
        out_specs=[hbm] * len(outs),
        scratch_shapes=[VMEM(*out) for out in outs + scratch]
        + [pltpu.SemaphoreType.DMA((copy_count,)), pltpu.SemaphoreType.DMA((copy_count,))],
        compiler_params=pltpu.CompilerParams(
            collective_id=1, has_side_effects=True, vmem_limit_bytes=60 * 2**20
        ),
    )(lengths, x, cot, *gains, frequency, *weights, *shards)


class Stream:
    def __init__(self, stack, low, high, axes, spread=False):
        self.stack, self.lanes = stack, pl.ds(low, high - low)
        self.axes = axes
        self.levels = (*axes, "z") if spread else axes
        self.spread = spread

    def landing_shapes(self, row_counts):
        rows = row_counts[self.stack] // 2
        shapes = []
        for axis in self.axes[1:]:
            rows = rows // SIZES[axis]
            shapes.append((3, rows, self.lanes.size))
        return shapes


STREAMS = (
    Stream(0, 0, 384, ("core", "z", "y", "x")),
    Stream(0, 384, 768, ("core", "x", "z", "y")),
    Stream(1, 0, 768, ("core", "x", "y")),
    Stream(1, 768, 1664, ("core", "y", "x")),
    Stream(2, 0, 384, ("core", "y", "x", "z")),
    Stream(2, 384, 768, ("core", "z", "x", "y")),
    Stream(2, 768, 1024, ("core", "y", "x", "z")),
    Stream(2, 1024, 1152, ("core", "z", "x", "y")),
    Stream(3, 0, 256, ("core", "x", "y"), True),
    Stream(3, 256, 512, ("core", "x", "y"), True),
)
STACK_SHAPES = ((HIDDEN, 768), COARSE_STACK, (HIDDEN, 1152), (WIDTH, WIDTH))
STACK_ROWS = tuple(shape[0] for shape in STACK_SHAPES)
ORDER = (
    -1, 0, 1, 2, 3, -1, -1, -1, -1, 0, 1, 2, 3, -1, -1, -1, -1, 4, 5, 6, -1, -1, 7, 4, 5, 6, 7, 3, 0, 1, -1,
    -1, 2, -1, 3, -1, -1, -1, 4, -1, -1, -1, 3, -1, 5, -1, 6, -1, 7, 4, -1, 0, -1, 1, 2, -1, 9, 8, 5, 9, 8, 6,
    7, 0, 3, 1, 2, 5, 3, 7, 9, 4, 8, 1, 0, 5, 7, 6, 9, 4, 8, 2, 1, 0, 2, 6, 9, 5, -1, 7, 8, 4, 9, 8, 1, 0, 6,
    1, 0, 4, 9, 4, 5, 9, 6, 5, 7, 8, 6, 7, 8,
)


ROWS_AT_ONCE = {128: 256, 256: 128, 384: 64, 512: 64, 640: 32, 768: 32, 896: 32, 1024: 32}


class Summing:
    def __init__(self, stream, source, total, out, landings, copies, coords):
        self.stream, self.source, self.total, self.out = stream, source, total, out
        self.landings, self.copies, self.coords = landings, copies, coords
        self.pending = []
        self.tick_count = 0

    def rows_at(self, level, who, whole):
        rows = STACK_ROWS[self.stream.stack]
        start = 0
        for axis in self.stream.axes[:level]:
            rows = rows // SIZES[axis]
            if whole or axis != "core":
                start = start + who[axis] * rows
        return pl.ds(pl.multiple_of(start, 16), rows)

    def start_down(self, level):
        axis = self.stream.axes[level]
        lanes = self.stream.lanes
        self.pending = []
        for step in range(1, SIZES[axis]):
            other = moved(self.coords, axis, step)
            where = self.rows_at(level + 1, other, level == 0)
            if level == 0:
                source = self.source.at[where, lanes]
                target = self.total.at[pl.ds(0, where.size), lanes]
            else:
                source = self.total.at[where, lanes]
                target = self.landings[level - 1].at[step - 1]
            self.pending.append(self.copies.remote(source, target, other))

    def add_down(self, level):
        lanes = self.stream.lanes
        for move in self.pending:
            move.wait_recv()
        here = self.rows_at(level + 1, self.coords, False)
        mine = self.rows_at(1, self.coords, True)
        step_rows = min(here.size, ROWS_AT_ONCE[lanes.size])

        def add(index, carry):
            at = pl.multiple_of(index * step_rows, 16)
            part = pl.ds(pl.multiple_of(here.start + at, 16), step_rows)
            value = self.total[part, lanes].astype(WIDE)
            if level == 0:
                own = pl.ds(pl.multiple_of(mine.start + at, 16), step_rows)
                value = value + self.source[own, lanes].astype(WIDE)
            else:
                for slot in range(3):
                    landed = self.landings[level - 1][slot, pl.ds(at, step_rows), :]
                    value = value + landed.astype(WIDE)
            self.total[part, lanes] = value.astype(LOW)
            return carry

        lax.fori_loop(0, here.size // step_rows, add, 0)

    def start_up(self, level):
        axes = self.stream.axes
        where = self.rows_at(min(level + 1, len(axes)), self.coords, True)
        if level == len(axes):
            part = self.out.at[self.coords["z"], where, self.stream.lanes]
        elif self.stream.spread:
            part = self.out.at[pl.ds(0, 4), where, self.stream.lanes]
        else:
            part = self.out.at[where, self.stream.lanes]
        axis = self.stream.levels[level]
        self.pending = [
            self.copies.remote(part, part, moved(self.coords, axis, step))
            for step in range(1, SIZES[axis])
        ]

    def tick(self):
        now = self.tick_count
        self.tick_count += 1
        down, depth = len(self.stream.axes), len(self.stream.levels)
        if now < down:
            if now:
                self.add_down(now - 1)
            self.start_down(now)
        elif now == down:
            self.add_down(down - 1)
            last = self.rows_at(down, self.coords, True)
            value = self.total[self.rows_at(down, self.coords, False), self.stream.lanes]
            if self.stream.spread:
                self.out[self.coords["z"], last, self.stream.lanes] = value
            else:
                self.out[last, self.stream.lanes] = value
            self.start_up(depth - 1)
        elif now <= down + depth:
            for move in self.pending:
                move.wait_recv()
            if now < down + depth:
                self.start_up(depth - 1 - (now - down))

    def done(self):
        return self.tick_count > len(self.stream.axes) + len(self.stream.levels)


def back_kernel(*refs):
    (x_hbm, ds_hbm, h_hbm, a2_hbm, act_hbm, slope_hbm, o_own_hbm, wqkv_hbm, wq_hbm, wk_hbm, wv_hbm,
     wo_hbm, we_hbm, wc_hbm, a1_hbm, q_hbm, k_hbm, v_hbm, o_hbm, level_hbm, early_hbm,
     coarse_hbm) = refs[:22]
    (frequency, a_gain, a_shift, f_gain) = refs[22:26]
    x_out, *total_outs = refs[26:31]
    (x, ds, h, a2, act, slope, o_own, wqkv, wo, we, wc, a1, q, k, v, o, level, early, coarse, cosine,
     sine, wall, low, d_pre, dh, d_own, d_heads, d_acc, turned, d_rows, d_weight, middle, late) = refs[31:64]
    totals, outs = refs[64:68], refs[68:72]
    *landings, send_sem, recv_sem = refs[72:]
    coords = my_coords()
    z = coords["z"]
    others = [moved(coords, "z", step) for step in (1, 3, 2)]
    copies = Copies(send_sem, recv_sem)
    lane = pl.ds(pl.multiple_of(z * 128, 128), 128)
    own = pl.ds(pl.multiple_of(z * OWN, OWN), OWN)
    loads, writes = {}, []

    def load(name, *pairs):
        loads[name] = [copies.local(source, target) for source, target in pairs]

    def loaded(name):
        for move in loads.pop(name):
            move.wait()

    load("first", (ds_hbm, ds), (wc_hbm, wc), (slope_hbm, slope), (act_hbm, act), (a2_hbm, a2))
    load("early", (early_hbm, early), (coarse_hbm, coarse))
    meet(coords, ("core", "x", "y", "z"))

    sources = (early, coarse, middle, late)
    streams = []
    for stream in STREAMS:
        count = len(stream.axes) - 1
        streams.append(
            Summing(
                stream,
                sources[stream.stack],
                totals[stream.stack],
                outs[stream.stack],
                landings[:count],
                copies,
                coords,
            )
        )
        landings = landings[count:]

    def tick(number):
        streams[number].tick()
        if streams[number].done():
            stack, lanes = streams[number].stream.stack, streams[number].stream.lanes
            part = (slice(None),) * (len(outs[stack].shape) - 1) + (lanes,)
            writes.append(copies.local(outs[stack].at[part], total_outs[stack].at[part]))

    def widen_back(index):
        here = pl.ds(256 * index, 256)
        back = (slope[:, here].astype(WIDE) * dot_nt(low[...], wc[here, :])).astype(LOW)
        d_pre[:, here] = back
        middle[here, :512] = dot_tn(act[:, here], low[...]).astype(LOW)
        down = pl.ds(512 * (index // 2), 512)
        across = pl.ds(512 + 256 * (index % 2), 256)
        middle[down, across] = dot_tn(a2[...], back).astype(LOW)

    sent_blocks = send_sem.shape[0] - 4
    got_blocks = recv_sem.shape[0] - 4

    def rows_move(target, source):
        return pltpu.make_async_remote_copy(
            src_ref=turned.at[pl.ds(pl.multiple_of(target * OWN, OWN), OWN), :],
            dst_ref=d_rows.at[:, pl.ds(pl.multiple_of(source * OWN, 128), OWN)],
            send_sem=send_sem.at[sent_blocks + target],
            recv_sem=recv_sem.at[got_blocks + source],
            device_id=device_of({**coords, "z": target}),
            device_id_type=MESH,
        )

    def steps():
        loaded("first")
        low[...] = ds[...].astype(LOW)
        load("second", (we_hbm, we), (h_hbm, h), (wo_hbm, wo), (o_own_hbm, o_own))
        yield
        for index in range(8):
            widen_back(index)
            yield
        load(
            "third",
            (q_hbm, q),
            (k_hbm, k),
            (v_hbm, v),
            (o_hbm, o),
            (level_hbm, level),
            (a1_hbm, a1),
            (wqkv_hbm, wqkv),
            (x_hbm, x),
            *(
                (
                    weight.at[:, pl.ds(128 * group, 128)],
                    wall.at[:, pl.ds(OWN * group + 128 * place, 128)],
                )
                for group in range(4)
                for place, weight in enumerate((wq_hbm, wk_hbm, wv_hbm))
            ),
        )
        loaded("second")
        for part in range(2):
            here = slice(256 * part, 256 * part + 256)
            dh[:, here] = dot_nt(d_pre[...], we[here, :])
        sums = [jnp.zeros((1, WIDTH), WIDE) for _ in range(2)]
        for step in range(3):
            here = pl.ds(128 * step, 128)
            grad = dh[here, :]
            back, unit_grad = norm_back(h[here, :], f_gain[...], grad)
            sums[0] = sums[0] + jnp.sum(unit_grad, axis=0, keepdims=True)
            sums[1] = sums[1] + jnp.sum(grad, axis=0, keepdims=True)
            back = ds[here, :] + back
            dh[here, :] = back
            low[here, :] = back.astype(LOW)
        d_own[...] = dot_nt(low[...], wo[...]).astype(LOW)
        head_moves = [
            copies.remote(
                d_own.at[:, pl.ds(pl.multiple_of(other["z"] * 128, 128), 128)],
                d_heads.at[own, :],
                other,
            )
            for other in others
        ]
        d_heads[own, :] = d_own[:, lane]
        yield
        output_grad = dot_tn(o_own[...], low[...]).astype(LOW)
        for part in range(4):
            middle[512 * part : 512 * part + 512, 1024:] = output_grad[
                :, 128 * part : 128 * part + 128
            ]
        late_columns = as_columns(sums)
        fill_tables(frequency[...], cosine, sine)
        d_acc[...] = jnp.zeros_like(d_acc)
        d_weight[...] = jnp.zeros_like(d_weight)
        yield
        loaded("third")
        for move in head_moves:
            move.wait_recv()
        column_sums = jnp.zeros((1, OWN), WIDE)
        for block in reversed(range(4)):
            here = pl.ds(OWN * block, OWN)
            deltas = pair_sums(d_heads[here, :].astype(WIDE) * o[here, :].astype(WIDE))
            for past in reversed(range(block + 1)):
                there = pl.ds(OWN * past, OWN)
                ((d_q, d_k, d_v),) = attend_back_blocks(
                    [
                        (
                            q[here, :],
                            d_heads[here, :],
                            k[there, :],
                            v[there, :],
                            level[:, here],
                            deltas,
                        )
                    ],
                    0 if past == block else None,
                )
                d_acc[here, :128] += d_q
                d_acc[there, 128:256] += d_k
                d_acc[there, 256:] += d_v
                yield
            cos, sin = cosine[here, :], -sine[here, :]
            turned[here, :128] = turn(d_acc[here, :128], cos, sin).astype(LOW)
            turned[here, 128:256] = turn(d_acc[here, 128:256], cos, sin).astype(LOW)
            turned[here, 256:] = d_acc[here, 256:].astype(LOW)

            @pl.when(z != block)
            def send():
                rows_move(block, z).start()

            d_weight[...] += dot_tn(a1[here, :], turned[here, :])
            column_sums = column_sums + jnp.sum(
                turned[here, :].astype(WIDE), axis=0, keepdims=True
            )
            yield
        weight = wqkv[...].astype(WIDE)
        late[:, :OWN] = d_weight[...].astype(LOW)
        shift_grad = jnp.sum(weight * column_sums, axis=1, keepdims=True)
        whole = jnp.sum(weight * d_weight[...], axis=1, keepdims=True)
        columns = as_columns([a_gain[...], a_shift[...]])
        gain_grad = (whole - columns[:, 1:2] * shift_grad) * (1.0 / columns[:, 0:1])
        lanes = lanes_iota((WIDTH, 128))
        columns = jnp.where(lanes == 2, gain_grad, jnp.where(lanes == 3, shift_grad, late_columns))
        late[:, OWN:] = columns.astype(LOW)
        yield
        d_rows[:, pl.ds(pl.multiple_of(z * OWN, 128), OWN)] = turned[own, :]
        for step in range(1, 4):
            rows_move(z, lax.rem(z + step, 4)).wait_recv()
        ds[...] = dot_nt(d_rows[...], wall[...])
        for step in range(3):
            here = pl.ds(128 * step, 128)
            back, _ = norm_back(x[here, :].astype(WIDE), a_gain[...], ds[here, :])
            dh[here, :] = dh[here, :] + back
        writes.append(copies.local(dh, x_out))
        yield

    walk = steps()
    next(walk)
    loaded("early")
    for number in ORDER[1:]:
        if number < 0:
            next(walk)
        else:
            tick(number)
    copies.finish()
    for step in range(1, 4):
        rows_move(lax.rem(z + step, 4), z).wait_send()
    for move in writes:
        move.wait()


def back(operands, frequency, gains):
    def shape(*dims, kind=LOW):
        return (dims, kind)

    outs = [shape(OWN, WIDTH, kind=WIDE)] + [shape(*dims) for dims in STACK_SHAPES[:3]]
    outs.append(shape(4, WIDTH, WIDTH))
    scratch = [
        shape(OWN, WIDTH),
        shape(OWN, WIDTH, kind=WIDE),
        shape(OWN, WIDTH, kind=WIDE),
        shape(OWN, WIDTH),
        shape(OWN, HIDDEN),
        shape(OWN, HIDDEN),
        shape(OWN, WIDTH),
        shape(WIDTH, OWN),
        shape(WIDTH, WIDTH),
        shape(WIDTH, HIDDEN),
        shape(HIDDEN, WIDTH),
        shape(ROWS, WIDTH),
        shape(ROWS, 128),
        shape(ROWS, 128),
        shape(ROWS, 128),
        shape(ROWS, 128),
        shape(8, ROWS, kind=WIDE),
        shape(*STACK_SHAPES[0]),
        shape(*STACK_SHAPES[1]),
        shape(ROWS, 128, kind=WIDE),
        shape(ROWS, 128, kind=WIDE),
        shape(WIDTH, ROWS),
        shape(OWN, WIDTH),
        shape(OWN, HIDDEN),
        shape(OWN, WIDTH, kind=WIDE),
        shape(OWN, WIDTH),
        shape(ROWS, 128),
        shape(ROWS, OWN, kind=WIDE),
        shape(ROWS, OWN),
        shape(OWN, ROWS),
        shape(WIDTH, OWN, kind=WIDE),
        shape(*STACK_SHAPES[2]),
        shape(*STACK_SHAPES[3]),
    ]
    scratch += [shape(rows // 2, lanes) for rows, lanes in STACK_SHAPES]
    scratch += outs[1:]
    for stream in STREAMS:
        scratch += [shape(*dims) for dims in stream.landing_shapes(STACK_ROWS)]
    vmem = pl.BlockSpec(memory_space=VMEM)
    hbm = pl.BlockSpec(memory_space=pl.ANY)
    copy_count = 280
    return pl.pallas_call(
        back_kernel,
        out_shape=[jax.ShapeDtypeStruct(*out) for out in outs],
        in_specs=[hbm] * len(operands) + [vmem] * 4,
        out_specs=[hbm] * len(outs),
        scratch_shapes=[VMEM(*part) for part in scratch]
        + [pltpu.SemaphoreType.DMA((copy_count,)), pltpu.SemaphoreType.DMA((copy_count,))],
        compiler_params=pltpu.CompilerParams(
            collective_id=2, has_side_effects=True, vmem_limit_bytes=63 * 2**20
        ),
    )(*operands, frequency, *gains)


def unstack_kernel(*refs):
    stacks_hbm, passed_hbm, vectors = refs[:4], refs[4:6], refs[6:14]
    passed_out, outs_hbm = refs[14:16], refs[16:30]
    stacks, passed, wides, sems = refs[30:34], refs[34:36], refs[36:50], refs[50]
    loads = [
        pltpu.make_async_copy(source, target, sems.at[place])
        for place, (source, target) in enumerate(zip(stacks_hbm, stacks))
    ]
    for place in (2, 0, 1, 3):
        loads[place].start()
    passing = []
    for place in range(2):
        passing.append(
            pltpu.make_async_copy(passed_hbm[place], passed[place], sems.at[18 + place])
        )
        passing[place].start()
    early, coarse, middle, late = stacks
    (wq, wk, wv, wo, we, wc, wp, cq, ck, cv, co, ce, cc, wu) = wides
    writes = []

    def write(place):
        move = pltpu.make_async_copy(wides[place], outs_hbm[place], sems.at[4 + place])
        move.start()
        writes.append(move)

    loads[2].wait()
    for step in range(4):
        here = slice(512 * step, 512 * step + 512)
        wc[here, :] = middle[here, :512].astype(WIDE)
    write(5)
    for part in range(4):
        here = slice(512 * part, 512 * part + 512)
        we[:, here] = middle[here, 512:1024].astype(WIDE)
        wo[:, 128 * part : 128 * part + 128] = middle[here, 1024:].astype(WIDE)
    write(4)
    write(3)
    loads[0].wait()
    for number in range(6):
        for part in range(2):
            down, across = divmod(2 * number + part, 3)
            block = early[512 * down : 512 * down + 512, 256 * across : 256 * across + 256].astype(WIDE)
            inside = 256 * part
            if number < 3:
                wp[512 * number : 512 * number + 512, inside : inside + 256] = block
            else:
                start = 512 * (number - 3) + inside
                wu[:, start : start + 256] = block
        if number == 2:
            write(6)
    write(13)
    loads[1].wait()
    ce[...] = coarse[:, :512].astype(WIDE)
    write(11)
    cc[...] = coarse[:, 512:1024].astype(WIDE)
    write(12)
    for place, ref in enumerate((cq, ck, cv)):
        ref[...] = coarse[:, 1024 + 128 * place : 1152 + 128 * place].astype(WIDE)
        write(7 + place)
    for part in range(4):
        here = slice(128 * part, 128 * part + 128)
        co[:, here] = coarse[here, 1408:1536].astype(WIDE)
    write(10)
    loads[3].wait()
    for place, ref in enumerate((wq, wk, wv)):
        for group in range(4):
            ref[:, 128 * group : 128 * group + 128] = late[
                group, :, 128 * place : 128 * place + 128
            ].astype(WIDE)
        write(place)
    columns = sum(late[group, :, OWN:].astype(WIDE) for group in range(4))
    for place, row in enumerate(
        (jnp.transpose(columns), jnp.transpose(coarse[:, 1536:].astype(WIDE)))
    ):
        for line in range(4):
            vectors[4 * place + line][...] = row[line]
    for place in range(2):
        passing[place].wait()
        move = pltpu.make_async_copy(passed[place], passed_out[place], sems.at[20 + place])
        move.start()
        writes.append(move)
    for move in writes:
        move.wait()


def unstack(stacks, passed):
    shapes = (
        [(WIDTH, WIDTH)] * 4
        + [(WIDTH, HIDDEN), (HIDDEN, WIDTH), (ROWS, WIDTH)]
        + [(WIDTH, 128)] * 3
        + [(128, WIDTH), (WIDTH, WIDTH), (WIDTH, WIDTH), (WIDTH, ROWS)]
    )
    vmem = pl.BlockSpec(memory_space=VMEM)
    hbm = pl.BlockSpec(memory_space=pl.ANY)
    return pl.pallas_call(
        unstack_kernel,
        out_shape=[jax.ShapeDtypeStruct((WIDTH,), WIDE)] * 8
        + [jax.ShapeDtypeStruct(array.shape, array.dtype) for array in passed]
        + [jax.ShapeDtypeStruct(shape, WIDE) for shape in shapes],
        in_specs=[hbm] * 6,
        out_specs=[vmem] * 8 + [hbm] * (2 + len(shapes)),
        scratch_shapes=[VMEM(stack.shape, LOW) for stack in stacks]
        + [VMEM(array.shape, array.dtype) for array in passed]
        + [VMEM(shape, WIDE) for shape in shapes]
        + [pltpu.SemaphoreType.DMA((8 + len(shapes),))],
        compiler_params=pltpu.CompilerParams(vmem_limit_bytes=60 * 2**20),
    )(*stacks, *passed)


def body(
    inputs,
    lengths,
    cotangent,
    attention_gain,
    attention_shift,
    query_weight,
    key_weight,
    value_weight,
    output_weight,
    feedforward_gain,
    feedforward_shift,
    expand_weight,
    contract_weight,
    pooling_weight,
    coarse_gain,
    coarse_shift,
    coarse_query,
    coarse_key,
    coarse_value,
    coarse_output,
    widen_gain,
    widen_shift,
    coarse_expand,
    coarse_contract,
    upsample_weight,
):
    def row(vector):
        return vector.reshape(1, -1)

    frequency = jnp.asarray(frequency_row())
    square = (query_weight, key_weight, value_weight)
    (a1, q, k, v, o, level, o_own, h, a2, act, slope, wqkv, mixed, ds, early, coarse_stack) = front(
        lengths,
        inputs,
        cotangent,
        [
            row(vector)
            for vector in (
                attention_gain,
                attention_shift,
                feedforward_gain,
                feedforward_shift,
                coarse_gain,
                coarse_shift,
                widen_gain,
                widen_shift,
            )
        ],
        frequency,
        (*square, output_weight, expand_weight, contract_weight, pooling_weight, upsample_weight),
        (coarse_query, coarse_key, coarse_value, coarse_output, coarse_expand, coarse_contract),
    )
    input_grad, *stacks = back(
        (
            inputs,
            ds,
            h,
            a2,
            act,
            slope,
            o_own,
            wqkv,
            *square,
            output_weight,
            expand_weight,
            contract_weight,
            a1,
            q,
            k,
            v,
            o,
            level,
            early,
            coarse_stack,
        ),
        frequency,
        (
            row(attention_gain),
            row(attention_shift),
            row(feedforward_gain),
        ),
    )
    results = unstack(stacks, (mixed, input_grad))
    vectors, (mixed, input_grad) = results[:8], results[8:10]
    wq, wk, wv, wo, we, wc, wp, cq, ck, cv, co, ce, cc, wu = results[10:]
    return (
        mixed,
        input_grad,
        vectors[2],
        vectors[3],
        wq,
        wk,
        wv,
        wo,
        vectors[0],
        vectors[1],
        we,
        wc,
        wp,
        vectors[4],
        vectors[5],
        cq,
        ck,
        cv,
        co,
        vectors[6],
        vectors[7],
        ce,
        cc,
        wu,
    )


def solution(mesh):
    in_specs = (
        P(("seq", "head"), None),
        P("seq"),
        P(("seq", "head"), None),
        P(),
        P(),
        P(),
        P(),
        P(),
        P(),
        P(),
        P(),
        P(),
        P(),
        P(),
        P(),
        P(),
        P(None, "head"),
        P(None, "head"),
        P(None, "head"),
        P("head", None),
        P(),
        P(),
        P(None, "head"),
        P("head", None),
        P(),
    )
    out_specs = (
        P(("seq", "head"), None),
        P(("seq", "head"), None),
        P(),
        P(),
        P(),
        P(),
        P(),
        P(),
        P(),
        P(),
        P(),
        P(),
        P(),
        P(),
        P(),
        P(None, "head"),
        P(None, "head"),
        P(None, "head"),
        P("head", None),
        P(),
        P(),
        P(None, "head"),
        P("head", None),
        P(),
    )
    return jax.shard_map(body, mesh=mesh, in_specs=in_specs, out_specs=out_specs, check_vma=False)
```

```python
import functools
import math

import jax
import jax.numpy as jnp
import numpy as np
from jax import lax
from jax.experimental import pallas as pl
from jax.experimental.pallas import tpu as pltpu
from jax.sharding import PartitionSpec as P

MESH = pl.DeviceIdType.MESH
VMEM = pltpu.VMEM
LOW = jnp.bfloat16
WIDE = jnp.float32
EPSILON = 1e-05
OWN = 384
ROWS = 1536
WIDTH = 512
HIDDEN = 2048
SHORT = 528
PART = 144
SIZES = {"core": 2, "x": 4, "y": 4, "z": 4}


def my_coords():
    seq = lax.axis_index("seq")
    return {
        "core": lax.rem(seq, 2),
        "y": lax.rem(lax.div(seq, 2), 4),
        "x": lax.div(seq, 8),
        "z": lax.axis_index("head"),
    }


def moved(coords, axis, step):
    other = dict(coords)
    other[axis] = lax.rem(coords[axis] + step, SIZES[axis])
    return other


def device_of(coords):
    return {
        "seq": (coords["x"] * 4 + coords["y"]) * 2 + coords["core"],
        "head": coords["z"],
    }


def meet(coords, axes):
    barrier = pltpu.get_barrier_semaphore()
    count = 0
    for axis in axes:
        for step in range(1, SIZES[axis]):
            pl.semaphore_signal(
                barrier,
                inc=1,
                device_id=device_of(moved(coords, axis, step)),
                device_id_type=MESH,
            )
            count += 1
    pl.semaphore_wait(barrier, count)


def dot(left, right):
    return lax.dot_general(left, right, (((1,), (0,)), ((), ())), preferred_element_type=WIDE)


def dot_nt(left, right):
    return lax.dot_general(left, right, (((1,), (1,)), ((), ())), preferred_element_type=WIDE)


def dot_tn(left, right):
    return lax.dot_general(left, right, (((0,), (0,)), ((), ())), preferred_element_type=WIDE)


def lanes_iota(shape):
    return lax.broadcasted_iota(jnp.int32, shape, len(shape) - 1)


def rows_iota(shape):
    return lax.broadcasted_iota(jnp.int32, shape, 0)


def standard(values):
    centred = values - jnp.mean(values, axis=-1, keepdims=True)
    scale = lax.rsqrt(jnp.mean(centred * centred, axis=-1, keepdims=True) + EPSILON)
    return centred * scale, scale


def norm(values, gain, shift):
    return standard(values)[0] * gain + shift


def norm_back(values, gain, grad):
    unit, scale = standard(values)
    inner = grad * gain
    first = jnp.mean(inner, axis=-1, keepdims=True)
    second = jnp.mean(inner * unit, axis=-1, keepdims=True)
    return scale * (inner - first - unit * second), grad * unit


def turn(values, cosine, sine):
    lane = lanes_iota(values.shape)
    other = jnp.where(
        lax.rem(lane, 64) < 32, pltpu.roll(values, 96, 1), pltpu.roll(values, 32, 1)
    )
    return values * cosine + other * sine


def gelu_parts(values):
    half = 0.5 + 0.5 * lax.erf(values * math.sqrt(0.5))
    bell = jnp.exp(values * values * -0.5) * (1.0 / math.sqrt(2.0 * math.pi))
    return values * half, half + values * bell


def head_lanes(head, values):
    return jnp.where(lanes_iota(values.shape) // 64 == head, values, jnp.zeros_like(values))


def by_head(first, second):
    return jnp.where(lanes_iota(first.shape) < 64, first, second)


def head_rows(columns):
    shape = (8, 128)
    pick = (lanes_iota(shape) == rows_iota(shape) * 64).astype(WIDE)
    return lax.dot_general(
        pick,
        columns,
        (((1,), (1,)), ((), ())),
        precision=lax.Precision.HIGHEST,
        preferred_element_type=WIDE,
    )


def frequency_row():
    frequency = np.exp(np.arange(32, dtype=np.float32) * np.float32(-math.log(10000.0) / 32))
    return np.tile(frequency.astype(np.float32), 4)[None, :]


def fill_tables(frequency, cosine, sine):
    coarse = rows_iota((24, 128)).astype(WIDE) * 64.0 * frequency
    fine = rows_iota((64, 128)).astype(WIDE) * frequency
    sign = jnp.where(lax.rem(lanes_iota((64, 128)), 64) < 32, -1.0, 1.0)
    coarse_cos, coarse_sin = jnp.cos(coarse), jnp.sin(coarse)
    fine_cos, fine_sin = jnp.cos(fine), jnp.sin(fine)
    for place in range(24):
        one_cos, one_sin = coarse_cos[place : place + 1], coarse_sin[place : place + 1]
        here = pl.ds(64 * place, 64)
        cosine[here, :] = one_cos * fine_cos - one_sin * fine_sin
        sine[here, :] = (one_sin * fine_cos + one_cos * fine_sin) * sign


def as_columns(vectors):
    filler = jnp.zeros((128 - len(vectors), WIDTH), WIDE)
    return jnp.transpose(jnp.concatenate(vectors + [filler], axis=0))


class Copies:
    def __init__(self, send_sem, recv_sem):
        self.send_sem, self.recv_sem, self.count, self.sent = send_sem, recv_sem, 0, []

    def remote(self, source, target, other):
        place = self.count
        self.count += 1
        move = pltpu.make_async_remote_copy(
            src_ref=source,
            dst_ref=target,
            send_sem=self.send_sem.at[place],
            recv_sem=self.recv_sem.at[place],
            device_id=device_of(other),
            device_id_type=MESH,
        )
        move.start()
        self.sent.append(move)
        return move

    def local(self, source, target):
        place = self.count
        self.count += 1
        move = pltpu.make_async_copy(source, target, self.recv_sem.at[place])
        move.start()
        return move

    def finish(self):
        for move in self.sent:
            move.wait_send()


def pair_sums(columns):
    shape = (8, 128)
    pick = (lanes_iota(shape) // 64 == rows_iota(shape)).astype(WIDE)
    return lax.dot_general(
        pick,
        columns,
        (((1,), (1,)), ((), ())),
        precision=lax.Precision.HIGHEST,
        preferred_element_type=WIDE,
    )


def attend_tiles(items, before, width, offset):
    last, first = pl.ds(before, width), pl.ds(0, before)
    chains = [(item, head) for item in items for head in range(2)]
    queries = [head_lanes(head, item[0]) for item, head in chains]
    near = [dot_nt(query, item[1][last, item[3]]) for query, (item, _) in zip(queries, chains)]
    keep = [
        lanes_iota(near[0].shape) <= rows_iota(near[0].shape) + shift
        for shift in (offset if isinstance(offset, tuple) else (offset,) * len(items))
    ]
    near = [jnp.where(keep[place // 2], scores, -1e30) for place, scores in enumerate(near)]
    tops = [jnp.max(scores, axis=-1, keepdims=True) for scores in near]
    if before:
        far = [dot_nt(query, item[1][first, item[3]]) for query, (item, _) in zip(queries, chains)]
        tops = [jnp.maximum(t, jnp.max(s, axis=-1, keepdims=True)) for t, s in zip(tops, far)]
        far = [jnp.exp(scores - t) for scores, t in zip(far, tops)]
    near = [jnp.exp(scores - t) for scores, t in zip(near, tops)]
    totals = [jnp.sum(probs, axis=-1, keepdims=True) for probs in near]
    mixed = [dot(probs.astype(LOW), item[2][last, item[3]]) for probs, (item, _) in zip(near, chains)]
    if before:
        totals = [t + jnp.sum(probs, axis=-1, keepdims=True) for t, probs in zip(totals, far)]
        mixed = [
            m + dot(probs.astype(LOW), item[2][first, item[3]])
            for m, probs, (item, _) in zip(mixed, far, chains)
        ]
    outs = [m * (1.0 / t) for m, t in zip(mixed, totals)]
    levels = [t + jnp.log(total) for t, total in zip(tops, totals)]
    shape = (items[0][0].shape[0], 128)
    results = []
    for place in range(len(items)):
        a, b = 2 * place, 2 * place + 1
        level = by_head(jnp.broadcast_to(levels[a], shape), jnp.broadcast_to(levels[b], shape))
        results.append((by_head(outs[a], outs[b]), head_rows(level)))
    return results


def attend_back_blocks(items, offset):
    chains = [(item, head) for item in items for head in range(2)]
    queries = [head_lanes(head, item[0]) for item, head in chains]
    d_outs = [head_lanes(head, item[1]) for item, head in chains]
    scores = [dot_nt(item[2], query) for query, (item, _) in zip(queries, chains)]
    d_probs = [dot_nt(item[3], d_out) for d_out, (item, _) in zip(d_outs, chains)]
    probs = [
        jnp.exp(score - item[4][head : head + 1]) for score, (item, head) in zip(scores, chains)
    ]
    if offset is not None:
        keep = rows_iota(probs[0].shape) <= lanes_iota(probs[0].shape) + offset
        probs = [jnp.where(keep, prob, 0.0) for prob in probs]
    d_scores = [
        (prob * (d_prob - item[5][head : head + 1])).astype(LOW)
        for prob, d_prob, (item, head) in zip(probs, d_probs, chains)
    ]
    d_values = [dot(prob.astype(LOW), d_out) for prob, d_out in zip(probs, d_outs)]
    d_keys = [dot(d_score, query) for d_score, query in zip(d_scores, queries)]
    d_queries = [dot_tn(d_score, item[2]) for d_score, (item, _) in zip(d_scores, chains)]
    return [
        (
            by_head(d_queries[i], d_queries[i + 1]) * 0.125,
            d_keys[i] + d_keys[i + 1],
            d_values[i] + d_values[i + 1],
        )
        for i in range(0, len(chains), 2)
    ]


COARSE_STACK = (WIDTH, 1664)
COARSE_TILES = ((0, 256, 256), (256, 256, 256), (512, 16, 128))


def front_kernel(*refs):
    (lengths, x, cot, a_gain, a_shift, f_gain, f_shift, c_gain, c_shift, w_gain, w_shift) = refs[:11]
    (frequency, wq_hbm, wk_hbm, wv_hbm, wo_hbm, we_hbm, wc_hbm, wp_hbm, wu_hbm) = refs[11:20]
    shards = refs[20:26]
    out_refs = refs[26:42]
    (a1, q, k, v, o, level, o_own, h, a2, act, slope, wqkv, mixed, ds, early, stack) = refs[42:58]
    (wo, we, wc, wp, wu, cosine, sine, landing, thin, s, m, c0g, dcg, fqkv, fo, fe, fc) = refs[58:75]
    (c0, c1, b1, b2, dr, cq, ck, cv, co, clevel, d_out, c_act, d_pre, total, top, d_pair, d_three,
     kept_act, kept_pre, send_sem, recv_sem) = refs[75:]
    saved = {}

    def save(key, source, part=None, place=None):
        target = out_refs[key if place is None else place]
        saved[key] = copies.local(source, target if part is None else target.at[part])

    coords = my_coords()
    z = coords["z"]
    core = coords["core"]
    right, left, far = (moved(coords, "z", step) for step in (1, 3, 2))
    copies = Copies(send_sem, recv_sem)
    lane = pl.ds(pl.multiple_of(z * 128, 128), 128)
    first_loads = [
        copies.local(weight.at[:, lane], wqkv.at[:, pl.ds(128 * place, 128)])
        for place, weight in enumerate((wq_hbm, wk_hbm, wv_hbm))
    ]
    loads = [
        copies.local(source, target)
        for source, target in ((wu_hbm, wu), (wo_hbm, wo), (we_hbm, we), (wc_hbm, wc), (wp_hbm, wp))
    ]
    own_weights = [
        copies.local(shard, full)
        for shard, full in zip(
            shards,
            [fqkv.at[z, :, pl.ds(128 * place, 128)] for place in range(3)]
            + [fo.at[z], fe.at[z], fc.at[z]],
        )
    ]
    meet(coords, ("core", "x", "y", "z"))
    low, high = pl.ds(0, OWN // 2), pl.ds(OWN // 2, OWN // 2)
    to_right = copies.remote(x.at[low], landing.at[0, low], right)
    to_left = copies.remote(x.at[high], landing.at[1, high], left)
    to_right_more = copies.remote(x.at[high], landing.at[0, high], right)
    to_left_more = copies.remote(x.at[low], landing.at[1, low], left)

    def project(block, index):
        start = pl.multiple_of(index * OWN, OWN)

        def rows_of(step, carry):
            here = pl.multiple_of(step * 128, 128)
            there = pl.ds(pl.multiple_of(start + here, 128), 128)
            values = block[pl.ds(here, 128), :].astype(WIDE)
            a1[there, :] = norm(values, a_gain[...], a_shift[...]).astype(LOW)
            return carry

        lax.fori_loop(0, OWN // 128, rows_of, 0)
        here = pl.ds(start, OWN)
        both = dot(a1[here, :], wqkv[...])
        cos, sin = cosine[here, :], sine[here, :]
        q[here, :] = (turn(both[:, :128], cos, sin) * 0.125).astype(LOW)
        k[here, :] = turn(both[:, 128:256], cos, sin).astype(LOW)
        v[here, :] = both[:, 256:].astype(LOW)

    fill_tables(frequency[...], cosine, sine)
    for load in first_loads:
        load.wait()
    project(x, z)
    to_right.wait_recv()
    far_right = copies.remote(landing.at[0, low], landing.at[2, low], right)
    to_left.wait_recv()
    far_left = copies.remote(landing.at[1, high], landing.at[2, high], left)

    valid = (rows_iota((OWN, 128)) + z * OWN < lengths[0]).astype(WIDE)
    for part in range(4):
        thin[part, pl.ds(0, 8), :] = jnp.zeros((8, 128), WIDE)
        thin[part, pl.ds(392, 48), :] = jnp.zeros((48, 128), WIDE)
        thin[part, pl.ds(8, OWN), :] = cot[:, 128 * part : 128 * part + 128].astype(WIDE) * valid

    def every_third(first, count):
        pieces = [thin[part, pl.ds(first, count, 3), :].astype(LOW) for part in range(4)]
        return jnp.concatenate(pieces, axis=1)

    loads[0].wait()
    lifted_back = sum(
        dot_nt(every_third(8 + r, 128), wu[:, 512 * r : 512 * r + 512]) for r in range(3)
    )
    dcg[z] = lifted_back.astype(LOW)

    to_right_more.wait_recv()
    project(landing.at[0], left["z"])
    to_left_more.wait_recv()
    project(landing.at[1], right["z"])
    far_right.wait_recv()
    far_left.wait_recv()
    project(landing.at[2], far["z"])

    for load in own_weights:
        load.wait()
    z_others = (right, left, far)
    z_sources = (left, right, far)
    pieces = {}
    def first_pieces(place, full):
        for way, axis in enumerate(("x", "y")):
            rows = pl.ds(pl.multiple_of(core * 256 + way * 128 + coords[axis] * 32, 32), 32)
            for step, other in enumerate(z_others):
                pieces[place, way, step] = copies.remote(full.at[z, rows], full.at[z, rows], other)
    first_pieces(0, fqkv)
    fo_rows = pl.ds(pl.multiple_of(core * 64, 64), 64)
    fo_moves = [copies.remote(fo.at[z, fo_rows], fo.at[z, fo_rows], other) for other in z_others]

    sent_blocks = send_sem.shape[0] - 4
    got_blocks = recv_sem.shape[0] - 4

    def block_move(target, source):
        return pltpu.make_async_remote_copy(
            src_ref=o.at[pl.ds(pl.multiple_of(target * OWN, OWN), OWN), :],
            dst_ref=o_own.at[:, pl.ds(pl.multiple_of(source * 128, 128), 128)],
            send_sem=send_sem.at[sent_blocks + target],
            recv_sem=recv_sem.at[got_blocks + source],
            device_id=device_of({**coords, "z": target}),
            device_id_type=MESH,
        )

    everything = pl.ds(0, 128)
    for block in reversed(range(4)):
        tiles = [pl.ds(OWN * block + 128 * step, 128) for step in range(3)]
        results = attend_tiles(
            [(q[here, :], k, v, everything) for here in tiles], OWN * block, OWN, (0, 128, 256)
        )
        for here, (mixed_tile, tops) in zip(tiles, results):
            o[here, :] = mixed_tile.astype(LOW)
            level[:, here] = tops

        @pl.when(z != block)
        def send():
            block_move(block, z).start()

        if block == 2:
            first_pieces(1, fe)
            first_pieces(2, fc)

    for place, ref in ((0, a1), (1, q), (2, k), (3, v), (4, o), (5, level), (11, wqkv)):
        save(place, ref)
    o_own[:, lane] = o[pl.ds(pl.multiple_of(z * OWN, OWN), OWN), :]

    spread, swaps = {0: [], 1: [], 2: []}, {0: [], 1: [], 2: []}
    whole = (fqkv, fe, fc)
    sibling = moved(coords, "core", 1)

    def spread_out(place):
        for way, axis in enumerate(("x", "y")):
            rows = pl.ds(pl.multiple_of(core * 256 + way * 128 + coords[axis] * 32, 32), 32)
            for step, source in enumerate(z_sources):
                pieces[place, way, step].wait_recv()
                part = whole[place].at[source["z"], rows]
                for far_step in range(1, 4):
                    spread[place].append(copies.remote(part, part, moved(coords, axis, far_step)))

    def swap(place):
        for move in spread[place]:
            move.wait_recv()
        half = pl.ds(pl.multiple_of(core * 256, 256), 256)
        for source in z_sources:
            part = whole[place].at[source["z"], half]
            swaps[place].append(copies.remote(part, part, sibling))

    spread_out(0)
    for step in range(1, 4):
        other = lax.rem(z + step, 4)
        block_move(z, other).wait_recv()
    dc_moves = [copies.remote(dcg.at[z], dcg.at[z], other) for other in z_others]
    save(6, o_own)

    for load in loads[1:]:
        load.wait()

    def mix(step, carry):
        here = pl.ds(pl.multiple_of(step * 128, 128), 128)
        hidden = x[here, :].astype(WIDE) + dot(o_own[here, :], wo[...])
        h[here, :] = hidden
        a2[here, :] = norm(hidden, f_gain[...], f_shift[...]).astype(LOW)
        return carry

    lax.fori_loop(0, 3, mix, 0)

    def widen(step, carry):
        here = pl.ds(pl.multiple_of(step * 256, 256), 256)
        value, back = gelu_parts(dot(a2[...], we[:, here]))
        act[:, here] = value.astype(LOW)
        slope[:, here] = back.astype(LOW)
        return carry

    lax.fori_loop(0, HIDDEN // 256, widen, 0)
    spread_out(1)
    spread_out(2)
    for place, ref in ((7, h), (8, a2), (9, act), (10, slope)):
        save(place, ref)

    for part in range(4):
        here = slice(128 * part, 128 * part + 128)
        if part % 2 == 0:
            wide = slice(256 * (part // 2), 256 * (part // 2) + 256)
            summed = h[:, wide] + dot(act[...], wc[:, wide])
            s[:, wide] = summed
        kept = (s[:, here] * valid).astype(LOW)
        m[:, here] = kept
        thin[part, pl.ds(8, OWN), :] = kept.astype(WIDE)
    pooled = sum(
        dot(every_third(6 + r, PART), wp[512 * r : 512 * r + 512, :]) for r in range(3)
    )
    c0g[z] = pooled.astype(LOW)
    c0_moves = [copies.remote(c0g.at[z], c0g.at[z], other) for other in z_others]
    fo_swaps = []
    for step, source in enumerate(z_sources):
        fo_moves[step].wait_recv()
        part = fo.at[source["z"], fo_rows]
        fo_swaps.append(copies.remote(part, part, sibling))
    swap(0)
    for move in c0_moves:
        move.wait_recv()

    own_lane = pl.ds(pl.multiple_of(z * 128, 128), 128)
    own_rows = pl.ds(pl.multiple_of(z * 128, 128), 128)

    def row_chunks(body):
        def run(step, carry):
            body(pl.ds(pl.multiple_of(step * 176, 16), 176))
            return carry

        lax.fori_loop(0, 3, run, 0)

    for part in range(4):
        base = 128 * part
        c0[pl.ds(base, 128), :] = c0g[part, pl.ds(0, 128), :].astype(WIDE)
        if part:
            first = pl.ds(base, 1)
            c0[first, :] = c0[first, :] + c0g[part - 1, pl.ds(128, 16), :].astype(WIDE)[:1]
    c0[pl.ds(512, 16), :] = c0g[3, pl.ds(128, 16), :].astype(WIDE)

    def first_norm(here):
        b1[here, :] = norm(c0[here, :], c_gain[...], c_shift[...]).astype(LOW)

    row_chunks(first_norm)
    for move in swaps[0]:
        move.wait_recv()
    for ref in (cq, ck, cv):
        ref[pl.ds(SHORT, 640 - SHORT), :] = jnp.zeros((640 - SHORT, WIDTH), LOW)

    for pair in range(4):
        lane = pl.ds(pair * 128, 128)
        both = dot(b1[...], fqkv[pair])
        cos, sin = cosine[pl.ds(0, SHORT), :], sine[pl.ds(0, SHORT), :]
        rows = pl.ds(0, SHORT)
        cq[rows, lane] = (turn(both[:, :128], cos, sin) * 0.125).astype(LOW)
        ck[rows, lane] = turn(both[:, 128:256], cos, sin).astype(LOW)
        cv[rows, lane] = both[:, 256:].astype(LOW)
    for first, count, width in COARSE_TILES:
        here = pl.ds(first, count)
        for pair, (mixed_tile, tops) in enumerate(
            attend_tiles([(cq[here, pl.ds(128 * p, 128)], ck, cv, pl.ds(128 * p, 128)) for p in range(4)], first, width, 0)
        ):
            co[here, pl.ds(128 * pair, 128)] = mixed_tile.astype(LOW)
            clevel[pair, :, here] = tops

    swap(1)
    swap(2)
    for move in dc_moves + fo_swaps:
        move.wait_recv()
    for part in range(4):
        dr[pl.ds(128 * part, 128), :] = dcg[part]
    dr[pl.ds(512, 16), :] = jnp.zeros((16, WIDTH), LOW)

    def second_norm(here):
        value = c0[here, :]
        for part in range(4):
            value = value + dot(co[here, 128 * part : 128 * part + 128], fo[part])
        c1[here, :] = value
        b2[here, :] = norm(value, w_gain[...], w_shift[...]).astype(LOW)

    row_chunks(second_norm)
    for move in swaps[1] + swaps[2]:
        move.wait_recv()
    total[...] = jnp.zeros_like(total)
    top[...] = c1[own_rows, :]

    def widen(act_ref, back_ref, step, carry):
        slot = lax.rem(z + step, 4)
        halves = (pl.ds(0, 256), pl.ds(256, 256))
        ahead = [dot(b2[...], fe[slot, :, lane]) for lane in halves]
        behind = [dot_nt(dr[...], fc[slot, lane, :]) for lane in halves]
        for lane, values, grads in zip(halves, ahead, behind):
            value, slope = gelu_parts(values)
            act_ref[:, lane] = value.astype(LOW)
            back_ref[:, lane] = (slope * grads).astype(LOW)
        top[...] += dot(act_ref[own_rows, :], fc[slot])
        total[...] += dot_nt(back_ref[...], fe[slot])
        return carry

    widen(kept_act, kept_pre, 0, 0)
    lax.fori_loop(1, 4, functools.partial(widen, c_act, d_pre), 0)

    def put_early(number, grad):
        for part in range(2):
            down, across = divmod(2 * number + part, 3)
            early[512 * down : 512 * down + 512, 256 * across : 256 * across + 256] = grad[
                :, 256 * part : 256 * part + 256
            ].astype(LOW)

    crest = top[...].astype(LOW)
    for r in range(3):
        lifted = dot(crest, wu[:, 512 * r : 512 * r + 512])
        for part in range(4):
            thin[part, pl.ds(8 + r, 128, 3), :] = lifted[:, 128 * part : 128 * part + 128]
    for part in range(4):
        lane = slice(128 * part, 128 * part + 128)
        mixed[:, lane] = (valid * (s[:, lane] + thin[part, pl.ds(8, OWN), :])).astype(LOW)
        thin[part, pl.ds(8, OWN), :] = cot[:, lane].astype(WIDE) * valid

    for r in range(3):
        put_early(3 + r, dot_tn(crest, every_third(8 + r, 128)))

    save(12, mixed)
    save(16, early.at[pl.ds(1024, 1024)], (pl.ds(1024, 1024),), 14)
    stack[:, :512] = dot_tn(b2[...], kept_pre[...]).astype(LOW)
    stack[:, 512:1024] = dot_tn(kept_act[...], dr[...]).astype(LOW)
    sums = [jnp.zeros((1, WIDTH), WIDE) for _ in range(4)]
    for step in range(3):
        here = pl.ds(176 * step, 176)
        grad = total[here, :]
        back, unit_grad = norm_back(c1[here, :], w_gain[...], grad)
        sums[2] = sums[2] + jnp.sum(unit_grad, axis=0, keepdims=True)
        sums[3] = sums[3] + jnp.sum(grad, axis=0, keepdims=True)
        back = dr[here, :].astype(WIDE) + back
        c1[here, :] = back
        b2[here, :] = back.astype(LOW)
    output_grad = dot_tn(co[:, own_lane], b2[...]).astype(LOW)
    for part in range(4):
        stack[128 * part : 128 * part + 128, 1408:1536] = output_grad[:, 128 * part : 128 * part + 128]
    for pair in range(4):
        d_out[:, pl.ds(128 * pair, 128)] = dot_nt(b2[...], fo[pair]).astype(LOW)
    lanes = [pl.ds(128 * pair, 128) for pair in range(4)]
    deltas = [
        pair_sums(d_out[:, lane].astype(WIDE) * co[:, lane].astype(WIDE)) for lane in lanes
    ]
    for first, count, width in COARSE_TILES:
        here = pl.ds(first, count)
        near, past = pl.ds(first, width), pl.ds(0, first)

        def items(there):
            return [
                (
                    cq[here, lane],
                    d_out[here, lane],
                    ck[there, lane],
                    cv[there, lane],
                    clevel[pair, :, here],
                    deltas[pair][:, first : first + count],
                )
                for pair, lane in enumerate(lanes)
            ]

        results = attend_back_blocks(items(near), 0)
        for pair, (d_q, d_k, d_v) in enumerate(results):
            d_pair[pair, here, :128] = d_q
            d_pair[pair, near, 128:256] = d_k
            d_pair[pair, near, 256:] = d_v
        if first:
            results = attend_back_blocks(items(past), None)
            for pair, (d_q, d_k, d_v) in enumerate(results):
                d_pair[pair, here, :128] += d_q
                d_pair[pair, past, 128:256] += d_k
                d_pair[pair, past, 256:] += d_v
    for pair in range(4):
        cos, sin = cosine[pl.ds(0, SHORT), :], -sine[pl.ds(0, SHORT), :]
        rows = pl.ds(0, SHORT)
        d_three[pair, :, :128] = turn(d_pair[pair, rows, :128], cos, sin).astype(LOW)
        d_three[pair, :, 128:256] = turn(d_pair[pair, rows, 128:256], cos, sin).astype(LOW)
        d_three[pair, :, 256:] = d_pair[pair, rows, 256:].astype(LOW)
    total[...] = sum(dot_nt(d_three[pair], fqkv[pair]) for pair in range(4))
    stack[:, 1024:1408] = dot_tn(b1[...], d_three[z]).astype(LOW)

    for step in range(3):
        here = pl.ds(176 * step, 176)
        grad = total[here, :]
        back, unit_grad = norm_back(c0[here, :], c_gain[...], grad)
        sums[0] = sums[0] + jnp.sum(unit_grad, axis=0, keepdims=True)
        sums[1] = sums[1] + jnp.sum(grad, axis=0, keepdims=True)
        b1[here, :] = (c1[here, :] + back).astype(LOW)
    stack[:, 1536:] = as_columns(sums).astype(LOW)

    save(15, stack)
    down = b1[pl.ds(pl.multiple_of(z * 128, 128), PART), :]
    for part in range(4):
        lane = slice(128 * part, 128 * part + 128)
        thin[part, pl.ds(0, 8), :] = jnp.zeros((8, 128), WIDE)
        thin[part, pl.ds(392, 48), :] = jnp.zeros((48, 128), WIDE)
        thin[part, pl.ds(8, OWN), :] = m[:, lane].astype(WIDE)
    for r in range(3):
        put_early(r, dot_tn(every_third(6 + r, PART), down))
    for r in range(3):
        back = dot_nt(down, wp[512 * r : 512 * r + 512, :])
        for part in range(4):
            thin[part, pl.ds(6 + r, PART, 3), :] = back[:, 128 * part : 128 * part + 128]
    for part in range(4):
        lane = slice(128 * part, 128 * part + 128)
        ds[:, lane] = valid * (cot[:, lane].astype(WIDE) + thin[part, pl.ds(8, OWN), :])
    save(13, ds)
    save(14, early.at[pl.ds(0, 1024)], (pl.ds(0, 1024),))
    copies.finish()
    for step in range(1, 4):
        block_move(lax.rem(z + step, 4), z).wait_send()
    for move in saved.values():
        move.wait()


def front(lengths, x, cot, gains, frequency, weights, shards):
    def shape(*dims, kind=LOW):
        return (dims, kind)

    outs = [
        shape(ROWS, WIDTH),
        shape(ROWS, 128),
        shape(ROWS, 128),
        shape(ROWS, 128),
        shape(ROWS, 128),
        shape(8, ROWS, kind=WIDE),
        shape(OWN, WIDTH),
        shape(OWN, WIDTH, kind=WIDE),
        shape(OWN, WIDTH),
        shape(OWN, HIDDEN),
        shape(OWN, HIDDEN),
        shape(WIDTH, OWN),
        shape(OWN, WIDTH),
        shape(OWN, WIDTH, kind=WIDE),
        shape(HIDDEN, 768),
        shape(*COARSE_STACK),
    ]
    scratch = [
        shape(WIDTH, WIDTH),
        shape(WIDTH, HIDDEN),
        shape(HIDDEN, WIDTH),
        shape(ROWS, WIDTH),
        shape(WIDTH, ROWS),
        shape(ROWS, 128, kind=WIDE),
        shape(ROWS, 128, kind=WIDE),
        shape(3, OWN, WIDTH),
        shape(4, 440, 128, kind=WIDE),
        shape(OWN, WIDTH, kind=WIDE),
        shape(OWN, WIDTH),
        shape(4, PART, WIDTH),
        shape(4, 128, WIDTH),
        shape(4, WIDTH, OWN),
        shape(4, 128, WIDTH),
        shape(4, WIDTH, WIDTH),
        shape(4, WIDTH, WIDTH),
        shape(SHORT, WIDTH, kind=WIDE),
        shape(SHORT, WIDTH, kind=WIDE),
        shape(SHORT, WIDTH),
        shape(SHORT, WIDTH),
        shape(SHORT, WIDTH),
        shape(640, WIDTH),
        shape(640, WIDTH),
        shape(640, WIDTH),
        shape(SHORT, WIDTH),
        shape(4, 8, 640, kind=WIDE),
        shape(SHORT, WIDTH),
        shape(SHORT, WIDTH),
        shape(SHORT, WIDTH),
        shape(SHORT, WIDTH, kind=WIDE),
        shape(128, WIDTH, kind=WIDE),
        shape(4, 640, OWN, kind=WIDE),
        shape(4, SHORT, OWN),
        shape(SHORT, WIDTH),
        shape(SHORT, WIDTH),
    ]
    vmem = pl.BlockSpec(memory_space=VMEM)
    hbm = pl.BlockSpec(memory_space=pl.ANY)
    copy_count = 160
    return pl.pallas_call(
        front_kernel,
        out_shape=[jax.ShapeDtypeStruct(*out) for out in outs],
        in_specs=[pl.BlockSpec(memory_space=pltpu.SMEM)] + [vmem] * 11 + [hbm] * 14,
        out_specs=[hbm] * len(outs),
        scratch_shapes=[VMEM(*out) for out in outs + scratch]
        + [pltpu.SemaphoreType.DMA((copy_count,)), pltpu.SemaphoreType.DMA((copy_count,))],
        compiler_params=pltpu.CompilerParams(
            collective_id=1, has_side_effects=True, vmem_limit_bytes=60 * 2**20
        ),
    )(lengths, x, cot, *gains, frequency, *weights, *shards)


class Stream:
    def __init__(self, stack, low, high, axes, spread=False):
        self.stack, self.lanes = stack, pl.ds(low, high - low)
        self.axes = axes
        self.levels = (*axes, "z") if spread else axes
        self.spread = spread

    def landing_shapes(self, row_counts):
        rows = row_counts[self.stack] // 2
        shapes = []
        for axis in self.axes[1:]:
            rows = rows // SIZES[axis]
            shapes.append((3, rows, self.lanes.size))
        return shapes


STREAMS = (
    Stream(0, 0, 384, ("core", "z", "y", "x")),
    Stream(0, 384, 768, ("core", "x", "z", "y")),
    Stream(1, 0, 768, ("core", "x", "y")),
    Stream(1, 768, 1664, ("core", "y", "x")),
    Stream(2, 0, 384, ("core", "y", "x", "z")),
    Stream(2, 384, 768, ("core", "z", "x", "y")),
    Stream(2, 768, 1024, ("core", "y", "x", "z")),
    Stream(2, 1024, 1152, ("core", "z", "x", "y")),
    Stream(3, 0, 256, ("core", "x", "y"), True),
    Stream(3, 256, 512, ("core", "x", "y"), True),
)
STACK_SHAPES = ((HIDDEN, 768), COARSE_STACK, (HIDDEN, 1152), (WIDTH, WIDTH))
STACK_ROWS = tuple(shape[0] for shape in STACK_SHAPES)
ORDER = (
    -1, 0, 1, 2, 3, -1, -1, -1, -1, 0, 1, 2, 3, -1, -1, -1, -1, 4, 5, 6, -1, -1, 7, 4, 5, 6, 7, 3, 0, 1, -1,
    -1, 2, -1, 3, -1, -1, -1, 4, -1, -1, -1, 3, -1, 5, -1, 6, -1, 7, 4, -1, 0, -1, 1, 2, -1, 9, 8, 5, 9, 8, 6,
    7, 0, 3, 1, 2, 5, 3, 7, 9, 4, 8, 1, 0, 5, 7, 6, 9, 4, 8, 2, 1, 0, 2, 6, 9, 5, -1, 7, 8, 4, 9, 8, 1, 0, 6,
    1, 0, 4, 9, 4, 5, 9, 6, 5, 7, 8, 6, 7, 8,
)


ROWS_AT_ONCE = {128: 256, 256: 128, 384: 64, 512: 64, 640: 32, 768: 32, 896: 32, 1024: 32}


class Summing:
    def __init__(self, stream, source, total, out, landings, copies, coords):
        self.stream, self.source, self.total, self.out = stream, source, total, out
        self.landings, self.copies, self.coords = landings, copies, coords
        self.pending = []
        self.tick_count = 0

    def rows_at(self, level, who, whole):
        rows = STACK_ROWS[self.stream.stack]
        start = 0
        for axis in self.stream.axes[:level]:
            rows = rows // SIZES[axis]
            if whole or axis != "core":
                start = start + who[axis] * rows
        return pl.ds(pl.multiple_of(start, 16), rows)

    def start_down(self, level):
        axis = self.stream.axes[level]
        lanes = self.stream.lanes
        self.pending = []
        for step in range(1, SIZES[axis]):
            other = moved(self.coords, axis, step)
            where = self.rows_at(level + 1, other, level == 0)
            if level == 0:
                source = self.source.at[where, lanes]
                target = self.total.at[pl.ds(0, where.size), lanes]
            else:
                source = self.total.at[where, lanes]
                target = self.landings[level - 1].at[step - 1]
            self.pending.append(self.copies.remote(source, target, other))

    def add_down(self, level):
        lanes = self.stream.lanes
        for move in self.pending:
            move.wait_recv()
        here = self.rows_at(level + 1, self.coords, False)
        mine = self.rows_at(1, self.coords, True)
        step_rows = min(here.size, ROWS_AT_ONCE[lanes.size])

        def add(index, carry):
            at = pl.multiple_of(index * step_rows, 16)
            part = pl.ds(pl.multiple_of(here.start + at, 16), step_rows)
            value = self.total[part, lanes].astype(WIDE)
            if level == 0:
                own = pl.ds(pl.multiple_of(mine.start + at, 16), step_rows)
                value = value + self.source[own, lanes].astype(WIDE)
            else:
                for slot in range(3):
                    landed = self.landings[level - 1][slot, pl.ds(at, step_rows), :]
                    value = value + landed.astype(WIDE)
            self.total[part, lanes] = value.astype(LOW)
            return carry

        lax.fori_loop(0, here.size // step_rows, add, 0)

    def start_up(self, level):
        axes = self.stream.axes
        where = self.rows_at(min(level + 1, len(axes)), self.coords, True)
        if level == len(axes):
            part = self.out.at[self.coords["z"], where, self.stream.lanes]
        elif self.stream.spread:
            part = self.out.at[pl.ds(0, 4), where, self.stream.lanes]
        else:
            part = self.out.at[where, self.stream.lanes]
        axis = self.stream.levels[level]
        self.pending = [
            self.copies.remote(part, part, moved(self.coords, axis, step))
            for step in range(1, SIZES[axis])
        ]

    def tick(self):
        now = self.tick_count
        self.tick_count += 1
        down, depth = len(self.stream.axes), len(self.stream.levels)
        if now < down:
            if now:
                self.add_down(now - 1)
            self.start_down(now)
        elif now == down:
            self.add_down(down - 1)
            last = self.rows_at(down, self.coords, True)
            value = self.total[self.rows_at(down, self.coords, False), self.stream.lanes]
            if self.stream.spread:
                self.out[self.coords["z"], last, self.stream.lanes] = value
            else:
                self.out[last, self.stream.lanes] = value
            self.start_up(depth - 1)
        elif now <= down + depth:
            for move in self.pending:
                move.wait_recv()
            if now < down + depth:
                self.start_up(depth - 1 - (now - down))

    def done(self):
        return self.tick_count > len(self.stream.axes) + len(self.stream.levels)


def back_kernel(*refs):
    (x_hbm, ds_hbm, h_hbm, a2_hbm, act_hbm, slope_hbm, o_own_hbm, wqkv_hbm, wq_hbm, wk_hbm, wv_hbm,
     wo_hbm, we_hbm, wc_hbm, a1_hbm, q_hbm, k_hbm, v_hbm, o_hbm, level_hbm, early_hbm,
     coarse_hbm) = refs[:22]
    (frequency, a_gain, a_shift, f_gain) = refs[22:26]
    x_out, *total_outs = refs[26:31]
    (x, ds, h, a2, act, slope, o_own, wqkv, wo, we, wc, a1, q, k, v, o, level, early, coarse, cosine,
     sine, wall, low, d_pre, dh, d_own, d_heads, d_acc, turned, d_rows, d_weight, middle, late) = refs[31:64]
    totals, outs = refs[64:68], refs[68:72]
    *landings, send_sem, recv_sem = refs[72:]
    coords = my_coords()
    z = coords["z"]
    others = [moved(coords, "z", step) for step in (1, 3, 2)]
    copies = Copies(send_sem, recv_sem)
    lane = pl.ds(pl.multiple_of(z * 128, 128), 128)
    own = pl.ds(pl.multiple_of(z * OWN, OWN), OWN)
    loads, writes = {}, []

    def load(name, *pairs):
        loads[name] = [copies.local(source, target) for source, target in pairs]

    def loaded(name):
        for move in loads.pop(name):
            move.wait()

    load("first", (ds_hbm, ds), (wc_hbm, wc), (slope_hbm, slope), (act_hbm, act), (a2_hbm, a2))
    load("early", (early_hbm, early), (coarse_hbm, coarse))
    meet(coords, ("core", "x", "y", "z"))

    sources = (early, coarse, middle, late)
    streams = []
    for stream in STREAMS:
        count = len(stream.axes) - 1
        streams.append(
            Summing(
                stream,
                sources[stream.stack],
                totals[stream.stack],
                outs[stream.stack],
                landings[:count],
                copies,
                coords,
            )
        )
        landings = landings[count:]

    def tick(number):
        streams[number].tick()
        if streams[number].done():
            stack, lanes = streams[number].stream.stack, streams[number].stream.lanes
            part = (slice(None),) * (len(outs[stack].shape) - 1) + (lanes,)
            writes.append(copies.local(outs[stack].at[part], total_outs[stack].at[part]))

    def widen_back(index):
        here = pl.ds(256 * index, 256)
        back = (slope[:, here].astype(WIDE) * dot_nt(low[...], wc[here, :])).astype(LOW)
        d_pre[:, here] = back
        middle[here, :512] = dot_tn(act[:, here], low[...]).astype(LOW)
        down = pl.ds(512 * (index // 2), 512)
        across = pl.ds(512 + 256 * (index % 2), 256)
        middle[down, across] = dot_tn(a2[...], back).astype(LOW)

    sent_blocks = send_sem.shape[0] - 4
    got_blocks = recv_sem.shape[0] - 4

    def rows_move(target, source):
        return pltpu.make_async_remote_copy(
            src_ref=turned.at[pl.ds(pl.multiple_of(target * OWN, OWN), OWN), :],
            dst_ref=d_rows.at[:, pl.ds(pl.multiple_of(source * OWN, 128), OWN)],
            send_sem=send_sem.at[sent_blocks + target],
            recv_sem=recv_sem.at[got_blocks + source],
            device_id=device_of({**coords, "z": target}),
            device_id_type=MESH,
        )

    def steps():
        loaded("first")
        low[...] = ds[...].astype(LOW)
        load("second", (we_hbm, we), (h_hbm, h), (wo_hbm, wo), (o_own_hbm, o_own))
        yield
        for index in range(8):
            widen_back(index)
            yield
        load(
            "third",
            (q_hbm, q),
            (k_hbm, k),
            (v_hbm, v),
            (o_hbm, o),
            (level_hbm, level),
            (a1_hbm, a1),
            (wqkv_hbm, wqkv),
            (x_hbm, x),
            *(
                (
                    weight.at[:, pl.ds(128 * group, 128)],
                    wall.at[:, pl.ds(OWN * group + 128 * place, 128)],
                )
                for group in range(4)
                for place, weight in enumerate((wq_hbm, wk_hbm, wv_hbm))
            ),
        )
        loaded("second")
        for part in range(2):
            here = slice(256 * part, 256 * part + 256)
            dh[:, here] = dot_nt(d_pre[...], we[here, :])
        sums = [jnp.zeros((1, WIDTH), WIDE) for _ in range(2)]
        for step in range(3):
            here = pl.ds(128 * step, 128)
            grad = dh[here, :]
            back, unit_grad = norm_back(h[here, :], f_gain[...], grad)
            sums[0] = sums[0] + jnp.sum(unit_grad, axis=0, keepdims=True)
            sums[1] = sums[1] + jnp.sum(grad, axis=0, keepdims=True)
            back = ds[here, :] + back
            dh[here, :] = back
            low[here, :] = back.astype(LOW)
        d_own[...] = dot_nt(low[...], wo[...]).astype(LOW)
        head_moves = [
            copies.remote(
                d_own.at[:, pl.ds(pl.multiple_of(other["z"] * 128, 128), 128)],
                d_heads.at[own, :],
                other,
            )
            for other in others
        ]
        d_heads[own, :] = d_own[:, lane]
        yield
        output_grad = dot_tn(o_own[...], low[...]).astype(LOW)
        for part in range(4):
            middle[512 * part : 512 * part + 512, 1024:] = output_grad[
                :, 128 * part : 128 * part + 128
            ]
        late_columns = as_columns(sums)
        fill_tables(frequency[...], cosine, sine)
        d_acc[...] = jnp.zeros_like(d_acc)
        d_weight[...] = jnp.zeros_like(d_weight)
        yield
        loaded("third")
        for move in head_moves:
            move.wait_recv()
        column_sums = jnp.zeros((1, OWN), WIDE)
        for block in reversed(range(4)):
            here = pl.ds(OWN * block, OWN)
            deltas = pair_sums(d_heads[here, :].astype(WIDE) * o[here, :].astype(WIDE))
            for past in reversed(range(block + 1)):
                there = pl.ds(OWN * past, OWN)
                ((d_q, d_k, d_v),) = attend_back_blocks(
                    [
                        (
                            q[here, :],
                            d_heads[here, :],
                            k[there, :],
                            v[there, :],
                            level[:, here],
                            deltas,
                        )
                    ],
                    0 if past == block else None,
                )
                d_acc[here, :128] += d_q
                d_acc[there, 128:256] += d_k
                d_acc[there, 256:] += d_v
                yield
            cos, sin = cosine[here, :], -sine[here, :]
            turned[here, :128] = turn(d_acc[here, :128], cos, sin).astype(LOW)
            turned[here, 128:256] = turn(d_acc[here, 128:256], cos, sin).astype(LOW)
            turned[here, 256:] = d_acc[here, 256:].astype(LOW)

            @pl.when(z != block)
            def send():
                rows_move(block, z).start()

            d_weight[...] += dot_tn(a1[here, :], turned[here, :])
            column_sums = column_sums + jnp.sum(
                turned[here, :].astype(WIDE), axis=0, keepdims=True
            )
            yield
        weight = wqkv[...].astype(WIDE)
        late[:, :OWN] = d_weight[...].astype(LOW)
        shift_grad = jnp.sum(weight * column_sums, axis=1, keepdims=True)
        whole = jnp.sum(weight * d_weight[...], axis=1, keepdims=True)
        columns = as_columns([a_gain[...], a_shift[...]])
        gain_grad = (whole - columns[:, 1:2] * shift_grad) * (1.0 / columns[:, 0:1])
        lanes = lanes_iota((WIDTH, 128))
        columns = jnp.where(lanes == 2, gain_grad, jnp.where(lanes == 3, shift_grad, late_columns))
        late[:, OWN:] = columns.astype(LOW)
        yield
        d_rows[:, pl.ds(pl.multiple_of(z * OWN, 128), OWN)] = turned[own, :]
        for step in range(1, 4):
            rows_move(z, lax.rem(z + step, 4)).wait_recv()
        ds[...] = dot_nt(d_rows[...], wall[...])
        for step in range(3):
            here = pl.ds(128 * step, 128)
            back, _ = norm_back(x[here, :].astype(WIDE), a_gain[...], ds[here, :])
            dh[here, :] = dh[here, :] + back
        writes.append(copies.local(dh, x_out))
        yield

    walk = steps()
    next(walk)
    loaded("early")
    for number in ORDER[1:]:
        if number < 0:
            next(walk)
        else:
            tick(number)
    copies.finish()
    for step in range(1, 4):
        rows_move(lax.rem(z + step, 4), z).wait_send()
    for move in writes:
        move.wait()


def back(operands, frequency, gains):
    def shape(*dims, kind=LOW):
        return (dims, kind)

    outs = [shape(OWN, WIDTH, kind=WIDE)] + [shape(*dims) for dims in STACK_SHAPES[:3]]
    outs.append(shape(4, WIDTH, WIDTH))
    scratch = [
        shape(OWN, WIDTH),
        shape(OWN, WIDTH, kind=WIDE),
        shape(OWN, WIDTH, kind=WIDE),
        shape(OWN, WIDTH),
        shape(OWN, HIDDEN),
        shape(OWN, HIDDEN),
        shape(OWN, WIDTH),
        shape(WIDTH, OWN),
        shape(WIDTH, WIDTH),
        shape(WIDTH, HIDDEN),
        shape(HIDDEN, WIDTH),
        shape(ROWS, WIDTH),
        shape(ROWS, 128),
        shape(ROWS, 128),
        shape(ROWS, 128),
        shape(ROWS, 128),
        shape(8, ROWS, kind=WIDE),
        shape(*STACK_SHAPES[0]),
        shape(*STACK_SHAPES[1]),
        shape(ROWS, 128, kind=WIDE),
        shape(ROWS, 128, kind=WIDE),
        shape(WIDTH, ROWS),
        shape(OWN, WIDTH),
        shape(OWN, HIDDEN),
        shape(OWN, WIDTH, kind=WIDE),
        shape(OWN, WIDTH),
        shape(ROWS, 128),
        shape(ROWS, OWN, kind=WIDE),
        shape(ROWS, OWN),
        shape(OWN, ROWS),
        shape(WIDTH, OWN, kind=WIDE),
        shape(*STACK_SHAPES[2]),
        shape(*STACK_SHAPES[3]),
    ]
    scratch += [shape(rows // 2, lanes) for rows, lanes in STACK_SHAPES]
    scratch += outs[1:]
    for stream in STREAMS:
        scratch += [shape(*dims) for dims in stream.landing_shapes(STACK_ROWS)]
    vmem = pl.BlockSpec(memory_space=VMEM)
    hbm = pl.BlockSpec(memory_space=pl.ANY)
    copy_count = 280
    return pl.pallas_call(
        back_kernel,
        out_shape=[jax.ShapeDtypeStruct(*out) for out in outs],
        in_specs=[hbm] * len(operands) + [vmem] * 4,
        out_specs=[hbm] * len(outs),
        scratch_shapes=[VMEM(*part) for part in scratch]
        + [pltpu.SemaphoreType.DMA((copy_count,)), pltpu.SemaphoreType.DMA((copy_count,))],
        compiler_params=pltpu.CompilerParams(
            collective_id=2, has_side_effects=True, vmem_limit_bytes=63 * 2**20
        ),
    )(*operands, frequency, *gains)


def unstack_kernel(*refs):
    stacks_hbm, passed_hbm, vectors = refs[:4], refs[4:6], refs[6:14]
    passed_out, outs_hbm = refs[14:16], refs[16:30]
    stacks, passed, wides, sems = refs[30:34], refs[34:36], refs[36:50], refs[50]
    loads = [
        pltpu.make_async_copy(source, target, sems.at[place])
        for place, (source, target) in enumerate(zip(stacks_hbm, stacks))
    ]
    for place in (2, 0, 1, 3):
        loads[place].start()
    passing = []
    for place in range(2):
        passing.append(
            pltpu.make_async_copy(passed_hbm[place], passed[place], sems.at[18 + place])
        )
        passing[place].start()
    early, coarse, middle, late = stacks
    (wq, wk, wv, wo, we, wc, wp, cq, ck, cv, co, ce, cc, wu) = wides
    writes = []

    def write(place):
        move = pltpu.make_async_copy(wides[place], outs_hbm[place], sems.at[4 + place])
        move.start()
        writes.append(move)

    loads[2].wait()
    for step in range(4):
        here = slice(512 * step, 512 * step + 512)
        wc[here, :] = middle[here, :512].astype(WIDE)
    write(5)
    for part in range(4):
        here = slice(512 * part, 512 * part + 512)
        we[:, here] = middle[here, 512:1024].astype(WIDE)
        wo[:, 128 * part : 128 * part + 128] = middle[here, 1024:].astype(WIDE)
    write(4)
    write(3)
    loads[0].wait()
    for number in range(6):
        for part in range(2):
            down, across = divmod(2 * number + part, 3)
            block = early[512 * down : 512 * down + 512, 256 * across : 256 * across + 256].astype(WIDE)
            inside = 256 * part
            if number < 3:
                wp[512 * number : 512 * number + 512, inside : inside + 256] = block
            else:
                start = 512 * (number - 3) + inside
                wu[:, start : start + 256] = block
        if number == 2:
            write(6)
    write(13)
    loads[1].wait()
    ce[...] = coarse[:, :512].astype(WIDE)
    write(11)
    cc[...] = coarse[:, 512:1024].astype(WIDE)
    write(12)
    for place, ref in enumerate((cq, ck, cv)):
        ref[...] = coarse[:, 1024 + 128 * place : 1152 + 128 * place].astype(WIDE)
        write(7 + place)
    for part in range(4):
        here = slice(128 * part, 128 * part + 128)
        co[:, here] = coarse[here, 1408:1536].astype(WIDE)
    write(10)
    loads[3].wait()
    for place, ref in enumerate((wq, wk, wv)):
        for group in range(4):
            ref[:, 128 * group : 128 * group + 128] = late[
                group, :, 128 * place : 128 * place + 128
            ].astype(WIDE)
        write(place)
    columns = sum(late[group, :, OWN:].astype(WIDE) for group in range(4))
    for place, row in enumerate(
        (jnp.transpose(columns), jnp.transpose(coarse[:, 1536:].astype(WIDE)))
    ):
        for line in range(4):
            vectors[4 * place + line][...] = row[line]
    for place in range(2):
        passing[place].wait()
        move = pltpu.make_async_copy(passed[place], passed_out[place], sems.at[20 + place])
        move.start()
        writes.append(move)
    for move in writes:
        move.wait()


def unstack(stacks, passed):
    shapes = (
        [(WIDTH, WIDTH)] * 4
        + [(WIDTH, HIDDEN), (HIDDEN, WIDTH), (ROWS, WIDTH)]
        + [(WIDTH, 128)] * 3
        + [(128, WIDTH), (WIDTH, WIDTH), (WIDTH, WIDTH), (WIDTH, ROWS)]
    )
    vmem = pl.BlockSpec(memory_space=VMEM)
    hbm = pl.BlockSpec(memory_space=pl.ANY)
    return pl.pallas_call(
        unstack_kernel,
        out_shape=[jax.ShapeDtypeStruct((WIDTH,), WIDE)] * 8
        + [jax.ShapeDtypeStruct(array.shape, array.dtype) for array in passed]
        + [jax.ShapeDtypeStruct(shape, WIDE) for shape in shapes],
        in_specs=[hbm] * 6,
        out_specs=[vmem] * 8 + [hbm] * (2 + len(shapes)),
        scratch_shapes=[VMEM(stack.shape, LOW) for stack in stacks]
        + [VMEM(array.shape, array.dtype) for array in passed]
        + [VMEM(shape, WIDE) for shape in shapes]
        + [pltpu.SemaphoreType.DMA((8 + len(shapes),))],
        compiler_params=pltpu.CompilerParams(vmem_limit_bytes=60 * 2**20),
    )(*stacks, *passed)


def body(
    inputs,
    lengths,
    cotangent,
    attention_gain,
    attention_shift,
    query_weight,
    key_weight,
    value_weight,
    output_weight,
    feedforward_gain,
    feedforward_shift,
    expand_weight,
    contract_weight,
    pooling_weight,
    coarse_gain,
    coarse_shift,
    coarse_query,
    coarse_key,
    coarse_value,
    coarse_output,
    widen_gain,
    widen_shift,
    coarse_expand,
    coarse_contract,
    upsample_weight,
):
    def row(vector):
        return vector.reshape(1, -1)

    frequency = jnp.asarray(frequency_row())
    square = (query_weight, key_weight, value_weight)
    (a1, q, k, v, o, level, o_own, h, a2, act, slope, wqkv, mixed, ds, early, coarse_stack) = front(
        lengths,
        inputs,
        cotangent,
        [
            row(vector)
            for vector in (
                attention_gain,
                attention_shift,
                feedforward_gain,
                feedforward_shift,
                coarse_gain,
                coarse_shift,
                widen_gain,
                widen_shift,
            )
        ],
        frequency,
        (*square, output_weight, expand_weight, contract_weight, pooling_weight, upsample_weight),
        (coarse_query, coarse_key, coarse_value, coarse_output, coarse_expand, coarse_contract),
    )
    input_grad, *stacks = back(
        (
            inputs,
            ds,
            h,
            a2,
            act,
            slope,
            o_own,
            wqkv,
            *square,
            output_weight,
            expand_weight,
            contract_weight,
            a1,
            q,
            k,
            v,
            o,
            level,
            early,
            coarse_stack,
        ),
        frequency,
        (
            row(attention_gain),
            row(attention_shift),
            row(feedforward_gain),
        ),
    )
    results = unstack(stacks, (mixed, input_grad))
    vectors, (mixed, input_grad) = results[:8], results[8:10]
    wq, wk, wv, wo, we, wc, wp, cq, ck, cv, co, ce, cc, wu = results[10:]
    return (
        mixed,
        input_grad,
        vectors[2],
        vectors[3],
        wq,
        wk,
        wv,
        wo,
        vectors[0],
        vectors[1],
        we,
        wc,
        wp,
        vectors[4],
        vectors[5],
        cq,
        ck,
        cv,
        co,
        vectors[6],
        vectors[7],
        ce,
        cc,
        wu,
    )


def solution(mesh):
    in_specs = (
        P(("seq", "head"), None),
        P("seq"),
        P(("seq", "head"), None),
        P(),
        P(),
        P(),
        P(),
        P(),
        P(),
        P(),
        P(),
        P(),
        P(),
        P(),
        P(),
        P(),
        P(None, "head"),
        P(None, "head"),
        P(None, "head"),
        P("head", None),
        P(),
        P(),
        P(None, "head"),
        P("head", None),
        P(),
    )
    out_specs = (
        P(("seq", "head"), None),
        P(("seq", "head"), None),
        P(),
        P(),
        P(),
        P(),
        P(),
        P(),
        P(),
        P(),
        P(),
        P(),
        P(),
        P(),
        P(),
        P(None, "head"),
        P(None, "head"),
        P(None, "head"),
        P("head", None),
        P(),
        P(),
        P(None, "head"),
        P("head", None),
        P(),
    )
    return jax.shard_map(body, mesh=mesh, in_specs=in_specs, out_specs=out_specs, check_vma=False)
```

```python
import functools
import math

import jax
import jax.numpy as jnp
import numpy as np
from jax import lax
from jax.experimental import pallas as pl
from jax.experimental.pallas import tpu as pltpu
from jax.sharding import PartitionSpec as P

MESH = pl.DeviceIdType.MESH
VMEM = pltpu.VMEM
LOW = jnp.bfloat16
WIDE = jnp.float32
EPSILON = 1e-05
OWN = 384
ROWS = 1536
WIDTH = 512
HIDDEN = 2048
SHORT = 528
PART = 144
SIZES = {"core": 2, "x": 4, "y": 4, "z": 4}


def my_coords():
    seq = lax.axis_index("seq")
    return {
        "core": lax.rem(seq, 2),
        "y": lax.rem(lax.div(seq, 2), 4),
        "x": lax.div(seq, 8),
        "z": lax.axis_index("head"),
    }


def moved(coords, axis, step):
    other = dict(coords)
    other[axis] = lax.rem(coords[axis] + step, SIZES[axis])
    return other


def device_of(coords):
    return {
        "seq": (coords["x"] * 4 + coords["y"]) * 2 + coords["core"],
        "head": coords["z"],
    }


def meet(coords, axes):
    barrier = pltpu.get_barrier_semaphore()
    count = 0
    for axis in axes:
        for step in range(1, SIZES[axis]):
            pl.semaphore_signal(
                barrier,
                inc=1,
                device_id=device_of(moved(coords, axis, step)),
                device_id_type=MESH,
            )
            count += 1
    pl.semaphore_wait(barrier, count)


def dot(left, right):
    return lax.dot_general(left, right, (((1,), (0,)), ((), ())), preferred_element_type=WIDE)


def dot_nt(left, right):
    return lax.dot_general(left, right, (((1,), (1,)), ((), ())), preferred_element_type=WIDE)


def dot_tn(left, right):
    return lax.dot_general(left, right, (((0,), (0,)), ((), ())), preferred_element_type=WIDE)


def lanes_iota(shape):
    return lax.broadcasted_iota(jnp.int32, shape, len(shape) - 1)


def rows_iota(shape):
    return lax.broadcasted_iota(jnp.int32, shape, 0)


def standard(values):
    centred = values - jnp.mean(values, axis=-1, keepdims=True)
    scale = lax.rsqrt(jnp.mean(centred * centred, axis=-1, keepdims=True) + EPSILON)
    return centred * scale, scale


def norm(values, gain, shift):
    return standard(values)[0] * gain + shift


def norm_back(values, gain, grad):
    unit, scale = standard(values)
    inner = grad * gain
    first = jnp.mean(inner, axis=-1, keepdims=True)
    second = jnp.mean(inner * unit, axis=-1, keepdims=True)
    return scale * (inner - first - unit * second), grad * unit


def turn(values, cosine, sine):
    lane = lanes_iota(values.shape)
    other = jnp.where(
        lax.rem(lane, 64) < 32, pltpu.roll(values, 96, 1), pltpu.roll(values, 32, 1)
    )
    return values * cosine + other * sine


def gelu_parts(values):
    half = 0.5 + 0.5 * lax.erf(values * math.sqrt(0.5))
    bell = jnp.exp(values * values * -0.5) * (1.0 / math.sqrt(2.0 * math.pi))
    return values * half, half + values * bell


def head_lanes(head, values):
    return jnp.where(lanes_iota(values.shape) // 64 == head, values, jnp.zeros_like(values))


def by_head(first, second):
    return jnp.where(lanes_iota(first.shape) < 64, first, second)


def head_rows(columns):
    shape = (8, 128)
    pick = (lanes_iota(shape) == rows_iota(shape) * 64).astype(WIDE)
    return lax.dot_general(
        pick,
        columns,
        (((1,), (1,)), ((), ())),
        precision=lax.Precision.HIGHEST,
        preferred_element_type=WIDE,
    )


def frequency_row():
    frequency = np.exp(np.arange(32, dtype=np.float32) * np.float32(-math.log(10000.0) / 32))
    return np.tile(frequency.astype(np.float32), 4)[None, :]


def fill_tables(frequency, cosine, sine):
    coarse = rows_iota((24, 128)).astype(WIDE) * 64.0 * frequency
    fine = rows_iota((64, 128)).astype(WIDE) * frequency
    sign = jnp.where(lax.rem(lanes_iota((64, 128)), 64) < 32, -1.0, 1.0)
    coarse_cos, coarse_sin = jnp.cos(coarse), jnp.sin(coarse)
    fine_cos, fine_sin = jnp.cos(fine), jnp.sin(fine)
    for place in range(24):
        one_cos, one_sin = coarse_cos[place : place + 1], coarse_sin[place : place + 1]
        here = pl.ds(64 * place, 64)
        cosine[here, :] = one_cos * fine_cos - one_sin * fine_sin
        sine[here, :] = (one_sin * fine_cos + one_cos * fine_sin) * sign


def as_columns(vectors):
    filler = jnp.zeros((128 - len(vectors), WIDTH), WIDE)
    return jnp.transpose(jnp.concatenate(vectors + [filler], axis=0))


class Copies:
    def __init__(self, send_sem, recv_sem):
        self.send_sem, self.recv_sem, self.count, self.sent = send_sem, recv_sem, 0, []

    def remote(self, source, target, other):
        place = self.count
        self.count += 1
        move = pltpu.make_async_remote_copy(
            src_ref=source,
            dst_ref=target,
            send_sem=self.send_sem.at[place],
            recv_sem=self.recv_sem.at[place],
            device_id=device_of(other),
            device_id_type=MESH,
        )
        move.start()
        self.sent.append(move)
        return move

    def local(self, source, target):
        place = self.count
        self.count += 1
        move = pltpu.make_async_copy(source, target, self.recv_sem.at[place])
        move.start()
        return move

    def finish(self):
        for move in self.sent:
            move.wait_send()


def pair_sums(columns):
    shape = (8, 128)
    pick = (lanes_iota(shape) // 64 == rows_iota(shape)).astype(WIDE)
    return lax.dot_general(
        pick,
        columns,
        (((1,), (1,)), ((), ())),
        precision=lax.Precision.HIGHEST,
        preferred_element_type=WIDE,
    )


def attend_tiles(items, before, width, offset):
    last, first = pl.ds(before, width), pl.ds(0, before)
    chains = [(item, head) for item in items for head in range(2)]
    queries = [head_lanes(head, item[0]) for item, head in chains]
    near = [dot_nt(query, item[1][last, item[3]]) for query, (item, _) in zip(queries, chains)]
    keep = [
        lanes_iota(near[0].shape) <= rows_iota(near[0].shape) + shift
        for shift in (offset if isinstance(offset, tuple) else (offset,) * len(items))
    ]
    near = [jnp.where(keep[place // 2], scores, -1e30) for place, scores in enumerate(near)]
    tops = [jnp.max(scores, axis=-1, keepdims=True) for scores in near]
    if before:
        far = [dot_nt(query, item[1][first, item[3]]) for query, (item, _) in zip(queries, chains)]
        tops = [jnp.maximum(t, jnp.max(s, axis=-1, keepdims=True)) for t, s in zip(tops, far)]
        far = [jnp.exp(scores - t) for scores, t in zip(far, tops)]
    near = [jnp.exp(scores - t) for scores, t in zip(near, tops)]
    totals = [jnp.sum(probs, axis=-1, keepdims=True) for probs in near]
    mixed = [dot(probs.astype(LOW), item[2][last, item[3]]) for probs, (item, _) in zip(near, chains)]
    if before:
        totals = [t + jnp.sum(probs, axis=-1, keepdims=True) for t, probs in zip(totals, far)]
        mixed = [
            m + dot(probs.astype(LOW), item[2][first, item[3]])
            for m, probs, (item, _) in zip(mixed, far, chains)
        ]
    outs = [m * (1.0 / t) for m, t in zip(mixed, totals)]
    levels = [t + jnp.log(total) for t, total in zip(tops, totals)]
    shape = (items[0][0].shape[0], 128)
    results = []
    for place in range(len(items)):
        a, b = 2 * place, 2 * place + 1
        level = by_head(jnp.broadcast_to(levels[a], shape), jnp.broadcast_to(levels[b], shape))
        results.append((by_head(outs[a], outs[b]), head_rows(level)))
    return results


def attend_back_blocks(items, offset):
    chains = [(item, head) for item in items for head in range(2)]
    queries = [head_lanes(head, item[0]) for item, head in chains]
    d_outs = [head_lanes(head, item[1]) for item, head in chains]
    scores = [dot_nt(item[2], query) for query, (item, _) in zip(queries, chains)]
    d_probs = [dot_nt(item[3], d_out) for d_out, (item, _) in zip(d_outs, chains)]
    probs = [
        jnp.exp(score - item[4][head : head + 1]) for score, (item, head) in zip(scores, chains)
    ]
    if offset is not None:
        keep = rows_iota(probs[0].shape) <= lanes_iota(probs[0].shape) + offset
        probs = [jnp.where(keep, prob, 0.0) for prob in probs]
    d_scores = [
        (prob * (d_prob - item[5][head : head + 1])).astype(LOW)
        for prob, d_prob, (item, head) in zip(probs, d_probs, chains)
    ]
    d_values = [dot(prob.astype(LOW), d_out) for prob, d_out in zip(probs, d_outs)]
    d_keys = [dot(d_score, query) for d_score, query in zip(d_scores, queries)]
    d_queries = [dot_tn(d_score, item[2]) for d_score, (item, _) in zip(d_scores, chains)]
    return [
        (
            by_head(d_queries[i], d_queries[i + 1]) * 0.125,
            d_keys[i] + d_keys[i + 1],
            d_values[i] + d_values[i + 1],
        )
        for i in range(0, len(chains), 2)
    ]


COARSE_STACK = (WIDTH, 1664)
COARSE_TILES = ((0, 256, 256), (256, 256, 256), (512, 16, 128))


def front_kernel(*refs):
    (lengths, x, cot, a_gain, a_shift, f_gain, f_shift, c_gain, c_shift, w_gain, w_shift) = refs[:11]
    (frequency, wq_hbm, wk_hbm, wv_hbm, wo_hbm, we_hbm, wc_hbm, wp_hbm, wu_hbm) = refs[11:20]
    shards = refs[20:26]
    out_refs = refs[26:42]
    (a1, q, k, v, o, level, o_own, h, a2, act, slope, wqkv, mixed, ds, early, stack) = refs[42:58]
    (wo, we, wc, wp, wu, cosine, sine, landing, thin, s, m, c0g, dcg, fqkv, fo, fe, fc) = refs[58:75]
    (c0, c1, b1, b2, dr, cq, ck, cv, co, clevel, d_out, c_act, d_pre, total, top, d_pair, d_three,
     kept_act, kept_pre, send_sem, recv_sem) = refs[75:]
    saved = {}

    def save(key, source, part=None, place=None):
        target = out_refs[key if place is None else place]
        saved[key] = copies.local(source, target if part is None else target.at[part])

    coords = my_coords()
    z = coords["z"]
    core = coords["core"]
    right, left, far = (moved(coords, "z", step) for step in (1, 3, 2))
    copies = Copies(send_sem, recv_sem)
    lane = pl.ds(pl.multiple_of(z * 128, 128), 128)
    first_loads = [
        copies.local(weight.at[:, lane], wqkv.at[:, pl.ds(128 * place, 128)])
        for place, weight in enumerate((wq_hbm, wk_hbm, wv_hbm))
    ]
    loads = [
        copies.local(source, target)
        for source, target in ((wu_hbm, wu), (wo_hbm, wo), (we_hbm, we), (wc_hbm, wc), (wp_hbm, wp))
    ]
    own_weights = [
        copies.local(shard, full)
        for shard, full in zip(
            shards,
            [fqkv.at[z, :, pl.ds(128 * place, 128)] for place in range(3)]
            + [fo.at[z], fe.at[z], fc.at[z]],
        )
    ]
    meet(coords, ("core", "x", "y", "z"))
    low, high = pl.ds(0, OWN // 2), pl.ds(OWN // 2, OWN // 2)
    to_right = copies.remote(x.at[low], landing.at[0, low], right)
    to_left = copies.remote(x.at[high], landing.at[1, high], left)
    to_right_more = copies.remote(x.at[high], landing.at[0, high], right)
    to_left_more = copies.remote(x.at[low], landing.at[1, low], left)

    def project(block, index):
        start = pl.multiple_of(index * OWN, OWN)

        for step in range(OWN // 128):
            there = pl.ds(pl.multiple_of(start + 128 * step, 128), 128)
            values = block[pl.ds(128 * step, 128), :].astype(WIDE)
            a1[there, :] = norm(values, a_gain[...], a_shift[...]).astype(LOW)
        here = pl.ds(start, OWN)
        both = dot(a1[here, :], wqkv[...])
        cos, sin = cosine[here, :], sine[here, :]
        q[here, :] = (turn(both[:, :128], cos, sin) * 0.125).astype(LOW)
        k[here, :] = turn(both[:, 128:256], cos, sin).astype(LOW)
        v[here, :] = both[:, 256:].astype(LOW)

    fill_tables(frequency[...], cosine, sine)
    for load in first_loads:
        load.wait()
    project(x, z)
    to_right.wait_recv()
    far_right = copies.remote(landing.at[0, low], landing.at[2, low], right)
    to_left.wait_recv()
    far_left = copies.remote(landing.at[1, high], landing.at[2, high], left)

    valid = (rows_iota((OWN, 128)) + z * OWN < lengths[0]).astype(WIDE)
    for part in range(4):
        thin[part, pl.ds(0, 8), :] = jnp.zeros((8, 128), WIDE)
        thin[part, pl.ds(392, 48), :] = jnp.zeros((48, 128), WIDE)
        thin[part, pl.ds(8, OWN), :] = cot[:, 128 * part : 128 * part + 128].astype(WIDE) * valid

    def every_third(first, count):
        pieces = [thin[part, pl.ds(first, count, 3), :].astype(LOW) for part in range(4)]
        return jnp.concatenate(pieces, axis=1)

    loads[0].wait()
    lifted_back = sum(
        dot_nt(every_third(8 + r, 128), wu[:, 512 * r : 512 * r + 512]) for r in range(3)
    )
    dcg[z] = lifted_back.astype(LOW)

    to_right_more.wait_recv()
    project(landing.at[0], left["z"])
    to_left_more.wait_recv()
    project(landing.at[1], right["z"])
    far_right.wait_recv()
    far_left.wait_recv()
    project(landing.at[2], far["z"])

    for load in own_weights:
        load.wait()
    z_others = (right, left, far)
    z_sources = (left, right, far)
    pieces = {}
    def first_pieces(place, full):
        for way, axis in enumerate(("x", "y")):
            rows = pl.ds(pl.multiple_of(core * 256 + way * 128 + coords[axis] * 32, 32), 32)
            for step, other in enumerate(z_others):
                pieces[place, way, step] = copies.remote(full.at[z, rows], full.at[z, rows], other)
    first_pieces(0, fqkv)
    fo_rows = pl.ds(pl.multiple_of(core * 64, 64), 64)
    fo_moves = [copies.remote(fo.at[z, fo_rows], fo.at[z, fo_rows], other) for other in z_others]

    sent_blocks = send_sem.shape[0] - 4
    got_blocks = recv_sem.shape[0] - 4

    def block_move(target, source):
        return pltpu.make_async_remote_copy(
            src_ref=o.at[pl.ds(pl.multiple_of(target * OWN, OWN), OWN), :],
            dst_ref=o_own.at[:, pl.ds(pl.multiple_of(source * 128, 128), 128)],
            send_sem=send_sem.at[sent_blocks + target],
            recv_sem=recv_sem.at[got_blocks + source],
            device_id=device_of({**coords, "z": target}),
            device_id_type=MESH,
        )

    everything = pl.ds(0, 128)
    for block in reversed(range(4)):
        tiles = [pl.ds(OWN * block + 128 * step, 128) for step in range(3)]
        results = attend_tiles(
            [(q[here, :], k, v, everything) for here in tiles], OWN * block, OWN, (0, 128, 256)
        )
        for here, (mixed_tile, tops) in zip(tiles, results):
            o[here, :] = mixed_tile.astype(LOW)
            level[:, here] = tops

        @pl.when(z != block)
        def send():
            block_move(block, z).start()

        if block == 2:
            first_pieces(1, fe)
            first_pieces(2, fc)

    for place, ref in ((0, a1), (1, q), (2, k), (3, v), (4, o), (5, level), (11, wqkv)):
        save(place, ref)
    o_own[:, lane] = o[pl.ds(pl.multiple_of(z * OWN, OWN), OWN), :]

    spread, swaps = {0: [], 1: [], 2: []}, {0: [], 1: [], 2: []}
    whole = (fqkv, fe, fc)
    sibling = moved(coords, "core", 1)

    def spread_out(place):
        for way, axis in enumerate(("x", "y")):
            rows = pl.ds(pl.multiple_of(core * 256 + way * 128 + coords[axis] * 32, 32), 32)
            for step, source in enumerate(z_sources):
                pieces[place, way, step].wait_recv()
                part = whole[place].at[source["z"], rows]
                for far_step in range(1, 4):
                    spread[place].append(copies.remote(part, part, moved(coords, axis, far_step)))

    def swap(place):
        for move in spread[place]:
            move.wait_recv()
        half = pl.ds(pl.multiple_of(core * 256, 256), 256)
        for source in z_sources:
            part = whole[place].at[source["z"], half]
            swaps[place].append(copies.remote(part, part, sibling))

    spread_out(0)
    for step in range(1, 4):
        other = lax.rem(z + step, 4)
        block_move(z, other).wait_recv()
    dc_moves = [copies.remote(dcg.at[z], dcg.at[z], other) for other in z_others]
    save(6, o_own)

    for load in loads[1:]:
        load.wait()

    def mix(step, carry):
        here = pl.ds(pl.multiple_of(step * 128, 128), 128)
        hidden = x[here, :].astype(WIDE) + dot(o_own[here, :], wo[...])
        h[here, :] = hidden
        a2[here, :] = norm(hidden, f_gain[...], f_shift[...]).astype(LOW)
        return carry

    lax.fori_loop(0, 3, mix, 0)

    def widen(step, carry):
        halves = [pl.ds(pl.multiple_of(step * 512 + 256 * half, 256), 256) for half in range(2)]
        ahead = [dot(a2[...], we[:, here]) for here in halves]
        for here, values in zip(halves, ahead):
            value, back = gelu_parts(values)
            act[:, here] = value.astype(LOW)
            slope[:, here] = back.astype(LOW)
        return carry

    lax.fori_loop(0, HIDDEN // 512, widen, 0)
    spread_out(1)
    spread_out(2)
    for place, ref in ((7, h), (8, a2), (9, act), (10, slope)):
        save(place, ref)

    for part in range(4):
        here = slice(128 * part, 128 * part + 128)
        if part % 2 == 0:
            wide = slice(256 * (part // 2), 256 * (part // 2) + 256)
            summed = h[:, wide] + dot(act[...], wc[:, wide])
            s[:, wide] = summed
        kept = (s[:, here] * valid).astype(LOW)
        m[:, here] = kept
        thin[part, pl.ds(8, OWN), :] = kept.astype(WIDE)
    pooled = sum(
        dot(every_third(6 + r, PART), wp[512 * r : 512 * r + 512, :]) for r in range(3)
    )
    c0g[z] = pooled.astype(LOW)
    c0_moves = [copies.remote(c0g.at[z], c0g.at[z], other) for other in z_others]
    fo_swaps = []
    for step, source in enumerate(z_sources):
        fo_moves[step].wait_recv()
        part = fo.at[source["z"], fo_rows]
        fo_swaps.append(copies.remote(part, part, sibling))
    swap(0)
    for move in c0_moves:
        move.wait_recv()

    own_lane = pl.ds(pl.multiple_of(z * 128, 128), 128)
    own_rows = pl.ds(pl.multiple_of(z * 128, 128), 128)

    def row_chunks(body):
        def run(step, carry):
            body(pl.ds(pl.multiple_of(step * 176, 16), 176))
            return carry

        lax.fori_loop(0, 3, run, 0)

    for part in range(4):
        base = 128 * part
        c0[pl.ds(base, 128), :] = c0g[part, pl.ds(0, 128), :].astype(WIDE)
        if part:
            first = pl.ds(base, 1)
            c0[first, :] = c0[first, :] + c0g[part - 1, pl.ds(128, 16), :].astype(WIDE)[:1]
    c0[pl.ds(512, 16), :] = c0g[3, pl.ds(128, 16), :].astype(WIDE)

    def first_norm(here):
        b1[here, :] = norm(c0[here, :], c_gain[...], c_shift[...]).astype(LOW)

    row_chunks(first_norm)
    for move in swaps[0]:
        move.wait_recv()
    for ref in (cq, ck, cv):
        ref[pl.ds(SHORT, 640 - SHORT), :] = jnp.zeros((640 - SHORT, WIDTH), LOW)

    for pair in range(4):
        lane = pl.ds(pair * 128, 128)
        both = dot(b1[...], fqkv[pair])
        cos, sin = cosine[pl.ds(0, SHORT), :], sine[pl.ds(0, SHORT), :]
        rows = pl.ds(0, SHORT)
        cq[rows, lane] = (turn(both[:, :128], cos, sin) * 0.125).astype(LOW)
        ck[rows, lane] = turn(both[:, 128:256], cos, sin).astype(LOW)
        cv[rows, lane] = both[:, 256:].astype(LOW)
    for first, count, width in COARSE_TILES:
        here = pl.ds(first, count)
        for pair, (mixed_tile, tops) in enumerate(
            attend_tiles([(cq[here, pl.ds(128 * p, 128)], ck, cv, pl.ds(128 * p, 128)) for p in range(4)], first, width, 0)
        ):
            co[here, pl.ds(128 * pair, 128)] = mixed_tile.astype(LOW)
            clevel[pair, :, here] = tops

    swap(1)
    swap(2)
    for move in dc_moves + fo_swaps:
        move.wait_recv()
    for part in range(4):
        dr[pl.ds(128 * part, 128), :] = dcg[part]
    dr[pl.ds(512, 16), :] = jnp.zeros((16, WIDTH), LOW)

    def second_norm(here):
        value = c0[here, :]
        for part in range(4):
            value = value + dot(co[here, 128 * part : 128 * part + 128], fo[part])
        c1[here, :] = value
        b2[here, :] = norm(value, w_gain[...], w_shift[...]).astype(LOW)

    row_chunks(second_norm)
    for move in swaps[1] + swaps[2]:
        move.wait_recv()
    total[...] = jnp.zeros_like(total)
    top[...] = c1[own_rows, :]

    def widen(act_ref, back_ref, step, carry):
        slot = lax.rem(z + step, 4)
        halves = (pl.ds(0, 256), pl.ds(256, 256))
        ahead = [dot(b2[...], fe[slot, :, lane]) for lane in halves]
        behind = [dot_nt(dr[...], fc[slot, lane, :]) for lane in halves]
        for lane, values, grads in zip(halves, ahead, behind):
            value, slope = gelu_parts(values)
            act_ref[:, lane] = value.astype(LOW)
            back_ref[:, lane] = (slope * grads).astype(LOW)
        top[...] += dot(act_ref[own_rows, :], fc[slot])
        total[...] += dot_nt(back_ref[...], fe[slot])
        return carry

    widen(kept_act, kept_pre, 0, 0)
    lax.fori_loop(1, 4, functools.partial(widen, c_act, d_pre), 0)

    def put_early(number, grad):
        for part in range(2):
            down, across = divmod(2 * number + part, 3)
            early[512 * down : 512 * down + 512, 256 * across : 256 * across + 256] = grad[
                :, 256 * part : 256 * part + 256
            ].astype(LOW)

    crest = top[...].astype(LOW)
    for r in range(3):
        lifted = dot(crest, wu[:, 512 * r : 512 * r + 512])
        for part in range(4):
            thin[part, pl.ds(8 + r, 128, 3), :] = lifted[:, 128 * part : 128 * part + 128]
    for part in range(4):
        lane = slice(128 * part, 128 * part + 128)
        mixed[:, lane] = (valid * (s[:, lane] + thin[part, pl.ds(8, OWN), :])).astype(LOW)
        thin[part, pl.ds(8, OWN), :] = cot[:, lane].astype(WIDE) * valid

    for r in range(3):
        put_early(3 + r, dot_tn(crest, every_third(8 + r, 128)))

    save(12, mixed)
    save(16, early.at[pl.ds(1024, 1024)], (pl.ds(1024, 1024),), 14)
    stack[:, :512] = dot_tn(b2[...], kept_pre[...]).astype(LOW)
    stack[:, 512:1024] = dot_tn(kept_act[...], dr[...]).astype(LOW)
    sums = [jnp.zeros((1, WIDTH), WIDE) for _ in range(4)]
    for step in range(3):
        here = pl.ds(176 * step, 176)
        grad = total[here, :]
        back, unit_grad = norm_back(c1[here, :], w_gain[...], grad)
        sums[2] = sums[2] + jnp.sum(unit_grad, axis=0, keepdims=True)
        sums[3] = sums[3] + jnp.sum(grad, axis=0, keepdims=True)
        back = dr[here, :].astype(WIDE) + back
        c1[here, :] = back
        b2[here, :] = back.astype(LOW)
    output_grad = dot_tn(co[:, own_lane], b2[...]).astype(LOW)
    for part in range(4):
        stack[128 * part : 128 * part + 128, 1408:1536] = output_grad[:, 128 * part : 128 * part + 128]
    for pair in range(4):
        d_out[:, pl.ds(128 * pair, 128)] = dot_nt(b2[...], fo[pair]).astype(LOW)
    lanes = [pl.ds(128 * pair, 128) for pair in range(4)]
    deltas = [
        pair_sums(d_out[:, lane].astype(WIDE) * co[:, lane].astype(WIDE)) for lane in lanes
    ]
    for first, count, width in COARSE_TILES:
        here = pl.ds(first, count)
        near, past = pl.ds(first, width), pl.ds(0, first)

        def items(there):
            return [
                (
                    cq[here, lane],
                    d_out[here, lane],
                    ck[there, lane],
                    cv[there, lane],
                    clevel[pair, :, here],
                    deltas[pair][:, first : first + count],
                )
                for pair, lane in enumerate(lanes)
            ]

        results = attend_back_blocks(items(near), 0)
        for pair, (d_q, d_k, d_v) in enumerate(results):
            d_pair[pair, here, :128] = d_q
            d_pair[pair, near, 128:256] = d_k
            d_pair[pair, near, 256:] = d_v
        if first:
            results = attend_back_blocks(items(past), None)
            for pair, (d_q, d_k, d_v) in enumerate(results):
                d_pair[pair, here, :128] += d_q
                d_pair[pair, past, 128:256] += d_k
                d_pair[pair, past, 256:] += d_v
    for pair in range(4):
        cos, sin = cosine[pl.ds(0, SHORT), :], -sine[pl.ds(0, SHORT), :]
        rows = pl.ds(0, SHORT)
        d_three[pair, :, :128] = turn(d_pair[pair, rows, :128], cos, sin).astype(LOW)
        d_three[pair, :, 128:256] = turn(d_pair[pair, rows, 128:256], cos, sin).astype(LOW)
        d_three[pair, :, 256:] = d_pair[pair, rows, 256:].astype(LOW)
    total[...] = sum(dot_nt(d_three[pair], fqkv[pair]) for pair in range(4))
    stack[:, 1024:1408] = dot_tn(b1[...], d_three[z]).astype(LOW)

    for step in range(3):
        here = pl.ds(176 * step, 176)
        grad = total[here, :]
        back, unit_grad = norm_back(c0[here, :], c_gain[...], grad)
        sums[0] = sums[0] + jnp.sum(unit_grad, axis=0, keepdims=True)
        sums[1] = sums[1] + jnp.sum(grad, axis=0, keepdims=True)
        b1[here, :] = (c1[here, :] + back).astype(LOW)
    stack[:, 1536:] = as_columns(sums).astype(LOW)

    save(15, stack)
    down = b1[pl.ds(pl.multiple_of(z * 128, 128), PART), :]
    for part in range(4):
        lane = slice(128 * part, 128 * part + 128)
        thin[part, pl.ds(0, 8), :] = jnp.zeros((8, 128), WIDE)
        thin[part, pl.ds(392, 48), :] = jnp.zeros((48, 128), WIDE)
        thin[part, pl.ds(8, OWN), :] = m[:, lane].astype(WIDE)
    for r in range(3):
        put_early(r, dot_tn(every_third(6 + r, PART), down))
    for r in range(3):
        back = dot_nt(down, wp[512 * r : 512 * r + 512, :])
        for part in range(4):
            thin[part, pl.ds(6 + r, PART, 3), :] = back[:, 128 * part : 128 * part + 128]
    for part in range(4):
        lane = slice(128 * part, 128 * part + 128)
        ds[:, lane] = valid * (cot[:, lane].astype(WIDE) + thin[part, pl.ds(8, OWN), :])
    save(13, ds)
    save(14, early.at[pl.ds(0, 1024)], (pl.ds(0, 1024),))
    copies.finish()
    for step in range(1, 4):
        block_move(lax.rem(z + step, 4), z).wait_send()
    for move in saved.values():
        move.wait()


def front(lengths, x, cot, gains, frequency, weights, shards):
    def shape(*dims, kind=LOW):
        return (dims, kind)

    outs = [
        shape(ROWS, WIDTH),
        shape(ROWS, 128),
        shape(ROWS, 128),
        shape(ROWS, 128),
        shape(ROWS, 128),
        shape(8, ROWS, kind=WIDE),
        shape(OWN, WIDTH),
        shape(OWN, WIDTH, kind=WIDE),
        shape(OWN, WIDTH),
        shape(OWN, HIDDEN),
        shape(OWN, HIDDEN),
        shape(WIDTH, OWN),
        shape(OWN, WIDTH),
        shape(OWN, WIDTH, kind=WIDE),
        shape(HIDDEN, 768),
        shape(*COARSE_STACK),
    ]
    scratch = [
        shape(WIDTH, WIDTH),
        shape(WIDTH, HIDDEN),
        shape(HIDDEN, WIDTH),
        shape(ROWS, WIDTH),
        shape(WIDTH, ROWS),
        shape(ROWS, 128, kind=WIDE),
        shape(ROWS, 128, kind=WIDE),
        shape(3, OWN, WIDTH),
        shape(4, 440, 128, kind=WIDE),
        shape(OWN, WIDTH, kind=WIDE),
        shape(OWN, WIDTH),
        shape(4, PART, WIDTH),
        shape(4, 128, WIDTH),
        shape(4, WIDTH, OWN),
        shape(4, 128, WIDTH),
        shape(4, WIDTH, WIDTH),
        shape(4, WIDTH, WIDTH),
        shape(SHORT, WIDTH, kind=WIDE),
        shape(SHORT, WIDTH, kind=WIDE),
        shape(SHORT, WIDTH),
        shape(SHORT, WIDTH),
        shape(SHORT, WIDTH),
        shape(640, WIDTH),
        shape(640, WIDTH),
        shape(640, WIDTH),
        shape(SHORT, WIDTH),
        shape(4, 8, 640, kind=WIDE),
        shape(SHORT, WIDTH),
        shape(SHORT, WIDTH),
        shape(SHORT, WIDTH),
        shape(SHORT, WIDTH, kind=WIDE),
        shape(128, WIDTH, kind=WIDE),
        shape(4, 640, OWN, kind=WIDE),
        shape(4, SHORT, OWN),
        shape(SHORT, WIDTH),
        shape(SHORT, WIDTH),
    ]
    vmem = pl.BlockSpec(memory_space=VMEM)
    hbm = pl.BlockSpec(memory_space=pl.ANY)
    copy_count = 160
    return pl.pallas_call(
        front_kernel,
        out_shape=[jax.ShapeDtypeStruct(*out) for out in outs],
        in_specs=[pl.BlockSpec(memory_space=pltpu.SMEM)] + [vmem] * 11 + [hbm] * 14,
        out_specs=[hbm] * len(outs),
        scratch_shapes=[VMEM(*out) for out in outs + scratch]
        + [pltpu.SemaphoreType.DMA((copy_count,)), pltpu.SemaphoreType.DMA((copy_count,))],
        compiler_params=pltpu.CompilerParams(
            collective_id=1, has_side_effects=True, vmem_limit_bytes=60 * 2**20
        ),
    )(lengths, x, cot, *gains, frequency, *weights, *shards)


class Stream:
    def __init__(self, stack, low, high, axes, spread=False):
        self.stack, self.lanes = stack, pl.ds(low, high - low)
        self.axes = axes
        self.levels = (*axes, "z") if spread else axes
        self.spread = spread

    def landing_shapes(self, row_counts):
        rows = row_counts[self.stack] // 2
        shapes = []
        for axis in self.axes[1:]:
            rows = rows // SIZES[axis]
            shapes.append((3, rows, self.lanes.size))
        return shapes


STREAMS = (
    Stream(0, 0, 384, ("core", "z", "y", "x")),
    Stream(0, 384, 768, ("core", "x", "z", "y")),
    Stream(1, 0, 768, ("core", "x", "y")),
    Stream(1, 768, 1664, ("core", "y", "x")),
    Stream(2, 0, 384, ("core", "y", "x", "z")),
    Stream(2, 384, 768, ("core", "z", "x", "y")),
    Stream(2, 768, 1024, ("core", "y", "x", "z")),
    Stream(2, 1024, 1152, ("core", "z", "x", "y")),
    Stream(3, 0, 256, ("core", "x", "y"), True),
    Stream(3, 256, 512, ("core", "x", "y"), True),
)
STACK_SHAPES = ((HIDDEN, 768), COARSE_STACK, (HIDDEN, 1152), (WIDTH, WIDTH))
STACK_ROWS = tuple(shape[0] for shape in STACK_SHAPES)
ORDER = (
    -1, 0, 1, 2, 3, -1, -1, -1, -1, 0, 1, 2, 3, -1, -1, -1, -1, 4, 5, 6, -1, -1, 7, 4, 5, 6, 7, 3, 0, 1, -1,
    -1, 2, -1, 3, -1, -1, -1, 4, -1, -1, -1, 3, -1, 5, -1, 6, -1, 7, 4, -1, 0, -1, 1, 2, -1, 9, 8, 5, 9, 8, 6,
    7, 0, 3, 1, 2, 5, 3, 7, 9, 4, 8, 1, 0, 5, 7, 6, 9, 4, 8, 2, 1, 0, 2, 6, 9, 5, -1, 7, 8, 4, 9, 8, 1, 0, 6,
    1, 0, 4, 9, 4, 5, 9, 6, 5, 7, 8, 6, 7, 8,
)


ROWS_AT_ONCE = {128: 256, 256: 128, 384: 64, 512: 64, 640: 32, 768: 32, 896: 32, 1024: 32}


class Summing:
    def __init__(self, stream, source, total, out, landings, copies, coords):
        self.stream, self.source, self.total, self.out = stream, source, total, out
        self.landings, self.copies, self.coords = landings, copies, coords
        self.pending = []
        self.tick_count = 0

    def rows_at(self, level, who, whole):
        rows = STACK_ROWS[self.stream.stack]
        start = 0
        for axis in self.stream.axes[:level]:
            rows = rows // SIZES[axis]
            if whole or axis != "core":
                start = start + who[axis] * rows
        return pl.ds(pl.multiple_of(start, 16), rows)

    def start_down(self, level):
        axis = self.stream.axes[level]
        lanes = self.stream.lanes
        self.pending = []
        for step in range(1, SIZES[axis]):
            other = moved(self.coords, axis, step)
            where = self.rows_at(level + 1, other, level == 0)
            if level == 0:
                source = self.source.at[where, lanes]
                target = self.total.at[pl.ds(0, where.size), lanes]
            else:
                source = self.total.at[where, lanes]
                target = self.landings[level - 1].at[step - 1]
            self.pending.append(self.copies.remote(source, target, other))

    def add_down(self, level):
        lanes = self.stream.lanes
        for move in self.pending:
            move.wait_recv()
        here = self.rows_at(level + 1, self.coords, False)
        mine = self.rows_at(1, self.coords, True)
        step_rows = min(here.size, ROWS_AT_ONCE[lanes.size])

        def add(index, carry):
            at = pl.multiple_of(index * step_rows, 16)
            part = pl.ds(pl.multiple_of(here.start + at, 16), step_rows)
            value = self.total[part, lanes].astype(WIDE)
            if level == 0:
                own = pl.ds(pl.multiple_of(mine.start + at, 16), step_rows)
                value = value + self.source[own, lanes].astype(WIDE)
            else:
                for slot in range(3):
                    landed = self.landings[level - 1][slot, pl.ds(at, step_rows), :]
                    value = value + landed.astype(WIDE)
            self.total[part, lanes] = value.astype(LOW)
            return carry

        lax.fori_loop(0, here.size // step_rows, add, 0)

    def start_up(self, level):
        axes = self.stream.axes
        where = self.rows_at(min(level + 1, len(axes)), self.coords, True)
        if level == len(axes):
            part = self.out.at[self.coords["z"], where, self.stream.lanes]
        elif self.stream.spread:
            part = self.out.at[pl.ds(0, 4), where, self.stream.lanes]
        else:
            part = self.out.at[where, self.stream.lanes]
        axis = self.stream.levels[level]
        self.pending = [
            self.copies.remote(part, part, moved(self.coords, axis, step))
            for step in range(1, SIZES[axis])
        ]

    def tick(self):
        now = self.tick_count
        self.tick_count += 1
        down, depth = len(self.stream.axes), len(self.stream.levels)
        if now < down:
            if now:
                self.add_down(now - 1)
            self.start_down(now)
        elif now == down:
            self.add_down(down - 1)
            last = self.rows_at(down, self.coords, True)
            value = self.total[self.rows_at(down, self.coords, False), self.stream.lanes]
            if self.stream.spread:
                self.out[self.coords["z"], last, self.stream.lanes] = value
            else:
                self.out[last, self.stream.lanes] = value
            self.start_up(depth - 1)
        elif now <= down + depth:
            for move in self.pending:
                move.wait_recv()
            if now < down + depth:
                self.start_up(depth - 1 - (now - down))

    def done(self):
        return self.tick_count > len(self.stream.axes) + len(self.stream.levels)


def back_kernel(*refs):
    (x_hbm, ds_hbm, h_hbm, a2_hbm, act_hbm, slope_hbm, o_own_hbm, wqkv_hbm, wq_hbm, wk_hbm, wv_hbm,
     wo_hbm, we_hbm, wc_hbm, a1_hbm, q_hbm, k_hbm, v_hbm, o_hbm, level_hbm, early_hbm,
     coarse_hbm) = refs[:22]
    (frequency, a_gain, a_shift, f_gain) = refs[22:26]
    x_out, *total_outs = refs[26:31]
    (x, ds, h, a2, act, slope, o_own, wqkv, wo, we, wc, a1, q, k, v, o, level, early, coarse, cosine,
     sine, wall, low, d_pre, dh, d_own, d_heads, d_acc, turned, d_rows, d_weight, middle, late) = refs[31:64]
    totals, outs = refs[64:68], refs[68:72]
    *landings, send_sem, recv_sem = refs[72:]
    coords = my_coords()
    z = coords["z"]
    others = [moved(coords, "z", step) for step in (1, 3, 2)]
    copies = Copies(send_sem, recv_sem)
    lane = pl.ds(pl.multiple_of(z * 128, 128), 128)
    own = pl.ds(pl.multiple_of(z * OWN, OWN), OWN)
    loads, writes = {}, []

    def load(name, *pairs):
        loads[name] = [copies.local(source, target) for source, target in pairs]

    def loaded(name):
        for move in loads.pop(name):
            move.wait()

    load("first", (ds_hbm, ds), (wc_hbm, wc), (slope_hbm, slope), (act_hbm, act), (a2_hbm, a2))
    load("early", (early_hbm, early), (coarse_hbm, coarse))
    meet(coords, ("core", "x", "y", "z"))

    sources = (early, coarse, middle, late)
    streams = []
    for stream in STREAMS:
        count = len(stream.axes) - 1
        streams.append(
            Summing(
                stream,
                sources[stream.stack],
                totals[stream.stack],
                outs[stream.stack],
                landings[:count],
                copies,
                coords,
            )
        )
        landings = landings[count:]

    def tick(number):
        streams[number].tick()
        if streams[number].done():
            stack, lanes = streams[number].stream.stack, streams[number].stream.lanes
            part = (slice(None),) * (len(outs[stack].shape) - 1) + (lanes,)
            writes.append(copies.local(outs[stack].at[part], total_outs[stack].at[part]))

    def widen_back(index):
        here = pl.ds(256 * index, 256)
        back = (slope[:, here].astype(WIDE) * dot_nt(low[...], wc[here, :])).astype(LOW)
        d_pre[:, here] = back
        middle[here, :512] = dot_tn(act[:, here], low[...]).astype(LOW)
        down = pl.ds(512 * (index // 2), 512)
        across = pl.ds(512 + 256 * (index % 2), 256)
        middle[down, across] = dot_tn(a2[...], back).astype(LOW)

    sent_blocks = send_sem.shape[0] - 4
    got_blocks = recv_sem.shape[0] - 4

    def rows_move(target, source):
        return pltpu.make_async_remote_copy(
            src_ref=turned.at[pl.ds(pl.multiple_of(target * OWN, OWN), OWN), :],
            dst_ref=d_rows.at[:, pl.ds(pl.multiple_of(source * OWN, 128), OWN)],
            send_sem=send_sem.at[sent_blocks + target],
            recv_sem=recv_sem.at[got_blocks + source],
            device_id=device_of({**coords, "z": target}),
            device_id_type=MESH,
        )

    def steps():
        loaded("first")
        low[...] = ds[...].astype(LOW)
        load("second", (we_hbm, we), (h_hbm, h), (wo_hbm, wo), (o_own_hbm, o_own))
        yield
        for index in range(8):
            widen_back(index)
            yield
        load(
            "third",
            (q_hbm, q),
            (k_hbm, k),
            (v_hbm, v),
            (o_hbm, o),
            (level_hbm, level),
            (a1_hbm, a1),
            (wqkv_hbm, wqkv),
            (x_hbm, x),
            *(
                (
                    weight.at[:, pl.ds(128 * group, 128)],
                    wall.at[:, pl.ds(OWN * group + 128 * place, 128)],
                )
                for group in range(4)
                for place, weight in enumerate((wq_hbm, wk_hbm, wv_hbm))
            ),
        )
        loaded("second")
        for part in range(2):
            here = slice(256 * part, 256 * part + 256)
            dh[:, here] = dot_nt(d_pre[...], we[here, :])
        sums = [jnp.zeros((1, WIDTH), WIDE) for _ in range(2)]
        for step in range(3):
            here = pl.ds(128 * step, 128)
            grad = dh[here, :]
            back, unit_grad = norm_back(h[here, :], f_gain[...], grad)
            sums[0] = sums[0] + jnp.sum(unit_grad, axis=0, keepdims=True)
            sums[1] = sums[1] + jnp.sum(grad, axis=0, keepdims=True)
            back = ds[here, :] + back
            dh[here, :] = back
            low[here, :] = back.astype(LOW)
        d_own[...] = dot_nt(low[...], wo[...]).astype(LOW)
        head_moves = [
            copies.remote(
                d_own.at[:, pl.ds(pl.multiple_of(other["z"] * 128, 128), 128)],
                d_heads.at[own, :],
                other,
            )
            for other in others
        ]
        d_heads[own, :] = d_own[:, lane]
        yield
        output_grad = dot_tn(o_own[...], low[...]).astype(LOW)
        for part in range(4):
            middle[512 * part : 512 * part + 512, 1024:] = output_grad[
                :, 128 * part : 128 * part + 128
            ]
        late_columns = as_columns(sums)
        fill_tables(frequency[...], cosine, sine)
        d_acc[...] = jnp.zeros_like(d_acc)
        d_weight[...] = jnp.zeros_like(d_weight)
        yield
        loaded("third")
        for move in head_moves:
            move.wait_recv()
        column_sums = jnp.zeros((1, OWN), WIDE)
        for block in reversed(range(4)):
            here = pl.ds(OWN * block, OWN)
            deltas = pair_sums(d_heads[here, :].astype(WIDE) * o[here, :].astype(WIDE))
            for past in reversed(range(block + 1)):
                there = pl.ds(OWN * past, OWN)
                ((d_q, d_k, d_v),) = attend_back_blocks(
                    [
                        (
                            q[here, :],
                            d_heads[here, :],
                            k[there, :],
                            v[there, :],
                            level[:, here],
                            deltas,
                        )
                    ],
                    0 if past == block else None,
                )
                d_acc[here, :128] += d_q
                d_acc[there, 128:256] += d_k
                d_acc[there, 256:] += d_v
                yield
            cos, sin = cosine[here, :], -sine[here, :]
            turned[here, :128] = turn(d_acc[here, :128], cos, sin).astype(LOW)
            turned[here, 128:256] = turn(d_acc[here, 128:256], cos, sin).astype(LOW)
            turned[here, 256:] = d_acc[here, 256:].astype(LOW)

            @pl.when(z != block)
            def send():
                rows_move(block, z).start()

            d_weight[...] += dot_tn(a1[here, :], turned[here, :])
            column_sums = column_sums + jnp.sum(
                turned[here, :].astype(WIDE), axis=0, keepdims=True
            )
            yield
        weight = wqkv[...].astype(WIDE)
        late[:, :OWN] = d_weight[...].astype(LOW)
        shift_grad = jnp.sum(weight * column_sums, axis=1, keepdims=True)
        whole = jnp.sum(weight * d_weight[...], axis=1, keepdims=True)
        columns = as_columns([a_gain[...], a_shift[...]])
        gain_grad = (whole - columns[:, 1:2] * shift_grad) * (1.0 / columns[:, 0:1])
        lanes = lanes_iota((WIDTH, 128))
        columns = jnp.where(lanes == 2, gain_grad, jnp.where(lanes == 3, shift_grad, late_columns))
        late[:, OWN:] = columns.astype(LOW)
        yield
        d_rows[:, pl.ds(pl.multiple_of(z * OWN, 128), OWN)] = turned[own, :]
        for step in range(1, 4):
            rows_move(z, lax.rem(z + step, 4)).wait_recv()
        ds[...] = dot_nt(d_rows[...], wall[...])
        for step in range(3):
            here = pl.ds(128 * step, 128)
            back, _ = norm_back(x[here, :].astype(WIDE), a_gain[...], ds[here, :])
            dh[here, :] = dh[here, :] + back
        writes.append(copies.local(dh, x_out))
        yield

    walk = steps()
    next(walk)
    loaded("early")
    for number in ORDER[1:]:
        if number < 0:
            next(walk)
        else:
            tick(number)
    copies.finish()
    for step in range(1, 4):
        rows_move(lax.rem(z + step, 4), z).wait_send()
    for move in writes:
        move.wait()


def back(operands, frequency, gains):
    def shape(*dims, kind=LOW):
        return (dims, kind)

    outs = [shape(OWN, WIDTH, kind=WIDE)] + [shape(*dims) for dims in STACK_SHAPES[:3]]
    outs.append(shape(4, WIDTH, WIDTH))
    scratch = [
        shape(OWN, WIDTH),
        shape(OWN, WIDTH, kind=WIDE),
        shape(OWN, WIDTH, kind=WIDE),
        shape(OWN, WIDTH),
        shape(OWN, HIDDEN),
        shape(OWN, HIDDEN),
        shape(OWN, WIDTH),
        shape(WIDTH, OWN),
        shape(WIDTH, WIDTH),
        shape(WIDTH, HIDDEN),
        shape(HIDDEN, WIDTH),
        shape(ROWS, WIDTH),
        shape(ROWS, 128),
        shape(ROWS, 128),
        shape(ROWS, 128),
        shape(ROWS, 128),
        shape(8, ROWS, kind=WIDE),
        shape(*STACK_SHAPES[0]),
        shape(*STACK_SHAPES[1]),
        shape(ROWS, 128, kind=WIDE),
        shape(ROWS, 128, kind=WIDE),
        shape(WIDTH, ROWS),
        shape(OWN, WIDTH),
        shape(OWN, HIDDEN),
        shape(OWN, WIDTH, kind=WIDE),
        shape(OWN, WIDTH),
        shape(ROWS, 128),
        shape(ROWS, OWN, kind=WIDE),
        shape(ROWS, OWN),
        shape(OWN, ROWS),
        shape(WIDTH, OWN, kind=WIDE),
        shape(*STACK_SHAPES[2]),
        shape(*STACK_SHAPES[3]),
    ]
    scratch += [shape(rows // 2, lanes) for rows, lanes in STACK_SHAPES]
    scratch += outs[1:]
    for stream in STREAMS:
        scratch += [shape(*dims) for dims in stream.landing_shapes(STACK_ROWS)]
    vmem = pl.BlockSpec(memory_space=VMEM)
    hbm = pl.BlockSpec(memory_space=pl.ANY)
    copy_count = 280
    return pl.pallas_call(
        back_kernel,
        out_shape=[jax.ShapeDtypeStruct(*out) for out in outs],
        in_specs=[hbm] * len(operands) + [vmem] * 4,
        out_specs=[hbm] * len(outs),
        scratch_shapes=[VMEM(*part) for part in scratch]
        + [pltpu.SemaphoreType.DMA((copy_count,)), pltpu.SemaphoreType.DMA((copy_count,))],
        compiler_params=pltpu.CompilerParams(
            collective_id=2, has_side_effects=True, vmem_limit_bytes=63 * 2**20
        ),
    )(*operands, frequency, *gains)


def unstack_kernel(*refs):
    stacks_hbm, passed_hbm, vectors = refs[:4], refs[4:6], refs[6:14]
    passed_out, outs_hbm = refs[14:16], refs[16:30]
    stacks, passed, wides, sems = refs[30:34], refs[34:36], refs[36:50], refs[50]
    loads = [
        pltpu.make_async_copy(source, target, sems.at[place])
        for place, (source, target) in enumerate(zip(stacks_hbm, stacks))
    ]
    for place in (2, 0, 1, 3):
        loads[place].start()
    passing = []
    for place in range(2):
        passing.append(
            pltpu.make_async_copy(passed_hbm[place], passed[place], sems.at[18 + place])
        )
        passing[place].start()
    early, coarse, middle, late = stacks
    (wq, wk, wv, wo, we, wc, wp, cq, ck, cv, co, ce, cc, wu) = wides
    writes = []

    def write(place):
        move = pltpu.make_async_copy(wides[place], outs_hbm[place], sems.at[4 + place])
        move.start()
        writes.append(move)

    loads[2].wait()
    for step in range(4):
        here = slice(512 * step, 512 * step + 512)
        wc[here, :] = middle[here, :512].astype(WIDE)
    write(5)
    for part in range(4):
        here = slice(512 * part, 512 * part + 512)
        we[:, here] = middle[here, 512:1024].astype(WIDE)
        wo[:, 128 * part : 128 * part + 128] = middle[here, 1024:].astype(WIDE)
    write(4)
    write(3)
    loads[0].wait()
    for number in range(6):
        for part in range(2):
            down, across = divmod(2 * number + part, 3)
            block = early[512 * down : 512 * down + 512, 256 * across : 256 * across + 256].astype(WIDE)
            inside = 256 * part
            if number < 3:
                wp[512 * number : 512 * number + 512, inside : inside + 256] = block
            else:
                start = 512 * (number - 3) + inside
                wu[:, start : start + 256] = block
        if number == 2:
            write(6)
    write(13)
    loads[1].wait()
    ce[...] = coarse[:, :512].astype(WIDE)
    write(11)
    cc[...] = coarse[:, 512:1024].astype(WIDE)
    write(12)
    for place, ref in enumerate((cq, ck, cv)):
        ref[...] = coarse[:, 1024 + 128 * place : 1152 + 128 * place].astype(WIDE)
        write(7 + place)
    for part in range(4):
        here = slice(128 * part, 128 * part + 128)
        co[:, here] = coarse[here, 1408:1536].astype(WIDE)
    write(10)
    loads[3].wait()
    for place, ref in enumerate((wq, wk, wv)):
        for group in range(4):
            ref[:, 128 * group : 128 * group + 128] = late[
                group, :, 128 * place : 128 * place + 128
            ].astype(WIDE)
        write(place)
    columns = sum(late[group, :, OWN:].astype(WIDE) for group in range(4))
    for place, row in enumerate(
        (jnp.transpose(columns), jnp.transpose(coarse[:, 1536:].astype(WIDE)))
    ):
        for line in range(4):
            vectors[4 * place + line][...] = row[line]
    for place in range(2):
        passing[place].wait()
        move = pltpu.make_async_copy(passed[place], passed_out[place], sems.at[20 + place])
        move.start()
        writes.append(move)
    for move in writes:
        move.wait()


def unstack(stacks, passed):
    shapes = (
        [(WIDTH, WIDTH)] * 4
        + [(WIDTH, HIDDEN), (HIDDEN, WIDTH), (ROWS, WIDTH)]
        + [(WIDTH, 128)] * 3
        + [(128, WIDTH), (WIDTH, WIDTH), (WIDTH, WIDTH), (WIDTH, ROWS)]
    )
    vmem = pl.BlockSpec(memory_space=VMEM)
    hbm = pl.BlockSpec(memory_space=pl.ANY)
    return pl.pallas_call(
        unstack_kernel,
        out_shape=[jax.ShapeDtypeStruct((WIDTH,), WIDE)] * 8
        + [jax.ShapeDtypeStruct(array.shape, array.dtype) for array in passed]
        + [jax.ShapeDtypeStruct(shape, WIDE) for shape in shapes],
        in_specs=[hbm] * 6,
        out_specs=[vmem] * 8 + [hbm] * (2 + len(shapes)),
        scratch_shapes=[VMEM(stack.shape, LOW) for stack in stacks]
        + [VMEM(array.shape, array.dtype) for array in passed]
        + [VMEM(shape, WIDE) for shape in shapes]
        + [pltpu.SemaphoreType.DMA((8 + len(shapes),))],
        compiler_params=pltpu.CompilerParams(vmem_limit_bytes=60 * 2**20),
    )(*stacks, *passed)


def body(
    inputs,
    lengths,
    cotangent,
    attention_gain,
    attention_shift,
    query_weight,
    key_weight,
    value_weight,
    output_weight,
    feedforward_gain,
    feedforward_shift,
    expand_weight,
    contract_weight,
    pooling_weight,
    coarse_gain,
    coarse_shift,
    coarse_query,
    coarse_key,
    coarse_value,
    coarse_output,
    widen_gain,
    widen_shift,
    coarse_expand,
    coarse_contract,
    upsample_weight,
):
    def row(vector):
        return vector.reshape(1, -1)

    frequency = jnp.asarray(frequency_row())
    square = (query_weight, key_weight, value_weight)
    (a1, q, k, v, o, level, o_own, h, a2, act, slope, wqkv, mixed, ds, early, coarse_stack) = front(
        lengths,
        inputs,
        cotangent,
        [
            row(vector)
            for vector in (
                attention_gain,
                attention_shift,
                feedforward_gain,
                feedforward_shift,
                coarse_gain,
                coarse_shift,
                widen_gain,
                widen_shift,
            )
        ],
        frequency,
        (*square, output_weight, expand_weight, contract_weight, pooling_weight, upsample_weight),
        (coarse_query, coarse_key, coarse_value, coarse_output, coarse_expand, coarse_contract),
    )
    input_grad, *stacks = back(
        (
            inputs,
            ds,
            h,
            a2,
            act,
            slope,
            o_own,
            wqkv,
            *square,
            output_weight,
            expand_weight,
            contract_weight,
            a1,
            q,
            k,
            v,
            o,
            level,
            early,
            coarse_stack,
        ),
        frequency,
        (
            row(attention_gain),
            row(attention_shift),
            row(feedforward_gain),
        ),
    )
    results = unstack(stacks, (mixed, input_grad))
    vectors, (mixed, input_grad) = results[:8], results[8:10]
    wq, wk, wv, wo, we, wc, wp, cq, ck, cv, co, ce, cc, wu = results[10:]
    return (
        mixed,
        input_grad,
        vectors[2],
        vectors[3],
        wq,
        wk,
        wv,
        wo,
        vectors[0],
        vectors[1],
        we,
        wc,
        wp,
        vectors[4],
        vectors[5],
        cq,
        ck,
        cv,
        co,
        vectors[6],
        vectors[7],
        ce,
        cc,
        wu,
    )


def solution(mesh):
    in_specs = (
        P(("seq", "head"), None),
        P("seq"),
        P(("seq", "head"), None),
        P(),
        P(),
        P(),
        P(),
        P(),
        P(),
        P(),
        P(),
        P(),
        P(),
        P(),
        P(),
        P(),
        P(None, "head"),
        P(None, "head"),
        P(None, "head"),
        P("head", None),
        P(),
        P(),
        P(None, "head"),
        P("head", None),
        P(),
    )
    out_specs = (
        P(("seq", "head"), None),
        P(("seq", "head"), None),
        P(),
        P(),
        P(),
        P(),
        P(),
        P(),
        P(),
        P(),
        P(),
        P(),
        P(),
        P(),
        P(),
        P(None, "head"),
        P(None, "head"),
        P(None, "head"),
        P("head", None),
        P(),
        P(),
        P(None, "head"),
        P("head", None),
        P(),
    )
    return jax.shard_map(body, mesh=mesh, in_specs=in_specs, out_specs=out_specs, check_vma=False)
```
